512 devices in a mesh: dp: 64 (over y, z), tensor: 8 (over x, core).
Axes of the slice: x: 4, y: 4, z: 16, core: 2. Of those that a mesh axis runs over, the one named last changes fastest.
Arguments:
- features: bfloat16 [8192, 8192], P('dp', 'tensor'), may hold values from -300 to 300
- gate_pre: bfloat16 [8192, 14336], P('dp', 'tensor'), may hold values from -6 to 6
- up_pre: bfloat16 [8192, 14336], P('dp', 'tensor'), may hold values from -6 to 6
- hidden_grad: bfloat16 [8192, 14336], P('dp', 'tensor'), may hold values from -6 to 6
- tile_rows: int32 [8, 112], P('tensor'), may hold values from 0 to 63, as said below
- tile_cols: int32 [8, 112], P('tensor'), may hold values from 0 to 13, as said below
- owner_counts: int32 [8, 64], P('tensor'), may hold values from 1 to 2, 112 in all within a row
- delta_value: float32 [8, 128, 128, 128], P('tensor', 'dp'), may hold values from -1 to 1
- moment_one: float32 [8, 128, 128, 128], P('tensor', 'dp'), may hold values from -6 to 6
- moment_two: float32 [8, 128, 128, 128], P('tensor', 'dp'), may hold values from 0.05 to 5
Outputs:
- input_grad: bfloat16 [8192, 8192], P('dp')
- new_delta: float32 [8, 128, 128, 128], P('tensor', 'dp')
- new_moment_one: float32 [8, 128, 128, 128], P('tensor', 'dp')
- new_moment_two: float32 [8, 128, 128, 128], P('tensor', 'dp')
The draws below stay inside these ranges and needn't reach their ends.
Inputs may be any that keep to these rules, and one draw needn't show every extreme that they name: `tile_rows`: in each tensor shard the 112 tiles are distinct cells and are listed in increasing order of row tile, then column tile. `tile_cols`: pairs with tile_rows. `owner_counts`: each row sums to 112; the largest entry of each row is 2.
All inputs are finite; a program needn't handle non-finite values.
Results may differ from the reference program's by a relative error of at most 0.013.
Values may be sent and summed in bfloat16 or wider, within the bound.
No kernel may reach another device: no remote copies, remote signals or barrier semaphores. Data moves between devices by JAX's collectives and lax.ppermute only.
A program may use at most 128 MiB of HBM per device.

```python
import math
import jax
import jax.numpy as jnp
import numpy as np
from jax import lax

D = 8192
FF = 14336
TILE = 128
CAP = 2
TOKENS = 8192
TILES = 112
N_DP = 64
N_TENSOR = 8


def pick_cells(key):
    row_count = D // TILE
    col_count = FF // N_TENSOR // TILE
    cells = row_count * col_count
    scores = jax.random.randint(key, (N_TENSOR, cells), 0, 65536) * cells + jnp.arange(cells, dtype=jnp.int32)[None, :]
    best_scores, chosen = lax.top_k(-scores, TILES)
    ordered = jnp.sort(chosen.astype(jnp.int32), axis=1)
    return (ordered, col_count)


def draw_tile_rows(key, part):
    ordered, col_count = pick_cells(key)
    return (ordered // col_count).astype(jnp.int32)


def draw_tile_cols(key, part):
    ordered, col_count = pick_cells(key)
    return (ordered % col_count).astype(jnp.int32)


def draw_features(key, part):
    key = jax.random.fold_in(key, 3)
    key_base, key_cols, key_rows = jax.random.split(key, 3)
    ramp = jnp.power(3.0, jnp.arange(D, dtype=jnp.float32) / D)
    col_scale = ramp * jnp.exp(jax.random.uniform(key_cols, (D,), jnp.float32, 0.0, jnp.log(3.0)))
    base = jnp.clip(jax.random.normal(key_base, (TOKENS, D), jnp.float32), -4.0, 4.0)
    row_scale = jnp.exp(jax.random.uniform(key_rows, (TOKENS,), jnp.float32, 0.0, jnp.log(3.0)))
    return (base * row_scale[:, None] * col_scale[None, :]).astype(jnp.bfloat16)


def steps_of(stream_key, extent, shards, smallest, largest):
    gain = 1.0
    for dim, shards_of in shards:
        heights = jax.random.uniform(jax.random.fold_in(jax.random.fold_in(stream_key, 6), dim), (shards_of,), jnp.float32, smallest / len(shards), largest / len(shards))
        gain = gain * jnp.repeat(jnp.exp(heights), extent[dim] // shards_of).reshape((-1,) + (1,) * (len(extent) - 1 - dim))
    return gain


def length_profile(number_of, total, limit, skew):
    portions = [(1 << 20) // math.isqrt(rank ** skew) + 1 for rank in range(2, number_of + 1)]
    spare, given = total - limit - (number_of - 1), [1] * (number_of - 1)
    while spare > 0:
        free = [i for i in range(number_of - 1) if given[i] < limit]
        whole, remaining = sum([portions[i] for i in free]), spare
        for i in free:
            addition = min(limit - given[i], max(1, remaining * portions[i] // whole), spare)
            given[i] = given[i] + addition
            spare = spare - addition
    return np.array([limit] + given)


def uneven_parts(rng, amount, total, limit, lean):
    if amount == 2:
        one = jax.random.randint(rng, (), max(1, total - limit), min(limit, total - 1) + 1)
        return jnp.stack([one, total - one])
    tallies = jnp.asarray(length_profile(amount, total, limit, lean), jnp.int32)
    pairs = (amount - 1) // 2
    source_of, receiver = tallies[1:1 + 2 * pairs:2], tallies[2:2 + 2 * pairs:2]
    slack = jnp.minimum(source_of - 1, limit - receiver)
    shifted = jax.random.randint(jax.random.fold_in(rng, 1), (pairs,), 0, 1 << 20) % (slack + 1)
    tallies = tallies.at[1:1 + 2 * pairs:2].set(source_of - shifted).at[2:2 + 2 * pairs:2].set(receiver + shifted)
    return tallies[jax.random.permutation(jax.random.fold_in(rng, 2), amount)]


def scatter_about(rng, shape, scale, most, cuts=(), held_as=jnp.bfloat16):
    array = jax.random.normal(rng, shape, jnp.float32) * scale
    if len(cuts) > 0:
        array = steps_of(rng, shape, cuts, -0.22, 0.18) * array
    return jnp.clip(array, min=-most, max=most).astype(held_as)


def setup_inputs(seed: int = 0) -> dict:
    seeds = jax.random.split(jax.random.key(seed), 11)
    return {
        "features": draw_features(jax.random.fold_in(seeds[10], 71), 0),
        "gate_pre": scatter_about(seeds[1], (TOKENS, FF), 1.0, 6.0, ((0, 64), (1, 8))),
        "up_pre": scatter_about(seeds[2], (TOKENS, FF), 1.0, 6.0, ((0, 64), (1, 8))),
        "hidden_grad": scatter_about(seeds[3], (TOKENS, FF), 1.0, 6.0, ((0, 64), (1, 8))),
        "tile_rows": draw_tile_rows(jax.random.fold_in(seeds[10], 71), 0),
        "tile_cols": draw_tile_cols(jax.random.fold_in(seeds[10], 71), 0),
        "owner_counts": jax.vmap(lambda own: uneven_parts(own, N_DP, TILES, CAP, 2))(jax.random.split(seeds[6], N_TENSOR)).reshape((N_TENSOR, N_DP)).astype(jnp.int32),
        "delta_value": scatter_about(seeds[7], (N_TENSOR, N_DP * CAP, TILE, TILE), 0.2, 1.0, ((0, 8), (1, 64)), jnp.float32),
        "moment_one": scatter_about(seeds[8], (N_TENSOR, N_DP * CAP, TILE, TILE), 1.0, 6.0, ((0, 8), (1, 64)), jnp.float32),
        "moment_two": jnp.clip(jnp.exp(math.log(5.0) - 4.6051702 * jax.random.uniform(seeds[9], (N_TENSOR, N_DP * CAP, TILE, TILE), jnp.float32) ** steps_of(seeds[9], (N_TENSOR, N_DP * CAP, TILE, TILE), ((0, 8), (1, 64)), -0.2, 0.2)), 0.05, 5.0),
    }


def slot_maps(counts, tile_total, slot_cap):
    owner_total = counts.shape[0]
    ends = jnp.cumsum(counts).astype(jnp.int32)
    starts = (ends - counts).astype(jnp.int32)
    slot_rank = jnp.arange(owner_total * slot_cap, dtype=jnp.int32) % slot_cap
    slot_valid = slot_rank < jnp.repeat(counts, slot_cap)
    slot_list = jnp.minimum(jnp.repeat(starts, slot_cap) + slot_rank, tile_total - 1).astype(jnp.int32)
    positions = jnp.arange(tile_total, dtype=jnp.int32)
    owner_of = lax.optimization_barrier(jnp.sum((ends[None, :] <= positions[:, None]).astype(jnp.int32), axis=1))
    owner_ids = jnp.arange(owner_total, dtype=jnp.int32)
    start_of = lax.optimization_barrier(jnp.sum(jnp.where(owner_of[:, None] == owner_ids[None, :], starts[None, :], 0), axis=1))
    list_slot = (owner_of * slot_cap + positions - start_of).astype(jnp.int32)
    return (slot_valid, slot_list, list_slot)

def adam_update(grads, valid, delta_value, moment_one, moment_two, factor):
    clipped = factor * grads
    first = 0.9 * moment_one + 0.1 * clipped
    second = 0.95 * moment_two + 0.05 * clipped * clipped
    step_size = first / (1.0 - 0.9 ** 10) / (jnp.sqrt(second / (1.0 - 0.95 ** 10)) + 1e-08)
    updated = delta_value - 0.02 * (step_size + 0.1 * delta_value)
    return (jnp.where(valid, updated, delta_value), jnp.where(valid, first, moment_one), jnp.where(valid, second, moment_two))

def reference(features, gate_pre, up_pre, hidden_grad, tile_rows, tile_cols, owner_counts, delta_value, moment_one, moment_two):
    ff_local = FF // N_TENSOR
    row_tiles = D // TILE
    pre_gate = gate_pre.astype(jnp.float32)
    sig = jax.nn.sigmoid(pre_gate)
    gate_grad = (hidden_grad.astype(jnp.float32) * up_pre.astype(jnp.float32) * sig * (1.0 + pre_gate * (1.0 - sig))).astype(jnp.bfloat16)
    x_blocks = features.reshape(TOKENS, row_tiles, TILE)
    input_sum = jnp.zeros((TOKENS, D), jnp.float32)
    slot_grads = []
    slot_flags = []
    for tensor_shard in range(N_TENSOR):
        tile_row = tile_rows[tensor_shard].astype(jnp.int32)
        tile_col = tile_cols[tensor_shard].astype(jnp.int32)
        g_blocks = gate_grad[:, tensor_shard * ff_local:(tensor_shard + 1) * ff_local].reshape(TOKENS, ff_local // TILE, TILE)
        slot_valid, slot_list, list_slot = slot_maps(owner_counts[tensor_shard].astype(jnp.int32), TILES, CAP)
        delta_half = delta_value[tensor_shard].astype(jnp.bfloat16)
        delta_list = jnp.take(delta_half, list_slot, axis=0)

        def one_tile(position):
            x_part = lax.dynamic_index_in_dim(x_blocks, tile_row[position], axis=1, keepdims=False)
            g_part = lax.dynamic_index_in_dim(g_blocks, tile_col[position], axis=1, keepdims=False)
            grad_tile = jnp.dot(x_part.T, g_part, preferred_element_type=jnp.float32)
            delta_tile = lax.dynamic_index_in_dim(delta_list, position, axis=0, keepdims=False)
            contrib = jnp.dot(g_part, delta_tile.T, preferred_element_type=jnp.float32)
            return (grad_tile, contrib)
        grad_list, contribs = lax.map(one_tile, jnp.arange(TILES, dtype=jnp.int32))
        onehot = (tile_row[None, :] == jnp.arange(row_tiles, dtype=jnp.int32)[:, None]).astype(jnp.float32)
        blocks = jnp.dot(onehot, contribs.reshape(TILES, TOKENS * TILE), precision=lax.Precision.HIGHEST, preferred_element_type=jnp.float32)
        partial_value = blocks.reshape(row_tiles, TOKENS, TILE).transpose(1, 0, 2).reshape(TOKENS, D)
        input_sum = input_sum + partial_value.astype(jnp.bfloat16).astype(jnp.float32)
        slot_grad = jnp.where(slot_valid[:, None, None], jnp.take(grad_list, slot_list, axis=0), 0.0)
        slot_grads.append(slot_grad)
        slot_flags.append(slot_valid)
    grads = jnp.stack(slot_grads)
    valid = jnp.stack(slot_flags)[:, :, None, None]
    squares = jnp.sum(grads * grads)
    root_mean = jnp.sqrt(squares / (N_TENSOR * TILES * TILE * TILE) + 1e-06)
    factor = jnp.minimum(1.0, 1.0 / root_mean)
    new_delta, new_first, new_second = adam_update(grads, valid, delta_value, moment_one, moment_two, factor)
    return (input_sum.astype(jnp.bfloat16), new_delta, new_first, new_second)
```

```python
import functools

import jax
import jax.numpy as jnp
import numpy as np
from jax import lax
from jax.experimental import pallas as pl
from jax.experimental.pallas import tpu as pltpu
from jax.sharding import Mesh, PartitionSpec as P

TILE = 128
VMEM_LIMIT = 48 * 1024 * 1024
SMEM = pl.BlockSpec(memory_space=pltpu.SMEM)
VMEM = pl.BlockSpec(memory_space=pltpu.VMEM)
ANY = pl.BlockSpec(memory_space=pl.ANY)


def shift(value, axis, step):
    size = lax.axis_size(axis)
    return lax.ppermute(value, axis, [(i, (i + step) % size) for i in range(size)])


def exchange(value, axis):
    return lax.all_to_all(value, axis, split_axis=0, concat_axis=0, tiled=True)


def spread(value, axis):
    copies = jnp.broadcast_to(value[None], (lax.axis_size(axis),) + value.shape)
    return exchange(copies, axis)


def gate_kernel(gate_ref, up_ref, hidden_ref, grad_ref, turned_ref):
    for col in range(grad_ref.shape[0]):
        cut = slice(col * TILE, (col + 1) * TILE)
        gate = gate_ref[:, cut].astype(jnp.float32)
        sig = 1.0 / (1.0 + jnp.exp(-gate))
        value = (
            hidden_ref[:, cut].astype(jnp.float32)
            * up_ref[:, cut].astype(jnp.float32)
            * sig
            * (1.0 + gate * (1.0 - sig))
        )
        grad_ref[col] = value.astype(jnp.bfloat16)
        turned_ref[col] = value.T.astype(jnp.bfloat16)


def find_slots(counts_ref, slot_ref, empty=None):
    def owner_step(owner, start):
        count = counts_ref[0, owner]
        slot_ref[start] = 2 * owner
        slot_ref[start + 1] = 2 * owner + 1
        if empty is not None:

            @pl.when(count < 2)
            def _():
                empty(2 * owner + 1)

        return start + count

    lax.fori_loop(0, counts_ref.shape[1], owner_step, 0)


def tile_kernel(
    core_ref, rows_ref, cols_ref, counts_ref, own_ref, other_ref, turned_ref,
    out_ref, features, slots, sems,
):
    first = pltpu.make_async_copy(own_ref, features.at[0], sems.at[0])
    second = pltpu.make_async_copy(other_ref, features.at[1], sems.at[1])
    first.start()
    second.start()

    def empty(slot):
        out_ref[slot] = jnp.zeros((TILE, TILE), jnp.bfloat16)

    find_slots(counts_ref, slots, empty)
    first.wait()
    second.wait()
    core = core_ref[0]
    per_step = 4

    def step(index, carry):
        for part in range(per_step):
            k = index * per_step + part
            row = rows_ref[0, k]
            side = ((row >> 3) & 1) ^ core
            lane = pl.multiple_of((row & 7) * TILE, TILE)
            x = features[side, row >> 4, :, pl.ds(lane, TILE)]
            product = jnp.dot(
                turned_ref[cols_ref[0, k]], x, preferred_element_type=jnp.float32
            )
            out_ref[slots[k]] = product.astype(jnp.bfloat16)
        return carry

    lax.fori_loop(0, rows_ref.shape[1] // per_step, step, 0)


def contrib_kernel(rows_ref, cols_ref, counts_ref, grad_ref, delta_ref, out_ref, slots):
    out_ref[...] = jnp.zeros_like(out_ref)
    find_slots(counts_ref, slots)
    per_step = 4

    def step(index, carry):
        last, total = carry
        for part in range(per_step):
            k = index * per_step + part
            row = rows_ref[0, k]
            slot = slots[k]
            owner = slot >> 1
            place = (((owner & 15) * 4 + (owner >> 4)) << 1) + (slot & 1)
            product = lax.dot_general(
                grad_ref[cols_ref[0, k]], delta_ref[place],
                (((1,), (1,)), ((), ())), preferred_element_type=jnp.float32,
            )
            total = jnp.where(row == last, total, 0.0) + product
            lane = pl.multiple_of(row * TILE, TILE)
            out_ref[:, pl.ds(lane, TILE)] = total.astype(jnp.bfloat16)
            last = row
        return last, total

    lax.fori_loop(
        0, rows_ref.shape[1] // per_step, step,
        (jnp.int32(-1), jnp.zeros((TILE, TILE), jnp.float32)),
    )


def adam_update(grads, valid, delta_value, moment_one, moment_two, factor):
    clipped = factor * grads
    first = 0.9 * moment_one + 0.1 * clipped
    second = 0.95 * moment_two + 0.05 * clipped * clipped
    step_size = first / (1.0 - 0.9**10) / (jnp.sqrt(second / (1.0 - 0.95**10)) + 1e-08)
    updated = delta_value - 0.02 * (step_size + 0.1 * delta_value)
    return (
        jnp.where(valid, updated, delta_value),
        jnp.where(valid, first, moment_one),
        jnp.where(valid, second, moment_two),
    )


def body(
    features, gate_pre, up_pre, hidden_grad, tile_rows, tile_cols, owner_counts,
    delta_value, moment_one, moment_two,
):
    ny, nz, nx = (lax.axis_size(name) for name in ("y", "z", "x"))
    core = lax.axis_index("core")
    owner = lax.axis_index("y") * nz + lax.axis_index("z")
    tokens, hidden = gate_pre.shape
    col_tiles = hidden // TILE
    width = features.shape[1] * nx * 2
    slot_cap = delta_value.shape[1]
    slot_total = ny * nz * slot_cap
    tile_total = tile_rows.shape[1]
    params = pltpu.CompilerParams(vmem_limit_bytes=VMEM_LIMIT)
    bf16 = jnp.bfloat16

    delta_y = lax.all_gather(delta_value[0].astype(bf16), "y", axis=0, tiled=True)
    delta_all = lax.all_gather(delta_y, "z", axis=0, tiled=True)

    own = spread(features, "x")
    other = shift(own, "core", 1)

    grads, turned = pl.pallas_call(
        gate_kernel,
        out_shape=[jax.ShapeDtypeStruct((col_tiles, tokens, TILE), bf16)] * 2,
        in_specs=[VMEM] * 3,
        out_specs=[VMEM] * 2,
        compiler_params=params,
        cost_estimate=pl.CostEstimate(
            flops=tokens * hidden * 12, bytes_accessed=tokens * hidden * 10, transcendentals=0
        ),
        name="gate",
    )(gate_pre, up_pre, hidden_grad)

    terms = pl.pallas_call(
        tile_kernel,
        out_shape=jax.ShapeDtypeStruct((slot_total, TILE, TILE), bf16),
        in_specs=[SMEM] * 4 + [ANY, ANY, VMEM],
        out_specs=VMEM,
        scratch_shapes=[
            pltpu.VMEM((2, nx, tokens, features.shape[1]), bf16),
            pltpu.SMEM((tile_total + 8,), jnp.int32),
            pltpu.SemaphoreType.DMA((2,)),
        ],
        compiler_params=params,
        cost_estimate=pl.CostEstimate(
            flops=2 * tile_total * TILE**3, bytes_accessed=8 << 20, transcendentals=0
        ),
        name="tiles",
    )(core[None], tile_rows, tile_cols, owner_counts, own, other, turned)

    arrived = exchange(terms, "y").reshape(ny, nz * slot_cap, TILE, TILE)
    summed = jnp.sum(arrived.astype(jnp.float32), axis=0).astype(bf16)
    arrived = exchange(summed, "z").reshape(nz, slot_cap, TILE, TILE)
    own_grad = jnp.sum(arrived.astype(jnp.float32), axis=0)
    own_count = lax.dynamic_index_in_dim(owner_counts[0], owner, axis=0, keepdims=False)
    own_valid = (jnp.arange(slot_cap, dtype=jnp.int32) < own_count)[:, None, None]
    own_grad = jnp.where(own_valid, own_grad, 0.0)

    squares = jnp.sum(own_grad * own_grad)
    for axes in (("x", "core"), "y", "z"):
        piece = jnp.broadcast_to(squares[None, None], (8, TILE))
        squares = jnp.sum(spread(piece, axes)[:, 0, 0])
    root_mean = jnp.sqrt(
        squares / (nx * 2 * tile_total * TILE * TILE) + 1e-06
    )
    factor = jnp.minimum(1.0, 1.0 / root_mean)
    new_delta, new_first, new_second = adam_update(
        own_grad.transpose(0, 2, 1)[None], own_valid[None], delta_value, moment_one,
        moment_two, factor,
    )

    partial = pl.pallas_call(
        contrib_kernel,
        out_shape=jax.ShapeDtypeStruct((tokens, width), bf16),
        in_specs=[SMEM] * 3 + [VMEM] * 2,
        out_specs=VMEM,
        scratch_shapes=[pltpu.SMEM((tile_total + 8,), jnp.int32)],
        compiler_params=params,
        cost_estimate=pl.CostEstimate(
            flops=2 * tile_total * TILE**3, bytes_accessed=8 << 20, transcendentals=0
        ),
        name="contribs",
    )(tile_rows, tile_cols, owner_counts, grads, delta_all)

    half = tokens // 2
    keep = lax.dynamic_slice_in_dim(partial, core * half, half, axis=0)
    give = lax.dynamic_slice_in_dim(partial, (1 - core) * half, half, axis=0)
    taken = shift(give, "core", 1)
    pair = (keep.astype(jnp.float32) + taken.astype(jnp.float32)).astype(bf16)
    quarters = exchange(pair, "x").reshape(nx, half // nx, width)
    mine = jnp.sum(quarters.astype(jnp.float32), axis=0).astype(bf16)
    near = spread(mine, "x").reshape(half, width)
    far = shift(near, "core", 1)
    input_grad = jnp.concatenate(
        [jnp.where(core == 0, near, far), jnp.where(core == 0, far, near)], axis=0
    )
    return (input_grad, new_delta, new_first, new_second)


def solution(mesh):
    grid = Mesh(mesh.devices.reshape(4, 16, 4, 2), ("y", "z", "x", "core"))
    dp, tensor = ("y", "z"), ("x", "core")
    tokens = P(dp, tensor)
    lists = P(tensor, None)
    slots = P(tensor, dp, None, None)
    return jax.shard_map(
        body,
        mesh=grid,
        in_specs=(tokens,) * 4 + (lists,) * 3 + (slots,) * 3,
        out_specs=(P(dp, None),) + (slots,) * 3,
        check_vma=False,
    )
```

```python
import functools

import jax
import jax.numpy as jnp
import numpy as np
from jax import lax
from jax.experimental import pallas as pl
from jax.experimental.pallas import tpu as pltpu
from jax.sharding import Mesh, PartitionSpec as P

TILE = 128
VMEM_LIMIT = 48 * 1024 * 1024
SMEM = pl.BlockSpec(memory_space=pltpu.SMEM)
VMEM = pl.BlockSpec(memory_space=pltpu.VMEM)
ANY = pl.BlockSpec(memory_space=pl.ANY)


def shift(value, axis, step):
    size = lax.axis_size(axis)
    return lax.ppermute(value, axis, [(i, (i + step) % size) for i in range(size)])


def exchange(value, axis):
    return lax.all_to_all(value, axis, split_axis=0, concat_axis=0, tiled=True)


def spread(value, axis):
    copies = jnp.broadcast_to(value[None], (lax.axis_size(axis),) + value.shape)
    return exchange(copies, axis)


def gate_kernel(gate_ref, up_ref, hidden_ref, grad_ref, turned_ref):
    for col in range(grad_ref.shape[0]):
        cut = slice(col * TILE, (col + 1) * TILE)
        gate = gate_ref[:, cut].astype(jnp.float32)
        sig = 1.0 / (1.0 + jnp.exp(-gate))
        value = (
            hidden_ref[:, cut].astype(jnp.float32)
            * up_ref[:, cut].astype(jnp.float32)
            * sig
            * (1.0 + gate * (1.0 - sig))
        )
        grad_ref[col] = value.astype(jnp.bfloat16)
        turned_ref[col] = value.T.astype(jnp.bfloat16)


def find_slots(counts_ref, slot_ref, empty=None):
    def owner_step(owner, start):
        count = counts_ref[0, owner]
        slot_ref[start] = 2 * owner
        slot_ref[start + 1] = 2 * owner + 1
        if empty is not None:

            @pl.when(count < 2)
            def _():
                empty(2 * owner + 1)

        return start + count

    lax.fori_loop(0, counts_ref.shape[1], owner_step, 0)


def tile_kernel(
    core_ref, rows_ref, cols_ref, counts_ref, own_ref, other_ref, turned_ref,
    out_ref, features, slots, sems,
):
    first = pltpu.make_async_copy(own_ref, features.at[0], sems.at[0])
    second = pltpu.make_async_copy(other_ref, features.at[1], sems.at[1])
    first.start()
    second.start()

    def empty(slot):
        out_ref[slot] = jnp.zeros((TILE, TILE), jnp.bfloat16)

    find_slots(counts_ref, slots, empty)
    first.wait()
    second.wait()
    core = core_ref[0]
    per_step = 4

    def step(index, carry):
        for part in range(per_step):
            k = index * per_step + part
            row = rows_ref[0, k]
            side = ((row >> 3) & 1) ^ core
            lane = pl.multiple_of((row & 7) * TILE, TILE)
            x = features[side, row >> 4, :, pl.ds(lane, TILE)]
            product = jnp.dot(
                turned_ref[cols_ref[0, k]], x, preferred_element_type=jnp.float32
            )
            out_ref[slots[k]] = product.astype(jnp.bfloat16)
        return carry

    lax.fori_loop(0, rows_ref.shape[1] // per_step, step, 0)


def contrib_kernel(rows_ref, cols_ref, counts_ref, grad_ref, delta_ref, out_ref, slots):
    out_ref[...] = jnp.zeros_like(out_ref)
    find_slots(counts_ref, slots)
    per_step = 4

    def step(index, carry):
        last, total = carry
        for part in range(per_step):
            k = index * per_step + part
            row = rows_ref[0, k]
            slot = slots[k]
            owner = slot >> 1
            place = (((owner & 15) * 4 + (owner >> 4)) << 1) + (slot & 1)
            product = lax.dot_general(
                grad_ref[cols_ref[0, k]], delta_ref[place],
                (((1,), (1,)), ((), ())), preferred_element_type=jnp.float32,
            )
            total = jnp.where(row == last, total, 0.0) + product
            lane = pl.multiple_of(row * TILE, TILE)
            out_ref[:, pl.ds(lane, TILE)] = total.astype(jnp.bfloat16)
            last = row
        return last, total

    lax.fori_loop(
        0, rows_ref.shape[1] // per_step, step,
        (jnp.int32(-1), jnp.zeros((TILE, TILE), jnp.float32)),
    )


def adam_update(grads, valid, delta_value, moment_one, moment_two, factor):
    clipped = factor * grads
    first = 0.9 * moment_one + 0.1 * clipped
    second = 0.95 * moment_two + 0.05 * clipped * clipped
    step_size = first / (1.0 - 0.9**10) / (jnp.sqrt(second / (1.0 - 0.95**10)) + 1e-08)
    updated = delta_value - 0.02 * (step_size + 0.1 * delta_value)
    return (
        jnp.where(valid, updated, delta_value),
        jnp.where(valid, first, moment_one),
        jnp.where(valid, second, moment_two),
    )


def body(
    features, gate_pre, up_pre, hidden_grad, tile_rows, tile_cols, owner_counts,
    delta_value, moment_one, moment_two,
):
    ny, nz, nx = (lax.axis_size(name) for name in ("y", "z", "x"))
    x, core = lax.axis_index("x"), lax.axis_index("core")
    owner = lax.axis_index("y") * nz + lax.axis_index("z")
    tokens, hidden = gate_pre.shape
    col_tiles = hidden // TILE
    width = features.shape[1] * nx * 2
    slot_cap = delta_value.shape[1]
    slot_total = ny * nz * slot_cap
    tile_total = tile_rows.shape[1]
    params = pltpu.CompilerParams(vmem_limit_bytes=VMEM_LIMIT)
    bf16 = jnp.bfloat16

    own = spread(features, "x")
    other = shift(own, "core", 1)

    delta_y = spread(delta_value[0].astype(bf16), "y").reshape(ny * slot_cap, TILE, TILE)
    delta_all = lax.all_gather(delta_y, "z", axis=0, tiled=True)

    grads, turned = pl.pallas_call(
        gate_kernel,
        out_shape=[jax.ShapeDtypeStruct((col_tiles, tokens, TILE), bf16)] * 2,
        in_specs=[VMEM] * 3,
        out_specs=[VMEM] * 2,
        compiler_params=params,
        cost_estimate=pl.CostEstimate(
            flops=tokens * hidden * 12, bytes_accessed=tokens * hidden * 10, transcendentals=0
        ),
        name="gate",
    )(gate_pre, up_pre, hidden_grad)

    terms = pl.pallas_call(
        tile_kernel,
        out_shape=jax.ShapeDtypeStruct((slot_total, TILE, TILE), bf16),
        in_specs=[SMEM] * 4 + [ANY, ANY, VMEM],
        out_specs=VMEM,
        scratch_shapes=[
            pltpu.VMEM((2, nx, tokens, features.shape[1]), bf16),
            pltpu.SMEM((tile_total + 8,), jnp.int32),
            pltpu.SemaphoreType.DMA((2,)),
        ],
        compiler_params=params,
        cost_estimate=pl.CostEstimate(
            flops=2 * tile_total * TILE**3, bytes_accessed=8 << 20, transcendentals=0
        ),
        name="tiles",
    )(core[None], tile_rows, tile_cols, owner_counts, own, other, turned)

    arrived = exchange(terms, "y").reshape(ny, nz * slot_cap, TILE, TILE)
    summed = jnp.sum(arrived.astype(jnp.float32), axis=0).astype(bf16)
    summed, grads = lax.optimization_barrier((summed, grads))
    arrived = exchange(summed, "z").reshape(nz, slot_cap, TILE, TILE)
    own_grad = jnp.sum(arrived.astype(jnp.float32), axis=0)
    own_count = lax.dynamic_index_in_dim(owner_counts[0], owner, axis=0, keepdims=False)
    own_valid = (jnp.arange(slot_cap, dtype=jnp.int32) < own_count)[:, None, None]
    own_grad = jnp.where(own_valid, own_grad, 0.0)

    partial = pl.pallas_call(
        contrib_kernel,
        out_shape=jax.ShapeDtypeStruct((tokens, width), bf16),
        in_specs=[SMEM] * 3 + [VMEM] * 2,
        out_specs=VMEM,
        scratch_shapes=[pltpu.SMEM((tile_total + 8,), jnp.int32)],
        compiler_params=params,
        cost_estimate=pl.CostEstimate(flops=0, bytes_accessed=1 << 16, transcendentals=0),
        name="contribs",
    )(tile_rows, tile_cols, owner_counts, grads, delta_all)

    rows = tokens // (2 * nx)
    blocks = partial.reshape(nx, 2, rows, width)
    keep = lax.dynamic_index_in_dim(blocks, core, axis=1, keepdims=False)
    give = lax.dynamic_index_in_dim(blocks, 1 - core, axis=1, keepdims=False)
    taken = shift(give, "core", 1)
    pair = (keep.astype(jnp.float32) + taken.astype(jnp.float32)).astype(bf16)

    def block(away):
        return lax.dynamic_index_in_dim(pair, (x + away) % nx, axis=0, keepdims=False)

    mine = block(0).astype(jnp.float32)
    for away in range(1, nx):
        mine = mine + shift(block(away), "x", away).astype(jnp.float32)
    own_grad, mine = lax.optimization_barrier((own_grad, mine.astype(bf16)))
    input_grad = lax.all_gather(mine, ("x", "core"), axis=0, tiled=True)

    def total_over(value, axes):
        return jnp.sum(spread(jnp.broadcast_to(value[None, None], (8, TILE)), axes)[:, 0, 0])

    squares = total_over(jnp.sum(own_grad * own_grad), ("y", "x", "core"))
    squares = total_over(squares, "z")
    root_mean = jnp.sqrt(
        squares / (nx * 2 * tile_total * TILE * TILE) + 1e-06
    )
    factor = jnp.minimum(1.0, 1.0 / root_mean)
    new_delta, new_first, new_second = adam_update(
        own_grad.transpose(0, 2, 1)[None], own_valid[None], delta_value, moment_one,
        moment_two, factor,
    )
    return (input_grad, new_delta, new_first, new_second)


def solution(mesh):
    grid = Mesh(mesh.devices.reshape(4, 16, 4, 2), ("y", "z", "x", "core"))
    dp, tensor = ("y", "z"), ("x", "core")
    tokens = P(dp, tensor)
    lists = P(tensor, None)
    slots = P(tensor, dp, None, None)
    return jax.shard_map(
        body,
        mesh=grid,
        in_specs=(tokens,) * 4 + (lists,) * 3 + (slots,) * 3,
        out_specs=(P(dp, None),) + (slots,) * 3,
        check_vma=False,
    )
```

```python
import jax
import jax.numpy as jnp
from jax import lax
from jax.experimental import pallas as pl
from jax.experimental.pallas import tpu as pltpu
from jax.sharding import Mesh, PartitionSpec as P

NY, NM, NX = 4, 8, 4
Z = ("m", "p")
TILE = 128
SLOT_CAP = 2
GROUP = 2 * NM * SLOT_CAP
BF16, F32 = jnp.bfloat16, jnp.float32
SMEM = pl.BlockSpec(memory_space=pltpu.SMEM)
VMEM = pl.BlockSpec(memory_space=pltpu.VMEM)
ANY = pl.BlockSpec(memory_space=pl.ANY)
SHAPE = jax.ShapeDtypeStruct


def kernel_call(kernel, name, outs, ins, out_specs, scratch=(), flops=0, moved=1 << 20):
    return pl.pallas_call(
        kernel,
        out_shape=outs,
        in_specs=ins,
        out_specs=out_specs,
        scratch_shapes=scratch,
        compiler_params=pltpu.CompilerParams(vmem_limit_bytes=48 * 1024 * 1024),
        cost_estimate=pl.CostEstimate(flops=flops, bytes_accessed=moved, transcendentals=0),
        name=name,
    )


def shift(value, axis, step):
    size = lax.axis_size(axis)
    return lax.ppermute(value, axis, [(i, (i + step) % size) for i in range(size)])


def exchange(value, axis):
    return lax.all_to_all(value, axis, split_axis=0, concat_axis=0, tiled=True)


def spread(value, axis):
    copies = jnp.broadcast_to(value[None], (lax.axis_size(axis),) + value.shape)
    return exchange(copies, axis)


def gate_kernel(ids_ref, gate_ref, up_ref, hidden_ref, grad_ref, turned_ref):
    blocks = 2 * NX
    rows = grad_ref.shape[1] // blocks
    core = ids_ref[3]
    for col in range(grad_ref.shape[0]):
        cut = slice(col * TILE, (col + 1) * TILE)
        gate = gate_ref[:, cut].astype(F32)
        sig = 1.0 / (1.0 + jnp.exp(-gate))
        value = (
            hidden_ref[:, cut].astype(F32)
            * up_ref[:, cut].astype(F32)
            * sig
            * (1.0 + gate * (1.0 - sig))
        )
        for block in range(blocks):
            place = pl.multiple_of((((block & 1) ^ core) * NX + (block >> 1)) * rows, rows)
            part = value[block * rows : (block + 1) * rows]
            grad_ref[col, pl.ds(place, rows)] = part.astype(BF16)
        turned_ref[col] = value.T.astype(BF16)


def load_features(own_ref, other_ref, features, sems, starts_ref, counts_ref):
    first = pltpu.make_async_copy(own_ref, features.at[0], sems.at[0])
    second = pltpu.make_async_copy(other_ref, features.at[1], sems.at[1])
    first.start()
    second.start()

    def owner_step(owner, start):
        starts_ref[owner] = start
        return start + counts_ref[0, owner]

    lax.fori_loop(0, counts_ref.shape[1], owner_step, 0)
    first.wait()
    second.wait()


def slot_products(group, owners, put, ids_ref, rows_ref, cols_ref, starts_ref, features, turned_ref):
    core = ids_ref[3]
    last = rows_ref.shape[1] - 1
    per_step = 4

    def step(index, carry):
        for part in range(per_step):
            owner = owners[0] + index * per_step + part
            start = starts_ref[group * 2 * NM + owner]
            for rank in range(SLOT_CAP):
                k = jnp.minimum(start + rank, last)
                row = rows_ref[0, k]
                lane = pl.multiple_of((row & 7) * TILE, TILE)
                x = features[((row >> 3) & 1) ^ core, row >> 4, :, pl.ds(lane, TILE)]
                term = jnp.dot(turned_ref[cols_ref[0, k]], x, preferred_element_type=F32)
                put((index * per_step + part) * SLOT_CAP + rank, term.astype(BF16))
        return carry

    lax.fori_loop(0, (owners[1] - owners[0]) // per_step, step, 0)


def far_kernel(
    ids_ref, rows_ref, cols_ref, counts_ref, own_ref, other_ref, turned_ref,
    low_ref, high_ref, features, starts_ref, sems,
):
    load_features(own_ref, other_ref, features, sems, starts_ref, counts_ref)
    group = (ids_ref[0] + 2) & (NY - 1)
    for ref, owners in ((low_ref, (0, NM)), (high_ref, (NM, 2 * NM))):

        def put(slot, term, ref=ref):
            ref[slot] = term

        slot_products(
            group, owners, put, ids_ref, rows_ref, cols_ref, starts_ref, features, turned_ref
        )


def near_kernel(
    ids_ref, rows_ref, cols_ref, counts_ref, own_ref, other_ref, turned_ref,
    up_ref, down_ref, mine_ref, features, starts_ref, sems,
):
    load_features(own_ref, other_ref, features, sems, starts_ref, counts_ref)
    for ref, away in ((up_ref, 1), (down_ref, 3), (mine_ref, 0)):

        def put(slot, term, ref=ref):
            ref[slot] = term

        slot_products(
            (ids_ref[0] + away) & (NY - 1), (0, 2 * NM), put,
            ids_ref, rows_ref, cols_ref, starts_ref, features, turned_ref,
        )


def passing_kernel(up_ref, low_ref, down_ref, high_ref, up_out, down_out):
    half = GROUP // 2
    up_out[:half] = (up_ref[:half].astype(F32) + low_ref[...].astype(F32)).astype(BF16)
    up_out[half:] = up_ref[half:]
    down_out[:half] = down_ref[:half]
    down_out[half:] = (down_ref[half:].astype(F32) + high_ref[...].astype(F32)).astype(BF16)


def y_sum_kernel(ids_ref, mine_ref, below_ref, above_ref, keep_ref, low_ref, high_ref):
    parity = ids_ref[1] & 1
    for m in range(NM):

        def total(side):
            return (
                mine_ref[m, side].astype(F32)
                + below_ref[m, side].astype(F32)
                + above_ref[m, side].astype(F32)
            ).astype(BF16)

        keep_ref[m] = total(parity)
        if m < NM // 2:
            low_ref[m] = total(1 - parity)
        else:
            high_ref[m - NM // 2] = total(1 - parity)


def pair_sum_kernel(keep_ref, low_ref, high_ref, out_ref):
    half = NM // 2
    out_ref[:half] = (keep_ref[:half].astype(F32) + low_ref[...].astype(F32)).astype(BF16)
    out_ref[half:] = (keep_ref[half:].astype(F32) + high_ref[...].astype(F32)).astype(BF16)


def own_grad_kernel(ids_ref, counts_ref, arrived_ref, grad_ref, squares_ref):
    count = counts_ref[0, ids_ref[0] * 2 * NM + ids_ref[1]]
    squares = jnp.zeros((TILE, TILE), F32)
    for rank in range(SLOT_CAP):
        total = arrived_ref[0, rank].astype(F32)
        for m in range(1, NM):
            total = total + arrived_ref[m, rank].astype(F32)
        total = jnp.where(rank < count, total, 0.0)
        grad_ref[rank] = total
        squares = squares + total * total
    squares_ref[...] = jnp.broadcast_to(jnp.sum(squares), squares_ref.shape)


def relay_kernel(arrived_ref, out_ref):
    total = jnp.sum(arrived_ref[...], axis=0, keepdims=True)
    out_ref[...] = jnp.broadcast_to(total, out_ref.shape)


def adam_kernel(
    count_all, ids_ref, counts_ref, arrived_ref, grad_ref, delta_ref, one_ref, two_ref,
    new_delta_ref, new_one_ref, new_two_ref,
):
    squares = jnp.sum(arrived_ref[...], axis=0)[0:1]
    factor = jnp.minimum(1.0, 1.0 / jnp.sqrt(squares / count_all + 1e-06))
    count = counts_ref[0, ids_ref[0] * 2 * NM + ids_ref[1]]
    for rank in range(SLOT_CAP):
        live = rank < count
        clipped = factor * grad_ref[rank].T
        delta, one, two = delta_ref[0, rank], one_ref[0, rank], two_ref[0, rank]
        first = 0.9 * one + 0.1 * clipped
        second = 0.95 * two + 0.05 * clipped * clipped
        size = first / (1.0 - 0.9**10) / (jnp.sqrt(second / (1.0 - 0.95**10)) + 1e-08)
        updated = delta - 0.02 * (size + 0.1 * delta)
        new_delta_ref[0, rank] = jnp.where(live, updated, delta)
        new_one_ref[0, rank] = jnp.where(live, first, one)
        new_two_ref[0, rank] = jnp.where(live, second, two)


def contrib_kernel(
    ids_ref, rows_ref, cols_ref, counts_ref, grad_ref, delta_ref, stay_ref, give_ref, places_ref
):
    stay_ref[...] = jnp.zeros_like(stay_ref)
    give_ref[...] = jnp.zeros_like(give_ref)
    half = stay_ref.shape[0]
    y = ids_ref[0]

    def owner_step(owner, start):
        place = ((owner & 15) * NY + (((owner >> 4) - y) & (NY - 1))) * SLOT_CAP
        places_ref[start] = place
        places_ref[start + 1] = place + 1
        return start + counts_ref[0, owner]

    lax.fori_loop(0, counts_ref.shape[1], owner_step, 0)
    per_step = 4

    def step(index, carry):
        last, total = carry
        for part in range(per_step):
            k = index * per_step + part
            row = rows_ref[0, k]
            product = lax.dot_general(
                grad_ref[cols_ref[0, k]], delta_ref[places_ref[k]],
                (((1,), (1,)), ((), ())), preferred_element_type=F32,
            )
            total = jnp.where(row == last, total, 0.0) + product
            lane = pl.multiple_of(row * TILE, TILE)
            stay_ref[:, pl.ds(lane, TILE)] = total[:half].astype(BF16)
            give_ref[:, pl.ds(lane, TILE)] = total[half:].astype(BF16)
            last = row
        return last, total

    lax.fori_loop(
        0, rows_ref.shape[1] // per_step, step,
        (jnp.int32(-1), jnp.zeros((TILE, TILE), F32)),
    )


def core_sum_kernel(ids_ref, stay_ref, taken_ref, *out_refs):
    for away, ref in enumerate(out_refs):
        at = (ids_ref[2] + away) & (NX - 1)
        ref[...] = (stay_ref[at].astype(F32) + taken_ref[at].astype(F32)).astype(BF16)


def copy_kernel(in_ref, out_ref, sem):
    copy = pltpu.make_async_copy(in_ref, out_ref, sem)
    copy.start()
    copy.wait()


def body(
    features, gate_pre, up_pre, hidden_grad, tile_rows, tile_cols, owner_counts,
    delta_value, moment_one, moment_two,
):
    ids = jnp.stack([lax.axis_index(name) for name in ("y", Z, "x", "core")]).astype(jnp.int32)
    tokens, hidden = gate_pre.shape
    shard_width = features.shape[1]
    width = shard_width * NX * 2
    tile_total = tile_rows.shape[1]
    lists = (tile_rows, tile_cols, owner_counts)

    own = spread(features, "x")
    other = shift(own, "core", 1)

    delta_half = delta_value[0].astype(BF16)
    delta_y = jnp.concatenate(
        [delta_half] + [shift(delta_half, "y", -away) for away in range(1, NY)], axis=0
    )
    _, delta_y = lax.optimization_barrier((own, delta_y))
    delta_all = lax.all_gather(delta_y, Z, axis=0, tiled=True)

    grads, turned = kernel_call(
        gate_kernel, "gate", [SHAPE((hidden // TILE, tokens, TILE), BF16)] * 2,
        [SMEM] + [VMEM] * 3, [VMEM] * 2, flops=tokens * hidden * 12, moved=tokens * hidden * 10,
    )(ids, gate_pre, up_pre, hidden_grad)

    tile_ins = [SMEM] * 4 + [ANY, ANY, VMEM]
    tile_scratch = [
        pltpu.VMEM((2, NX, tokens, shard_width), BF16),
        pltpu.SMEM((owner_counts.shape[1],), jnp.int32),
        pltpu.SemaphoreType.DMA((2,)),
    ]
    half = (GROUP // 2, TILE, TILE)
    whole = (GROUP, TILE, TILE)
    low, high = kernel_call(
        far_kernel, "tiles_far", [SHAPE(half, BF16)] * 2, tile_ins, [VMEM] * 2, tile_scratch,
        flops=2 * GROUP * TILE**3, moved=4 << 20,
    )(ids, *lists, own, other, turned)

    low = shift(low, "y", 1)
    high = shift(high, "y", -1)
    up, down, mine = kernel_call(
        near_kernel, "tiles_near", [SHAPE(whole, BF16)] * 3, tile_ins, [VMEM] * 3, tile_scratch,
        flops=6 * GROUP * TILE**3, moved=4 << 20,
    )(ids, *lists, own, other, turned)
    up, down = kernel_call(
        passing_kernel, "passing", [SHAPE(whole, BF16)] * 2, [VMEM] * 4, [VMEM] * 2
    )(up, low, down, high)
    below = shift(up, "y", 1)
    above = shift(down, "y", -1)
    parted = (NM, 2, SLOT_CAP, TILE, TILE)
    quarter = SHAPE((NM // 2, SLOT_CAP, TILE, TILE), BF16)
    kept = SHAPE((NM, SLOT_CAP, TILE, TILE), BF16)
    keep, low, high = kernel_call(
        y_sum_kernel, "y_sum", [kept, quarter, quarter], [SMEM] + [VMEM] * 3, [VMEM] * 3
    )(ids, mine.reshape(parted), below.reshape(parted), above.reshape(parted))

    low = shift(low, Z, 1)
    high = shift(high, Z, -1)
    pairs = kernel_call(pair_sum_kernel, "pair_sum", kept, [VMEM] * 3, VMEM)(keep, low, high)
    pairs, grads = lax.optimization_barrier((pairs, grads))
    arrived = exchange(pairs, "m")
    own_grad, squares = kernel_call(
        own_grad_kernel, "own_grad",
        [SHAPE((SLOT_CAP, TILE, TILE), F32), SHAPE((NY * NX * 2, 8, TILE), F32)],
        [SMEM, SMEM, VMEM], [VMEM] * 2,
    )(ids, owner_counts, arrived)

    stay, give = kernel_call(
        contrib_kernel, "contribs", [SHAPE((tokens // 2, width), BF16)] * 2,
        [SMEM] * 4 + [VMEM] * 2, [VMEM] * 2, [pltpu.SMEM((tile_total + 8,), jnp.int32)],
        moved=1 << 12,
    )(ids, *lists, grads, delta_all)

    rows = tokens // (2 * NX)
    taken = shift(give, "core", 1)
    share, *others = kernel_call(
        core_sum_kernel, "core_sum", [SHAPE((rows, width), BF16)] * NX,
        [SMEM] + [VMEM] * 2, [VMEM] * NX, moved=1 << 12,
    )(ids, stay.reshape(NX, rows, width), taken.reshape(NX, rows, width))
    share = share.astype(F32)
    for away, part in enumerate(others):
        share = share + shift(part, "x", away + 1).astype(F32)
    squares, share = lax.optimization_barrier((squares, share.astype(BF16)))
    gathered = lax.all_gather(share, ("x", "core"), axis=0, tiled=True)
    input_grad = kernel_call(
        copy_kernel, "result", SHAPE((tokens, width), BF16), [ANY], ANY,
        [pltpu.SemaphoreType.DMA], moved=4 << 20,
    )(gathered)

    squares = exchange(squares, ("y", "x", "core"))
    squares = kernel_call(relay_kernel, "relay", SHAPE((2 * NM, 8, TILE), F32), [VMEM], VMEM)(squares)
    squares = exchange(squares, Z)
    squares, input_grad = lax.optimization_barrier((squares, input_grad))
    count_all = float(NX * 2 * tile_total * TILE * TILE)

    def adam(*refs):
        adam_kernel(count_all, *refs)

    outs = kernel_call(
        adam, "adam", [SHAPE(delta_value.shape, F32)] * 3, [SMEM] * 2 + [VMEM] * 5, [VMEM] * 3
    )(ids, owner_counts, squares, own_grad, delta_value, moment_one, moment_two)
    return (input_grad, *outs)


def solution(mesh):
    grid = Mesh(mesh.devices.reshape(NY, NM, 2, NX, 2), ("y", "m", "p", "x", "core"))
    dp, tensor = ("y", "m", "p"), ("x", "core")
    tokens = P(dp, tensor)
    lists = P(tensor, None)
    slots = P(tensor, dp, None, None)
    return jax.shard_map(
        body,
        mesh=grid,
        in_specs=(tokens,) * 4 + (lists,) * 3 + (slots,) * 3,
        out_specs=(P(dp, None),) + (slots,) * 3,
        check_vma=False,
    )
```

```python
import functools

import jax
import jax.numpy as jnp
from jax import lax
from jax.experimental import pallas as pl
from jax.experimental.pallas import tpu as pltpu
from jax.sharding import Mesh, PartitionSpec as P

NY, NM, NX = 4, 8, 4
Z = ("m", "p")
TILE = 128
SLOT_CAP = 2
BF16, F32 = jnp.bfloat16, jnp.float32
SMEM = pl.BlockSpec(memory_space=pltpu.SMEM)
VMEM = pl.BlockSpec(memory_space=pltpu.VMEM)
ANY = pl.BlockSpec(memory_space=pl.ANY)
SHAPE = jax.ShapeDtypeStruct


def kernel_call(
    kernel, name, outs, ins, out_specs, scratch=(), flops=0, moved=1 << 20, vmem=48
):
    return pl.pallas_call(
        kernel,
        out_shape=outs,
        in_specs=ins,
        out_specs=out_specs,
        scratch_shapes=scratch,
        compiler_params=pltpu.CompilerParams(vmem_limit_bytes=vmem * 1024 * 1024),
        cost_estimate=pl.CostEstimate(flops=flops, bytes_accessed=moved, transcendentals=0),
        name=name,
    )


def shift(value, axis, step):
    size = lax.axis_size(axis)
    return lax.ppermute(value, axis, [(i, (i + step) % size) for i in range(size)])


def exchange(value, axis):
    return lax.all_to_all(value, axis, split_axis=0, concat_axis=0, tiled=True)


def spread(value, axis):
    copies = jnp.broadcast_to(value[None], (lax.axis_size(axis),) + value.shape)
    return exchange(copies, axis)


def gate_kernel(ids_ref, gate_ref, up_ref, hidden_ref, grad_ref, turned_ref):
    blocks = 2 * NX
    rows = grad_ref.shape[2] // NX
    core = ids_ref[3]
    for col in range(turned_ref.shape[0]):
        cut = slice(col * TILE, (col + 1) * TILE)
        gate = gate_ref[:, cut].astype(F32)
        sig = 1.0 / (1.0 + jnp.exp(-gate))
        value = (
            hidden_ref[:, cut].astype(F32)
            * up_ref[:, cut].astype(F32)
            * sig
            * (1.0 + gate * (1.0 - sig))
        )
        for block in range(blocks):
            part = value[block * rows : (block + 1) * rows].astype(BF16)
            place = (block >> 1) * rows
            grad_ref[(block & 1) ^ core, col, place : place + rows] = part
        turned_ref[col] = value.T.astype(BF16)


def load_features(own_ref, other_ref, features, sems, starts_ref, counts_ref):
    first = pltpu.make_async_copy(own_ref, features.at[0], sems.at[0])
    second = pltpu.make_async_copy(other_ref, features.at[1], sems.at[1])
    first.start()
    second.start()

    def owner_step(owner, start):
        starts_ref[owner] = start
        return start + counts_ref[0, owner]

    lax.fori_loop(0, counts_ref.shape[1], owner_step, 0)
    first.wait()
    second.wait()


def slot_products(
    parity, away, span, put, ids_ref, rows_ref, cols_ref, starts_ref, features, turned_ref
):
    core = ids_ref[3]
    last = rows_ref.shape[1] - 1
    group = (ids_ref[0] + away) & (NY - 1)
    per_step = 4

    def step(index, carry):
        for part in range(per_step):
            m = span[0] + index * per_step + part
            start = starts_ref[(group * NM + m) * 2 + parity]
            for rank in range(SLOT_CAP):
                k = jnp.minimum(start + rank, last)
                row = rows_ref[0, k]
                lane = pl.multiple_of((row & 7) * TILE, TILE)
                x = features[((row >> 3) & 1) ^ core, row >> 4, :, pl.ds(lane, TILE)]
                term = jnp.dot(turned_ref[cols_ref[0, k]], x, preferred_element_type=F32)
                put(m - span[0], rank, term.astype(BF16))
        return carry

    lax.fori_loop(0, (span[1] - span[0]) // per_step, step, 0)


def give_kernel(
    ids_ref, rows_ref, cols_ref, counts_ref, own_ref, other_ref, turned_ref,
    low_ref, high_ref, features, starts_ref, sems,
):
    load_features(own_ref, other_ref, features, sems, starts_ref, counts_ref)
    parity = 1 - (ids_ref[1] & 1)
    for away in range(NY):
        for ref, span in ((low_ref, (0, NM // 2)), (high_ref, (NM // 2, NM))):

            def put(m, rank, term, ref=ref, away=away):
                ref[away, m, rank] = term

            slot_products(
                parity, away, span, put,
                ids_ref, rows_ref, cols_ref, starts_ref, features, turned_ref,
            )


def keep_kernel(
    ids_ref, rows_ref, cols_ref, counts_ref, own_ref, other_ref, turned_ref,
    keep_ref, features, starts_ref, sems,
):
    load_features(own_ref, other_ref, features, sems, starts_ref, counts_ref)
    parity = ids_ref[1] & 1
    for away in range(NY):

        def put(m, rank, term, away=away):
            keep_ref[away, m, rank] = term

        slot_products(
            parity, away, (0, NM), put,
            ids_ref, rows_ref, cols_ref, starts_ref, features, turned_ref,
        )


def pair_sum(keep_ref, low_ref, high_ref, away, m):
    half = NM // 2
    other = low_ref[away, m] if m < half else high_ref[away, m - half]
    return keep_ref[away, m].astype(F32) + other.astype(F32)


def far_kernel(keep_ref, low_ref, high_ref, far_low_ref, far_high_ref):
    half = NM // 2
    for m in range(NM):
        ref = far_low_ref if m < half else far_high_ref
        ref[m % half] = pair_sum(keep_ref, low_ref, high_ref, 2, m).astype(BF16)


def near_kernel(
    keep_ref, low_ref, high_ref, far_low_ref, far_high_ref, up_ref, down_ref
):
    half = NM // 2
    for m in range(NM):
        up = pair_sum(keep_ref, low_ref, high_ref, 1, m)
        down = pair_sum(keep_ref, low_ref, high_ref, 3, m)
        if m < half:
            up = up + far_low_ref[m].astype(F32)
        else:
            down = down + far_high_ref[m - half].astype(F32)
        up_ref[m] = up.astype(BF16)
        down_ref[m] = down.astype(BF16)


def y_sum_kernel(keep_ref, low_ref, high_ref, below_ref, above_ref, out_ref):
    for m in range(NM):
        total = pair_sum(keep_ref, low_ref, high_ref, 0, m)
        total = total + below_ref[m].astype(F32) + above_ref[m].astype(F32)
        out_ref[m] = total.astype(BF16)


def own_grad_kernel(ids_ref, counts_ref, arrived_ref, grad_ref, squares_ref):
    count = counts_ref[0, ids_ref[0] * 2 * NM + ids_ref[1]]
    squares = jnp.zeros((TILE, TILE), F32)
    for rank in range(SLOT_CAP):
        total = arrived_ref[0, rank].astype(F32)
        for m in range(1, NM):
            total = total + arrived_ref[m, rank].astype(F32)
        total = jnp.where(rank < count, total, 0.0)
        grad_ref[rank] = total
        squares = squares + total * total
    squares_ref[...] = jnp.broadcast_to(jnp.sum(squares), squares_ref.shape)


def relay_kernel(arrived_ref, out_ref):
    total = jnp.sum(arrived_ref[...], axis=0, keepdims=True)
    out_ref[...] = jnp.broadcast_to(total, out_ref.shape)


def adam_kernel(
    count_all, ids_ref, counts_ref, arrived_ref, grad_ref, delta_ref, one_ref, two_ref,
    new_delta_ref, new_one_ref, new_two_ref,
):
    squares = jnp.sum(arrived_ref[...], axis=0)[0:1]
    factor = jnp.minimum(1.0, 1.0 / jnp.sqrt(squares / count_all + 1e-06))
    count = counts_ref[0, ids_ref[0] * 2 * NM + ids_ref[1]]
    for rank in range(SLOT_CAP):
        live = rank < count
        clipped = factor * grad_ref[rank].T
        delta, one, two = delta_ref[0, rank], one_ref[0, rank], two_ref[0, rank]
        first = 0.9 * one + 0.1 * clipped
        second = 0.95 * two + 0.05 * clipped * clipped
        size = first / (1.0 - 0.9**10) / (jnp.sqrt(second / (1.0 - 0.95**10)) + 1e-08)
        updated = delta - 0.02 * (size + 0.1 * delta)
        new_delta_ref[0, rank] = jnp.where(live, updated, delta)
        new_one_ref[0, rank] = jnp.where(live, first, one)
        new_two_ref[0, rank] = jnp.where(live, second, two)


def contrib_kernel(
    side, ids_ref, rows_ref, cols_ref, counts_ref, grad_ref, delta_ref, out_ref, places_ref
):
    out_ref[...] = jnp.zeros_like(out_ref)
    y = ids_ref[0]

    def owner_step(owner, start):
        place = ((owner & 15) * NY + (((owner >> 4) - y) & (NY - 1))) * SLOT_CAP
        places_ref[start] = place
        places_ref[start + 1] = place + 1
        return start + counts_ref[0, owner]

    lax.fori_loop(0, counts_ref.shape[1], owner_step, 0)
    per_step = 4

    def step(index, carry):
        last, total = carry
        for part in range(per_step):
            k = index * per_step + part
            row = rows_ref[0, k]
            product = lax.dot_general(
                grad_ref[side, cols_ref[0, k]], delta_ref[places_ref[k]],
                (((1,), (1,)), ((), ())), preferred_element_type=F32,
            )
            total = jnp.where(row == last, total, 0.0) + product
            lane = pl.multiple_of(row * TILE, TILE)
            out_ref[:, pl.ds(lane, TILE)] = total.astype(BF16)
            last = row
        return last, total

    lax.fori_loop(
        0, rows_ref.shape[1] // per_step, step,
        (jnp.int32(-1), jnp.zeros((out_ref.shape[0], TILE), F32)),
    )


def core_sum_kernel(ids_ref, stay_ref, taken_ref, *out_refs):
    for away, ref in enumerate(out_refs):
        at = (ids_ref[2] + away) & (NX - 1)
        ref[...] = (stay_ref[at].astype(F32) + taken_ref[at].astype(F32)).astype(BF16)


def copy_kernel(in_ref, out_ref, sem):
    copy = pltpu.make_async_copy(in_ref, out_ref, sem)
    copy.start()
    copy.wait()


def body(
    features, gate_pre, up_pre, hidden_grad, tile_rows, tile_cols, owner_counts,
    delta_value, moment_one, moment_two,
):
    ids = jnp.stack([lax.axis_index(name) for name in ("y", Z, "x", "core")]).astype(jnp.int32)
    tokens, hidden = gate_pre.shape
    shard_width = features.shape[1]
    width = shard_width * NX * 2
    tile_total = tile_rows.shape[1]
    lists = (tile_rows, tile_cols, owner_counts)

    own = spread(features, "x")
    other = shift(own, "core", 1)

    delta_half = delta_value[0].astype(BF16)
    delta_y = jnp.concatenate(
        [delta_half] + [shift(delta_half, "y", -away) for away in range(1, NY)], axis=0
    )
    _, delta_y = lax.optimization_barrier((own, delta_y))
    delta_all = lax.all_gather(delta_y, Z, axis=0, tiled=True)

    grads, turned = kernel_call(
        gate_kernel, "gate",
        [
            SHAPE((2, hidden // TILE, tokens // 2, TILE), BF16),
            SHAPE((hidden // TILE, TILE, tokens), BF16),
        ],
        [SMEM] + [VMEM] * 3, [VMEM] * 2, flops=tokens * hidden * 12, moved=tokens * hidden * 10,
    )(ids, gate_pre, up_pre, hidden_grad)

    tile_ins = [SMEM] * 4 + [ANY, ANY, VMEM]
    tile_scratch = [
        pltpu.VMEM((2, NX, tokens, shard_width), BF16),
        pltpu.SMEM((owner_counts.shape[1],), jnp.int32),
        pltpu.SemaphoreType.DMA((2,)),
    ]
    half = SHAPE((NM // 2, SLOT_CAP, TILE, TILE), BF16)
    whole = SHAPE((NM, SLOT_CAP, TILE, TILE), BF16)
    halves = SHAPE((NY,) + half.shape, BF16)

    low, high = kernel_call(
        give_kernel, "give", [halves] * 2, tile_ins, [VMEM] * 2, tile_scratch,
        flops=tile_total * TILE**3, moved=4 << 20,
    )(ids, *lists, own, other, turned)
    low = shift(low, Z, 1)
    high = shift(high, Z, -1)
    keep = kernel_call(
        keep_kernel, "keep", SHAPE((NY,) + whole.shape, BF16), tile_ins, VMEM, tile_scratch,
        flops=tile_total * TILE**3, moved=4 << 20,
    )(ids, *lists, own, other, turned)

    far_low, far_high = kernel_call(far_kernel, "far", [half] * 2, [VMEM] * 3, [VMEM] * 2)(
        keep, low, high
    )
    far_low = shift(far_low, "y", 1)
    far_high = shift(far_high, "y", -1)
    up, down = kernel_call(near_kernel, "near", [whole] * 2, [VMEM] * 5, [VMEM] * 2)(
        keep, low, high, far_low, far_high
    )
    below = shift(up, "y", 1)
    above = shift(down, "y", -1)
    pairs = kernel_call(y_sum_kernel, "y_sum", whole, [VMEM] * 5, VMEM)(
        keep, low, high, below, above
    )

    pairs, grads = lax.optimization_barrier((pairs, grads))
    arrived = exchange(pairs, "m")
    own_grad, squares = kernel_call(
        own_grad_kernel, "own_grad",
        [SHAPE((SLOT_CAP, TILE, TILE), F32), SHAPE((NY * NX * 2, 8, TILE), F32)],
        [SMEM, SMEM, VMEM], [VMEM] * 2,
    )(ids, owner_counts, arrived)

    def contribs(side):
        return kernel_call(
            functools.partial(contrib_kernel, side), "contribs",
            SHAPE((tokens // 2, width), BF16), [SMEM] * 4 + [VMEM] * 2, VMEM,
            [pltpu.SMEM((tile_total + 8,), jnp.int32)], moved=1 << 12,
        )(ids, *lists, grads, delta_all)

    give, stay = contribs(1), contribs(0)

    rows = tokens // (2 * NX)
    taken = shift(give, "core", 1)
    share, *others = kernel_call(
        core_sum_kernel, "core_sum", [SHAPE((rows, width), BF16)] * NX,
        [SMEM] + [VMEM] * 2, [VMEM] * NX, moved=1 << 12,
    )(ids, stay.reshape(NX, rows, width), taken.reshape(NX, rows, width))
    others = [shift(part, "x", away + 1) for away, part in enumerate(others)]

    squares = exchange(squares, ("y", "x", "core"))
    squares = kernel_call(relay_kernel, "relay", SHAPE((2 * NM, 8, TILE), F32), [VMEM], VMEM)(squares)
    squares, share, *others = lax.optimization_barrier((squares, share, *others))
    for part in others:
        share = share.astype(F32) + part.astype(F32)
    gathered = lax.all_gather(share.astype(BF16), ("x", "core"), axis=0, tiled=True)
    input_grad = kernel_call(
        copy_kernel, "result", SHAPE((tokens, width), BF16), [ANY], ANY,
        [pltpu.SemaphoreType.DMA], moved=4 << 20, vmem=63,
    )(gathered)
    squares = exchange(squares, Z)
    squares, input_grad = lax.optimization_barrier((squares, input_grad))
    count_all = float(NX * 2 * tile_total * TILE * TILE)

    outs = kernel_call(
        functools.partial(adam_kernel, count_all), "adam", [SHAPE(delta_value.shape, F32)] * 3, [SMEM] * 2 + [VMEM] * 5, [VMEM] * 3
    )(ids, owner_counts, squares, own_grad, delta_value, moment_one, moment_two)
    return (input_grad, *outs)


def solution(mesh):
    grid = Mesh(mesh.devices.reshape(NY, NM, 2, NX, 2), ("y", "m", "p", "x", "core"))
    dp, tensor = ("y", "m", "p"), ("x", "core")
    tokens = P(dp, tensor)
    lists = P(tensor, None)
    slots = P(tensor, dp, None, None)
    return jax.shard_map(
        body,
        mesh=grid,
        in_specs=(tokens,) * 4 + (lists,) * 3 + (slots,) * 3,
        out_specs=(P(dp, None),) + (slots,) * 3,
        check_vma=False,
    )
```

```python
import functools

import jax
import jax.numpy as jnp
from jax import lax
from jax.experimental import pallas as pl
from jax.experimental.pallas import tpu as pltpu
from jax.sharding import Mesh, PartitionSpec as P

NY, NM, NX = 4, 8, 4
Z = ("m", "p")
TILE = 128
SLOT_CAP = 2
GROUP = 2 * NM * SLOT_CAP
BF16, F32 = jnp.bfloat16, jnp.float32
SMEM = pl.BlockSpec(memory_space=pltpu.SMEM)
VMEM = pl.BlockSpec(memory_space=pltpu.VMEM)
ANY = pl.BlockSpec(memory_space=pl.ANY)
SHAPE = jax.ShapeDtypeStruct


def kernel_call(kernel, name, outs, ins, out_specs, scratch=(), flops=0, moved=1 << 20):
    return pl.pallas_call(
        kernel,
        out_shape=outs,
        in_specs=ins,
        out_specs=out_specs,
        scratch_shapes=scratch,
        compiler_params=pltpu.CompilerParams(vmem_limit_bytes=48 * 1024 * 1024),
        cost_estimate=pl.CostEstimate(flops=flops, bytes_accessed=moved, transcendentals=0),
        name=name,
    )


def shift(value, axis, step):
    size = lax.axis_size(axis)
    return lax.ppermute(value, axis, [(i, (i + step) % size) for i in range(size)])


def exchange(value, axis):
    return lax.all_to_all(value, axis, split_axis=0, concat_axis=0, tiled=True)


def spread(value, axis):
    copies = jnp.broadcast_to(value[None], (lax.axis_size(axis),) + value.shape)
    return exchange(copies, axis)


def gate_kernel(ids_ref, gate_ref, up_ref, hidden_ref, grad_ref, turned_ref):
    blocks = 2 * NX
    rows = grad_ref.shape[1] // blocks
    core = ids_ref[3]
    for col in range(grad_ref.shape[0]):
        cut = slice(col * TILE, (col + 1) * TILE)
        gate = gate_ref[:, cut].astype(F32)
        sig = 1.0 / (1.0 + jnp.exp(-gate))
        value = (
            hidden_ref[:, cut].astype(F32)
            * up_ref[:, cut].astype(F32)
            * sig
            * (1.0 + gate * (1.0 - sig))
        )
        for block in range(blocks):
            place = pl.multiple_of((((block & 1) ^ core) * NX + (block >> 1)) * rows, rows)
            part = value[block * rows : (block + 1) * rows]
            grad_ref[col, pl.ds(place, rows)] = part.astype(BF16)
        turned_ref[col] = value.T.astype(BF16)


def load_features(own_ref, other_ref, features, sems, starts_ref, counts_ref):
    first = pltpu.make_async_copy(own_ref, features.at[0], sems.at[0])
    second = pltpu.make_async_copy(other_ref, features.at[1], sems.at[1])
    first.start()
    second.start()

    def owner_step(owner, start):
        starts_ref[owner] = start
        return start + counts_ref[0, owner]

    lax.fori_loop(0, counts_ref.shape[1], owner_step, 0)
    first.wait()
    second.wait()


def slot_products(group, owners, put, ids_ref, rows_ref, cols_ref, starts_ref, features, turned_ref):
    core = ids_ref[3]
    last = rows_ref.shape[1] - 1
    per_step = 4

    def step(index, carry):
        for part in range(per_step):
            owner = owners[0] + index * per_step + part
            start = starts_ref[group * 2 * NM + owner]
            for rank in range(SLOT_CAP):
                k = jnp.minimum(start + rank, last)
                row = rows_ref[0, k]
                lane = pl.multiple_of((row & 7) * TILE, TILE)
                x = features[((row >> 3) & 1) ^ core, row >> 4, :, pl.ds(lane, TILE)]
                term = jnp.dot(turned_ref[cols_ref[0, k]], x, preferred_element_type=F32)
                put((index * per_step + part) * SLOT_CAP + rank, term.astype(BF16))
        return carry

    lax.fori_loop(0, (owners[1] - owners[0]) // per_step, step, 0)


def tile_kernel(
    aways, ids_ref, rows_ref, cols_ref, counts_ref, own_ref, other_ref, turned_ref, *refs
):
    features, starts_ref, sems = refs[len(aways) :]
    load_features(own_ref, other_ref, features, sems, starts_ref, counts_ref)
    for ref, away in zip(refs, aways):

        def put(slot, term, ref=ref):
            ref[slot] = term

        slot_products(
            (ids_ref[0] + away) & (NY - 1), (0, 2 * NM), put,
            ids_ref, rows_ref, cols_ref, starts_ref, features, turned_ref,
        )


def y_sum_kernel(ids_ref, mine_ref, below_ref, above_ref, far_ref, keep_ref, low_ref, high_ref):
    parity = ids_ref[1] & 1
    for m in range(NM):

        def total(side):
            return (
                mine_ref[m, side].astype(F32)
                + below_ref[m, side].astype(F32)
                + above_ref[m, side].astype(F32)
                + far_ref[m, side].astype(F32)
            ).astype(BF16)

        keep_ref[m] = total(parity)
        if m < NM // 2:
            low_ref[m] = total(1 - parity)
        else:
            high_ref[m - NM // 2] = total(1 - parity)


def pair_sum_kernel(keep_ref, low_ref, high_ref, out_ref):
    half = NM // 2
    out_ref[:half] = (keep_ref[:half].astype(F32) + low_ref[...].astype(F32)).astype(BF16)
    out_ref[half:] = (keep_ref[half:].astype(F32) + high_ref[...].astype(F32)).astype(BF16)


def own_grad_kernel(ids_ref, counts_ref, arrived_ref, grad_ref, squares_ref):
    count = counts_ref[0, ids_ref[0] * 2 * NM + ids_ref[1]]
    squares = jnp.zeros((TILE, TILE), F32)
    for rank in range(SLOT_CAP):
        total = arrived_ref[0, rank].astype(F32)
        for m in range(1, NM):
            total = total + arrived_ref[m, rank].astype(F32)
        total = jnp.where(rank < count, total, 0.0)
        grad_ref[rank] = total
        squares = squares + total * total
    squares_ref[...] = jnp.broadcast_to(jnp.sum(squares), squares_ref.shape)


def relay_kernel(arrived_ref, out_ref):
    total = jnp.sum(arrived_ref[...], axis=0, keepdims=True)
    out_ref[...] = jnp.broadcast_to(total, out_ref.shape)


def adam_kernel(
    count_all, ids_ref, counts_ref, arrived_ref, grad_ref, delta_ref, one_ref, two_ref,
    new_delta_ref, new_one_ref, new_two_ref,
):
    squares = jnp.sum(arrived_ref[...], axis=0)[0:1]
    factor = jnp.minimum(1.0, 1.0 / jnp.sqrt(squares / count_all + 1e-06))
    count = counts_ref[0, ids_ref[0] * 2 * NM + ids_ref[1]]
    for rank in range(SLOT_CAP):
        live = rank < count
        clipped = factor * grad_ref[rank].T
        delta, one, two = delta_ref[0, rank], one_ref[0, rank], two_ref[0, rank]
        first = 0.9 * one + 0.1 * clipped
        second = 0.95 * two + 0.05 * clipped * clipped
        size = first / (1.0 - 0.9**10) / (jnp.sqrt(second / (1.0 - 0.95**10)) + 1e-08)
        updated = delta - 0.02 * (size + 0.1 * delta)
        new_delta_ref[0, rank] = jnp.where(live, updated, delta)
        new_one_ref[0, rank] = jnp.where(live, first, one)
        new_two_ref[0, rank] = jnp.where(live, second, two)


def turn_kernel(delta_ref, out_ref):
    for rank in range(SLOT_CAP):
        out_ref[rank] = delta_ref[0, rank].T.astype(BF16)


def contrib_kernel(
    ids_ref, rows_ref, cols_ref, counts_ref, grad_ref, delta_ref, stay_ref, give_ref, places_ref
):
    stay_ref[...] = jnp.zeros_like(stay_ref)
    give_ref[...] = jnp.zeros_like(give_ref)
    half = stay_ref.shape[0]
    y = ids_ref[0]

    def owner_step(owner, start):
        place = ((owner & 15) * NY + (((owner >> 4) - y) & (NY - 1))) * SLOT_CAP
        places_ref[start] = place
        places_ref[start + 1] = place + 1
        return start + counts_ref[0, owner]

    lax.fori_loop(0, counts_ref.shape[1], owner_step, 0)
    per_step = 28

    def step(index, carry):
        last, total = carry
        for part in range(per_step):
            k = index * per_step + part
            row = rows_ref[0, k]
            product = jnp.dot(
                grad_ref[cols_ref[0, k]], delta_ref[places_ref[k]], preferred_element_type=F32
            )
            total = jnp.where(row == last, total, 0.0) + product
            lane = pl.multiple_of(row * TILE, TILE)
            stay_ref[:, pl.ds(lane, TILE)] = total[:half].astype(BF16)
            give_ref[:, pl.ds(lane, TILE)] = total[half:].astype(BF16)
            last = row
        return last, total

    lax.fori_loop(
        0, rows_ref.shape[1] // per_step, step,
        (jnp.int32(-1), jnp.zeros((TILE, TILE), F32)),
    )


def core_sum_kernel(ids_ref, stay_ref, taken_ref, *out_refs):
    for away, ref in enumerate(out_refs):
        at = (ids_ref[2] + away) & (NX - 1)
        ref[...] = (stay_ref[at].astype(F32) + taken_ref[at].astype(F32)).astype(BF16)


def copy_kernel(in_ref, out_ref, sem):
    copy = pltpu.make_async_copy(in_ref, out_ref, sem)
    copy.start()
    copy.wait()


def body(
    features, gate_pre, up_pre, hidden_grad, tile_rows, tile_cols, owner_counts,
    delta_value, moment_one, moment_two,
):
    ids = jnp.stack([lax.axis_index(name) for name in ("y", Z, "x", "core")]).astype(jnp.int32)
    tokens, hidden = gate_pre.shape
    shard_width = features.shape[1]
    width = shard_width * NX * 2
    tile_total = tile_rows.shape[1]
    lists = (tile_rows, tile_cols, owner_counts)

    own = spread(features, "x")
    other = shift(own, "core", 1)

    delta_half = kernel_call(
        turn_kernel, "turn", SHAPE(delta_value.shape[1:], BF16), [VMEM], VMEM
    )(delta_value)
    delta_y = jnp.concatenate(
        [delta_half] + [shift(delta_half, "y", -away) for away in range(1, NY)], axis=0
    )
    _, delta_y = lax.optimization_barrier((own, delta_y))
    delta_all = lax.all_gather(delta_y, Z, axis=0, tiled=True)

    grads, turned = kernel_call(
        gate_kernel, "gate", [SHAPE((hidden // TILE, tokens, TILE), BF16)] * 2,
        [SMEM] + [VMEM] * 3, [VMEM] * 2, flops=tokens * hidden * 12, moved=tokens * hidden * 10,
    )(ids, gate_pre, up_pre, hidden_grad)

    tile_ins = [SMEM] * 4 + [ANY, ANY, VMEM]
    tile_scratch = [
        pltpu.VMEM((2, NX, tokens, shard_width), BF16),
        pltpu.SMEM((owner_counts.shape[1],), jnp.int32),
        pltpu.SemaphoreType.DMA((2,)),
    ]

    def terms(*aways):
        return kernel_call(
            functools.partial(tile_kernel, aways), "tiles",
            [SHAPE((GROUP, TILE, TILE), BF16)] * len(aways), tile_ins, [VMEM] * len(aways),
            tile_scratch, flops=2 * len(aways) * GROUP * TILE**3, moved=4 << 20,
        )(ids, *lists, own, other, turned)

    (far,) = terms(2)
    far, turned = lax.optimization_barrier((far, turned))
    far = shift(far, "y", 2)
    up, down = terms(1, 3)
    below = shift(up, "y", 1)
    above = shift(down, "y", -1)
    (mine,) = terms(0)
    parted = (NM, 2, SLOT_CAP, TILE, TILE)
    quarter = SHAPE((NM // 2, SLOT_CAP, TILE, TILE), BF16)
    kept = SHAPE((NM, SLOT_CAP, TILE, TILE), BF16)
    keep, low, high = kernel_call(
        y_sum_kernel, "y_sum", [kept, quarter, quarter], [SMEM] + [VMEM] * 4, [VMEM] * 3
    )(ids, *(value.reshape(parted) for value in (mine, below, above, far)))

    low = shift(low, Z, 1)
    high = shift(high, Z, -1)
    pairs = kernel_call(pair_sum_kernel, "pair_sum", kept, [VMEM] * 3, VMEM)(keep, low, high)
    pairs, grads = lax.optimization_barrier((pairs, grads))
    arrived = exchange(pairs, "m")
    own_grad, squares = kernel_call(
        own_grad_kernel, "own_grad",
        [SHAPE((SLOT_CAP, TILE, TILE), F32), SHAPE((NY * NX * 2, 8, TILE), F32)],
        [SMEM, SMEM, VMEM], [VMEM] * 2,
    )(ids, owner_counts, arrived)

    stay, give = kernel_call(
        contrib_kernel, "contribs", [SHAPE((tokens // 2, width), BF16)] * 2,
        [SMEM] * 4 + [VMEM] * 2, [VMEM] * 2, [pltpu.SMEM((tile_total + 8,), jnp.int32)],
        moved=1 << 12,
    )(ids, *lists, grads, delta_all)

    rows = tokens // (2 * NX)
    taken = shift(give, "core", 1)
    share, *others = kernel_call(
        core_sum_kernel, "core_sum", [SHAPE((rows, width), BF16)] * NX,
        [SMEM] + [VMEM] * 2, [VMEM] * NX, moved=1 << 12,
    )(ids, stay.reshape(NX, rows, width), taken.reshape(NX, rows, width))
    share = share.astype(F32)
    for away, part in enumerate(others):
        share = share + shift(part, "x", away + 1).astype(F32)
    squares, share = lax.optimization_barrier((squares, share.astype(BF16)))
    gathered = lax.all_gather(share, ("x", "core"), axis=0, tiled=True)
    input_grad = kernel_call(
        copy_kernel, "result", SHAPE((tokens, width), BF16), [ANY], ANY,
        [pltpu.SemaphoreType.DMA], moved=4 << 20,
    )(gathered)

    squares = exchange(squares, ("y", "x", "core"))
    squares = kernel_call(relay_kernel, "relay", SHAPE((2 * NM, 8, TILE), F32), [VMEM], VMEM)(squares)
    squares = exchange(squares, Z)
    squares, input_grad = lax.optimization_barrier((squares, input_grad))
    count_all = float(NX * 2 * tile_total * TILE * TILE)

    def adam(*refs):
        adam_kernel(count_all, *refs)

    outs = kernel_call(
        adam, "adam", [SHAPE(delta_value.shape, F32)] * 3, [SMEM] * 2 + [VMEM] * 5, [VMEM] * 3
    )(ids, owner_counts, squares, own_grad, delta_value, moment_one, moment_two)
    return (input_grad, *outs)


def solution(mesh):
    grid = Mesh(mesh.devices.reshape(NY, NM, 2, NX, 2), ("y", "m", "p", "x", "core"))
    dp, tensor = ("y", "m", "p"), ("x", "core")
    tokens = P(dp, tensor)
    lists = P(tensor, None)
    slots = P(tensor, dp, None, None)
    return jax.shard_map(
        body,
        mesh=grid,
        in_specs=(tokens,) * 4 + (lists,) * 3 + (slots,) * 3,
        out_specs=(P(dp, None),) + (slots,) * 3,
        check_vma=False,
    )
```

```python
import functools

import jax
import jax.numpy as jnp
from jax import lax
from jax.experimental import pallas as pl
from jax.experimental.pallas import tpu as pltpu
from jax.sharding import Mesh, PartitionSpec as P

NY, NQ, NC, NX = 4, 4, 4, 4
NZ = NQ * NC
Z = ("q", "c")
TILE = 128
SLOT_CAP = 2
LOW, HIGH = (0, NZ // 2), (NZ // 2, NZ)
BF16, F32 = jnp.bfloat16, jnp.float32
SMEM = pl.BlockSpec(memory_space=pltpu.SMEM)
VMEM = pl.BlockSpec(memory_space=pltpu.VMEM)
ANY = pl.BlockSpec(memory_space=pl.ANY)
SHAPE = jax.ShapeDtypeStruct


def kernel_call(kernel, name, outs, ins, out_specs, scratch=(), flops=0, moved=1 << 20):
    return pl.pallas_call(
        kernel,
        out_shape=outs,
        in_specs=ins,
        out_specs=out_specs,
        scratch_shapes=scratch,
        compiler_params=pltpu.CompilerParams(vmem_limit_bytes=48 * 1024 * 1024),
        cost_estimate=pl.CostEstimate(flops=flops, bytes_accessed=moved, transcendentals=0),
        name=name,
    )


def shift(value, axis, step):
    size = lax.axis_size(axis)
    return lax.ppermute(value, axis, [(i, (i + step) % size) for i in range(size)])


def exchange(value, axis):
    return lax.all_to_all(value, axis, split_axis=0, concat_axis=0, tiled=True)


def spread(value, axis):
    copies = jnp.broadcast_to(value[None], (lax.axis_size(axis),) + value.shape)
    return exchange(copies, axis)


def gate_kernel(ids_ref, gate_ref, up_ref, hidden_ref, grad_ref, turned_ref):
    blocks = 2 * NX
    rows = grad_ref.shape[1] // blocks
    core = ids_ref[3]
    for col in range(grad_ref.shape[0]):
        cut = slice(col * TILE, (col + 1) * TILE)
        gate = gate_ref[:, cut].astype(F32)
        sig = 1.0 / (1.0 + jnp.exp(-gate))
        value = (
            hidden_ref[:, cut].astype(F32)
            * up_ref[:, cut].astype(F32)
            * sig
            * (1.0 + gate * (1.0 - sig))
        )
        for block in range(blocks):
            place = pl.multiple_of((((block & 1) ^ core) * NX + (block >> 1)) * rows, rows)
            part = value[block * rows : (block + 1) * rows]
            grad_ref[col, pl.ds(place, rows)] = part.astype(BF16)
        turned_ref[col] = value.T.astype(BF16)


def load_features(own_ref, other_ref, features, sems, starts_ref, counts_ref):
    first = pltpu.make_async_copy(own_ref, features.at[0], sems.at[0])
    second = pltpu.make_async_copy(other_ref, features.at[1], sems.at[1])
    first.start()
    second.start()

    def owner_step(owner, start):
        starts_ref[owner] = start
        return start + counts_ref[0, owner]

    lax.fori_loop(0, counts_ref.shape[1], owner_step, 0)
    first.wait()
    second.wait()


def slot_products(group, owners, put, ids_ref, rows_ref, cols_ref, starts_ref, features, turned_ref):
    core = ids_ref[3]
    last = rows_ref.shape[1] - 1
    per_step = 4

    def step(index, carry):
        for part in range(per_step):
            owner = owners[0] + index * per_step + part
            start = starts_ref[group * NZ + owner]
            for rank in range(SLOT_CAP):
                k = jnp.minimum(start + rank, last)
                row = rows_ref[0, k]
                lane = pl.multiple_of((row & 7) * TILE, TILE)
                x = features[((row >> 3) & 1) ^ core, row >> 4, :, pl.ds(lane, TILE)]
                term = jnp.dot(turned_ref[cols_ref[0, k]], x, preferred_element_type=F32)
                put((index * per_step + part) * SLOT_CAP + rank, term.astype(BF16))
        return carry

    lax.fori_loop(0, (owners[1] - owners[0]) // per_step, step, 0)


def tile_kernel(
    parts, ids_ref, rows_ref, cols_ref, counts_ref, own_ref, other_ref, turned_ref, *refs
):
    features, starts_ref, sems = refs[len(parts) :]
    load_features(own_ref, other_ref, features, sems, starts_ref, counts_ref)
    for ref, (away, owners) in zip(refs, parts):

        def put(slot, term, ref=ref):
            ref[slot] = term

        slot_products(
            (ids_ref[0] + away) & (NY - 1), owners, put,
            ids_ref, rows_ref, cols_ref, starts_ref, features, turned_ref,
        )


def passing_kernel(up_ref, far_low_ref, down_ref, far_high_ref, up_out, down_out):
    up_out[...] = (up_ref[...].astype(F32) + far_low_ref[...].astype(F32)).astype(BF16)
    down_out[...] = (down_ref[...].astype(F32) + far_high_ref[...].astype(F32)).astype(BF16)


def y_sum_kernel(
    ids_ref, mine_ref, below_low_ref, above_low_ref, below_high_ref, above_high_ref,
    keep_ref, up_ref, down_ref, up_two_ref, down_two_ref,
):
    mine_class = ids_ref[1] & (NC - 1)
    half = NQ // 2
    for q in range(NQ):
        below, above = (below_low_ref, above_low_ref) if q < half else (below_high_ref, above_high_ref)

        def total(step):
            side = (mine_class + step) & (NC - 1)
            return (
                mine_ref[q, side].astype(F32)
                + below[q % half, side].astype(F32)
                + above[q % half, side].astype(F32)
            ).astype(BF16)

        keep_ref[q] = total(0)
        up_ref[q] = total(1)
        down_ref[q] = total(3)
        (up_two_ref if q < half else down_two_ref)[q % half] = total(2)


def class_sum_kernel(keep_ref, one_ref, other_ref, low_ref, high_ref, out_ref):
    half = NQ // 2
    for q in range(NQ):
        two = low_ref[q] if q < half else high_ref[q - half]
        total = keep_ref[q].astype(F32) + one_ref[q].astype(F32)
        out_ref[q] = (total + other_ref[q].astype(F32) + two.astype(F32)).astype(BF16)


def own_grad_kernel(ids_ref, counts_ref, arrived_ref, grad_ref, squares_ref):
    count = counts_ref[0, ids_ref[0] * NZ + ids_ref[1]]
    squares = jnp.zeros((TILE, TILE), F32)
    for rank in range(SLOT_CAP):
        total = arrived_ref[0, rank].astype(F32)
        for q in range(1, NQ):
            total = total + arrived_ref[q, rank].astype(F32)
        total = jnp.where(rank < count, total, 0.0)
        grad_ref[rank] = total
        squares = squares + total * total
    squares_ref[...] = jnp.broadcast_to(jnp.sum(squares), squares_ref.shape)


def relay_kernel(arrived_ref, out_ref):
    total = jnp.sum(arrived_ref[...], axis=0, keepdims=True)
    out_ref[...] = jnp.broadcast_to(total, out_ref.shape)


def adam_kernel(
    count_all, ids_ref, counts_ref, arrived_ref, grad_ref, delta_ref, one_ref, two_ref,
    new_delta_ref, new_one_ref, new_two_ref,
):
    squares = jnp.sum(arrived_ref[...], axis=0)[0:1]
    factor = jnp.minimum(1.0, 1.0 / jnp.sqrt(squares / count_all + 1e-06))
    count = counts_ref[0, ids_ref[0] * NZ + ids_ref[1]]
    for rank in range(SLOT_CAP):
        live = rank < count
        clipped = factor * grad_ref[rank].T
        delta, one, two = delta_ref[0, rank], one_ref[0, rank], two_ref[0, rank]
        first = 0.9 * one + 0.1 * clipped
        second = 0.95 * two + 0.05 * clipped * clipped
        size = first / (1.0 - 0.9**10) / (jnp.sqrt(second / (1.0 - 0.95**10)) + 1e-08)
        updated = delta - 0.02 * (size + 0.1 * delta)
        new_delta_ref[0, rank] = jnp.where(live, updated, delta)
        new_one_ref[0, rank] = jnp.where(live, first, one)
        new_two_ref[0, rank] = jnp.where(live, second, two)


def turn_kernel(delta_ref, out_ref):
    for rank in range(SLOT_CAP):
        out_ref[rank] = delta_ref[0, rank].T.astype(BF16)


def contrib_kernel(
    rows_ref, cols_ref, counts_ref, grad_ref, delta_ref, stay_ref, give_ref, places_ref
):
    stay_ref[...] = jnp.zeros_like(stay_ref)
    give_ref[...] = jnp.zeros_like(give_ref)
    half = stay_ref.shape[0]

    def owner_step(owner, start):
        place = ((owner & (NZ - 1)) * NY + owner // NZ) * SLOT_CAP
        places_ref[start] = place
        places_ref[start + 1] = place + 1
        return start + counts_ref[0, owner]

    lax.fori_loop(0, counts_ref.shape[1], owner_step, 0)
    per_step = 28

    def step(index, carry):
        last, total = carry
        for part in range(per_step):
            k = index * per_step + part
            row = rows_ref[0, k]
            product = jnp.dot(
                grad_ref[cols_ref[0, k]], delta_ref[places_ref[k]], preferred_element_type=F32
            )
            total = jnp.where(row == last, total, 0.0) + product
            lane = pl.multiple_of(row * TILE, TILE)
            stay_ref[:, pl.ds(lane, TILE)] = total[:half].astype(BF16)
            give_ref[:, pl.ds(lane, TILE)] = total[half:].astype(BF16)
            last = row
        return last, total

    lax.fori_loop(
        0, rows_ref.shape[1] // per_step, step,
        (jnp.int32(-1), jnp.zeros((TILE, TILE), F32)),
    )


def core_sum_kernel(ids_ref, stay_ref, taken_ref, *out_refs):
    for away, ref in enumerate(out_refs):
        at = (ids_ref[2] + away) & (NX - 1)
        ref[...] = (stay_ref[at].astype(F32) + taken_ref[at].astype(F32)).astype(BF16)


def copy_kernel(in_ref, out_ref, sem):
    copy = pltpu.make_async_copy(in_ref, out_ref, sem)
    copy.start()
    copy.wait()


def body(
    features, gate_pre, up_pre, hidden_grad, tile_rows, tile_cols, owner_counts,
    delta_value, moment_one, moment_two,
):
    ids = jnp.stack([lax.axis_index(name) for name in ("y", Z, "x", "core")]).astype(jnp.int32)
    tokens, hidden = gate_pre.shape
    shard_width = features.shape[1]
    width = shard_width * NX * 2
    tile_total = tile_rows.shape[1]
    lists = (tile_rows, tile_cols, owner_counts)

    own = spread(features, "x")
    other = shift(own, "core", 1)

    delta_half = kernel_call(
        turn_kernel, "turn", SHAPE(delta_value.shape[1:], BF16), [VMEM], VMEM
    )(delta_value)
    delta_y = spread(delta_half, "y").reshape(NY * SLOT_CAP, TILE, TILE)
    delta_all = lax.all_gather(delta_y, Z, axis=0, tiled=True)

    grads, turned = kernel_call(
        gate_kernel, "gate", [SHAPE((hidden // TILE, tokens, TILE), BF16)] * 2,
        [SMEM] + [VMEM] * 3, [VMEM] * 2, flops=tokens * hidden * 12, moved=tokens * hidden * 10,
    )(ids, gate_pre, up_pre, hidden_grad)

    tile_ins = [SMEM] * 4 + [ANY, ANY, VMEM]
    tile_scratch = [
        pltpu.VMEM((2, NX, tokens, shard_width), BF16),
        pltpu.SMEM((owner_counts.shape[1],), jnp.int32),
        pltpu.SemaphoreType.DMA((2,)),
    ]

    def terms(turned, *parts):
        *values, turned = lax.optimization_barrier((*kernel_call(
            functools.partial(tile_kernel, parts), "tiles",
            [SHAPE(((last - first) * SLOT_CAP, TILE, TILE), BF16) for _, (first, last) in parts],
            tile_ins, [VMEM] * len(parts), tile_scratch,
            flops=2 * tile_total * TILE**3 // 4, moved=2 << 20,
        )(ids, *lists, own, other, turned), turned))
        return values, turned

    (far_low, far_high), turned = terms(turned, (2, LOW), (2, HIGH))
    far_low, far_high = shift(far_low, "y", 1), shift(far_high, "y", -1)
    (up_high, down_low), turned = terms(turned, (1, HIGH), (3, LOW))
    below_high, above_low = shift(up_high, "y", 1), shift(down_low, "y", -1)
    (up_low, down_high, mine), turned = terms(turned, (1, LOW), (3, HIGH), (0, (0, NZ)))
    half = SHAPE(up_low.shape, BF16)
    up_low, down_high = kernel_call(
        passing_kernel, "passing", [half] * 2, [VMEM] * 4, [VMEM] * 2
    )(up_low, far_low, down_high, far_high)
    below_low, above_high = shift(up_low, "y", 1), shift(down_high, "y", -1)

    def parted(value):
        return value.reshape(-1, NC, SLOT_CAP, TILE, TILE)

    four = SHAPE((NQ, SLOT_CAP, TILE, TILE), BF16)
    two = SHAPE((NQ // 2, SLOT_CAP, TILE, TILE), BF16)
    keep, up, down, up_two, down_two = kernel_call(
        y_sum_kernel, "y_sum", [four, four, four, two, two], [SMEM] + [VMEM] * 5, [VMEM] * 5
    )(ids, *map(parted, (mine, below_low, above_low, below_high, above_high)))

    moved = [shift(up, Z, 1), shift(down, Z, -1), shift(up_two, Z, 2), shift(down_two, Z, -2)]
    *moved, grads = lax.optimization_barrier((*moved, grads))
    pairs = kernel_call(class_sum_kernel, "class_sum", four, [VMEM] * 5, VMEM)(keep, *moved)
    arrived = exchange(pairs, "q")
    own_grad, squares = kernel_call(
        own_grad_kernel, "own_grad",
        [SHAPE((SLOT_CAP, TILE, TILE), F32), SHAPE((NY * NX * 2, 8, TILE), F32)],
        [SMEM, SMEM, VMEM], [VMEM] * 2,
    )(ids, owner_counts, arrived)

    stay, give = kernel_call(
        contrib_kernel, "contribs", [SHAPE((tokens // 2, width), BF16)] * 2,
        [SMEM] * 3 + [VMEM] * 2, [VMEM] * 2, [pltpu.SMEM((tile_total + 8,), jnp.int32)],
        moved=1 << 12,
    )(*lists, grads, delta_all)

    rows = tokens // (2 * NX)
    taken = shift(give, "core", 1)
    share, *others = kernel_call(
        core_sum_kernel, "core_sum", [SHAPE((rows, width), BF16)] * NX,
        [SMEM] + [VMEM] * 2, [VMEM] * NX, moved=1 << 12,
    )(ids, stay.reshape(NX, rows, width), taken.reshape(NX, rows, width))
    share = share.astype(F32)
    for away, part in enumerate(others):
        share = share + shift(part, "x", away + 1).astype(F32)
    squares, share = lax.optimization_barrier((squares, share.astype(BF16)))
    gathered = lax.all_gather(share, ("x", "core"), axis=0, tiled=True)
    input_grad = kernel_call(
        copy_kernel, "result", SHAPE((tokens, width), BF16), [ANY], ANY,
        [pltpu.SemaphoreType.DMA], moved=4 << 20,
    )(gathered)

    squares = exchange(squares, ("y", "x", "core"))
    squares = kernel_call(relay_kernel, "relay", SHAPE((NZ, 8, TILE), F32), [VMEM], VMEM)(squares)
    squares = exchange(squares, Z)
    squares, input_grad = lax.optimization_barrier((squares, input_grad))
    count_all = float(NX * 2 * tile_total * TILE * TILE)

    def adam(*refs):
        adam_kernel(count_all, *refs)

    outs = kernel_call(
        adam, "adam", [SHAPE(delta_value.shape, F32)] * 3, [SMEM] * 2 + [VMEM] * 5, [VMEM] * 3
    )(ids, owner_counts, squares, own_grad, delta_value, moment_one, moment_two)
    return (input_grad, *outs)


def solution(mesh):
    grid = Mesh(mesh.devices.reshape(NY, NQ, NC, NX, 2), ("y", "q", "c", "x", "core"))
    dp, tensor = ("y", "q", "c"), ("x", "core")
    tokens = P(dp, tensor)
    lists = P(tensor, None)
    slots = P(tensor, dp, None, None)
    return jax.shard_map(
        body,
        mesh=grid,
        in_specs=(tokens,) * 4 + (lists,) * 3 + (slots,) * 3,
        out_specs=(P(dp, None),) + (slots,) * 3,
        check_vma=False,
    )
```

```python
import functools

import jax
import jax.numpy as jnp
from jax import lax
from jax.experimental import pallas as pl
from jax.experimental.pallas import tpu as pltpu
from jax.sharding import Mesh, PartitionSpec as P

NY, NZ, NX = 4, 16, 4
NM = NZ // 2
Z = ("q", "d", "p")
TILE = 128
SLOT_CAP = 2
LOW, HIGH = (0, NZ // 2), (NZ // 2, NZ)
BF16, F32 = jnp.bfloat16, jnp.float32
SMEM = pl.BlockSpec(memory_space=pltpu.SMEM)
VMEM = pl.BlockSpec(memory_space=pltpu.VMEM)
ANY = pl.BlockSpec(memory_space=pl.ANY)
SHAPE = jax.ShapeDtypeStruct


def kernel_call(kernel, name, outs, ins, out_specs, scratch=(), flops=0, moved=1 << 20):
    return pl.pallas_call(
        kernel,
        out_shape=outs,
        in_specs=ins,
        out_specs=out_specs,
        scratch_shapes=scratch,
        compiler_params=pltpu.CompilerParams(vmem_limit_bytes=48 * 1024 * 1024),
        cost_estimate=pl.CostEstimate(flops=flops, bytes_accessed=moved, transcendentals=0),
        name=name,
    )


def shift(value, axis, step):
    size = lax.axis_size(axis)
    return lax.ppermute(value, axis, [(i, (i + step) % size) for i in range(size)])


def exchange(value, axis):
    return lax.all_to_all(value, axis, split_axis=0, concat_axis=0, tiled=True)


def spread(value, axis):
    copies = jnp.broadcast_to(value[None], (lax.axis_size(axis),) + value.shape)
    return exchange(copies, axis)


def gate_kernel(ids_ref, gate_ref, up_ref, hidden_ref, grad_ref, turned_ref):
    blocks = 2 * NX
    rows = grad_ref.shape[1] // blocks
    core = ids_ref[3]
    for col in range(grad_ref.shape[0]):
        cut = slice(col * TILE, (col + 1) * TILE)
        gate = gate_ref[:, cut].astype(F32)
        sig = 1.0 / (1.0 + jnp.exp(-gate))
        value = (
            hidden_ref[:, cut].astype(F32)
            * up_ref[:, cut].astype(F32)
            * sig
            * (1.0 + gate * (1.0 - sig))
        )
        for block in range(blocks):
            place = pl.multiple_of((((block & 1) ^ core) * NX + (block >> 1)) * rows, rows)
            part = value[block * rows : (block + 1) * rows]
            grad_ref[col, pl.ds(place, rows)] = part.astype(BF16)
        turned_ref[col] = value.T.astype(BF16)


def load_features(own_ref, other_ref, features, sems, starts_ref, counts_ref):
    first = pltpu.make_async_copy(own_ref, features.at[0], sems.at[0])
    second = pltpu.make_async_copy(other_ref, features.at[1], sems.at[1])
    first.start()
    second.start()

    def owner_step(owner, start):
        starts_ref[owner] = start
        return start + counts_ref[0, owner]

    lax.fori_loop(0, counts_ref.shape[1], owner_step, 0)
    first.wait()
    second.wait()


def slot_products(group, owners, put, ids_ref, rows_ref, cols_ref, starts_ref, features, turned_ref):
    core = ids_ref[3]
    last = rows_ref.shape[1] - 1
    per_step = 4

    def step(index, carry):
        for part in range(per_step):
            owner = owners[0] + index * per_step + part
            start = starts_ref[group * NZ + owner]
            for rank in range(SLOT_CAP):
                k = jnp.minimum(start + rank, last)
                row = rows_ref[0, k]
                lane = pl.multiple_of((row & 7) * TILE, TILE)
                x = features[((row >> 3) & 1) ^ core, row >> 4, :, pl.ds(lane, TILE)]
                term = jnp.dot(turned_ref[cols_ref[0, k]], x, preferred_element_type=F32)
                put((index * per_step + part) * SLOT_CAP + rank, term.astype(BF16))
        return carry

    lax.fori_loop(0, (owners[1] - owners[0]) // per_step, step, 0)


def tile_kernel(
    parts, ids_ref, rows_ref, cols_ref, counts_ref, own_ref, other_ref, turned_ref, *refs
):
    features, starts_ref, sems = refs[len(parts) :]
    load_features(own_ref, other_ref, features, sems, starts_ref, counts_ref)
    for ref, (away, owners) in zip(refs, parts):

        def put(slot, term, ref=ref):
            ref[slot] = term

        slot_products(
            (ids_ref[0] + away) & (NY - 1), owners, put,
            ids_ref, rows_ref, cols_ref, starts_ref, features, turned_ref,
        )


def passing_kernel(up_ref, far_low_ref, down_ref, far_high_ref, up_out, down_out):
    up_out[...] = (up_ref[...].astype(F32) + far_low_ref[...].astype(F32)).astype(BF16)
    down_out[...] = (down_ref[...].astype(F32) + far_high_ref[...].astype(F32)).astype(BF16)


def y_sum_kernel(
    ids_ref, mine_ref, below_low_ref, above_low_ref, below_high_ref, above_high_ref,
    keep_ref, low_ref, high_ref,
):
    parity = ids_ref[1] & 1
    half = NM // 2
    for m in range(NM):
        below, above = (below_low_ref, above_low_ref) if m < half else (below_high_ref, above_high_ref)

        def total(side):
            return (
                mine_ref[m, side].astype(F32)
                + below[m % half, side].astype(F32)
                + above[m % half, side].astype(F32)
            ).astype(BF16)

        keep_ref[m] = total(parity)
        (low_ref if m < half else high_ref)[m % half] = total(1 - parity)


def pair_sum_kernel(keep_ref, low_ref, high_ref, out_ref):
    half = NM // 2
    out_ref[:half] = (keep_ref[:half].astype(F32) + low_ref[...].astype(F32)).astype(BF16)
    out_ref[half:] = (keep_ref[half:].astype(F32) + high_ref[...].astype(F32)).astype(BF16)


def own_grad_kernel(ids_ref, counts_ref, arrived_ref, grad_ref, squares_ref):
    count = counts_ref[0, ids_ref[0] * NZ + ids_ref[1]]
    squares = jnp.zeros((TILE, TILE), F32)
    for rank in range(SLOT_CAP):
        total = arrived_ref[0, rank].astype(F32)
        for m in range(1, NM):
            total = total + arrived_ref[m, rank].astype(F32)
        total = jnp.where(rank < count, total, 0.0)
        grad_ref[rank] = total
        squares = squares + total * total
    squares_ref[...] = jnp.broadcast_to(jnp.sum(squares), squares_ref.shape)


def relay_kernel(arrived_ref, out_ref):
    total = jnp.sum(arrived_ref[...], axis=0, keepdims=True)
    out_ref[...] = jnp.broadcast_to(total, out_ref.shape)


def adam_kernel(
    count_all, ids_ref, counts_ref, arrived_ref, grad_ref, delta_ref, one_ref, two_ref,
    new_delta_ref, new_one_ref, new_two_ref,
):
    squares = jnp.sum(arrived_ref[...], axis=0)[0:1]
    factor = jnp.minimum(1.0, 1.0 / jnp.sqrt(squares / count_all + 1e-06))
    count = counts_ref[0, ids_ref[0] * NZ + ids_ref[1]]
    for rank in range(SLOT_CAP):
        live = rank < count
        clipped = factor * grad_ref[rank].T
        delta, one, two = delta_ref[0, rank], one_ref[0, rank], two_ref[0, rank]
        first = 0.9 * one + 0.1 * clipped
        second = 0.95 * two + 0.05 * clipped * clipped
        size = first / (1.0 - 0.9**10) / (jnp.sqrt(second / (1.0 - 0.95**10)) + 1e-08)
        updated = delta - 0.02 * (size + 0.1 * delta)
        new_delta_ref[0, rank] = jnp.where(live, updated, delta)
        new_one_ref[0, rank] = jnp.where(live, first, one)
        new_two_ref[0, rank] = jnp.where(live, second, two)


def turn_kernel(delta_ref, out_ref):
    for rank in range(SLOT_CAP):
        out_ref[rank] = delta_ref[0, rank].T.astype(BF16)


def contrib_kernel(
    rows_ref, cols_ref, counts_ref, grad_ref, delta_ref, stay_ref, give_ref, places_ref
):
    stay_ref[...] = jnp.zeros_like(stay_ref)
    give_ref[...] = jnp.zeros_like(give_ref)
    half = stay_ref.shape[0]

    def owner_step(owner, start):
        place = ((owner & (NZ - 1)) * NY + owner // NZ) * SLOT_CAP
        places_ref[start] = place
        places_ref[start + 1] = place + 1
        return start + counts_ref[0, owner]

    lax.fori_loop(0, counts_ref.shape[1], owner_step, 0)
    per_step = 28

    def step(index, carry):
        last, total = carry
        for part in range(per_step):
            k = index * per_step + part
            row = rows_ref[0, k]
            product = jnp.dot(
                grad_ref[cols_ref[0, k]], delta_ref[places_ref[k]], preferred_element_type=F32
            )
            total = jnp.where(row == last, total, 0.0) + product
            lane = pl.multiple_of(row * TILE, TILE)
            stay_ref[:, pl.ds(lane, TILE)] = total[:half].astype(BF16)
            give_ref[:, pl.ds(lane, TILE)] = total[half:].astype(BF16)
            last = row
        return last, total

    lax.fori_loop(
        0, rows_ref.shape[1] // per_step, step,
        (jnp.int32(-1), jnp.zeros((TILE, TILE), F32)),
    )


def core_sum_kernel(ids_ref, stay_ref, taken_ref, *out_refs):
    for away, ref in enumerate(out_refs):
        at = (ids_ref[2] + away) & (NX - 1)
        ref[...] = (stay_ref[at].astype(F32) + taken_ref[at].astype(F32)).astype(BF16)


def copy_kernel(in_ref, out_ref, sem):
    copy = pltpu.make_async_copy(in_ref, out_ref, sem)
    copy.start()
    copy.wait()


def body(
    features, gate_pre, up_pre, hidden_grad, tile_rows, tile_cols, owner_counts,
    delta_value, moment_one, moment_two,
):
    ids = jnp.stack([lax.axis_index(name) for name in ("y", Z, "x", "core")]).astype(jnp.int32)
    tokens, hidden = gate_pre.shape
    shard_width = features.shape[1]
    width = shard_width * NX * 2
    tile_total = tile_rows.shape[1]
    lists = (tile_rows, tile_cols, owner_counts)

    own = spread(features, "x")
    other = shift(own, "core", 1)

    delta_half = kernel_call(
        turn_kernel, "turn", SHAPE(delta_value.shape[1:], BF16), [VMEM], VMEM
    )(delta_value)
    delta_y = spread(delta_half, "y").reshape(NY * SLOT_CAP, TILE, TILE)
    delta_all = lax.all_gather(delta_y, Z, axis=0, tiled=True)

    grads, turned = kernel_call(
        gate_kernel, "gate", [SHAPE((hidden // TILE, tokens, TILE), BF16)] * 2,
        [SMEM] + [VMEM] * 3, [VMEM] * 2, flops=tokens * hidden * 12, moved=tokens * hidden * 10,
    )(ids, gate_pre, up_pre, hidden_grad)

    tile_ins = [SMEM] * 4 + [ANY, ANY, VMEM]
    tile_scratch = [
        pltpu.VMEM((2, NX, tokens, shard_width), BF16),
        pltpu.SMEM((owner_counts.shape[1],), jnp.int32),
        pltpu.SemaphoreType.DMA((2,)),
    ]

    def terms(turned, *parts):
        *values, turned = lax.optimization_barrier((*kernel_call(
            functools.partial(tile_kernel, parts), "tiles",
            [SHAPE(((last - first) * SLOT_CAP, TILE, TILE), BF16) for _, (first, last) in parts],
            tile_ins, [VMEM] * len(parts), tile_scratch,
            flops=2 * tile_total * TILE**3 // 4, moved=2 << 20,
        )(ids, *lists, own, other, turned), turned))
        return values, turned

    (far_low, far_high), turned = terms(turned, (2, LOW), (2, HIGH))
    far_low, far_high = shift(far_low, "y", 1), shift(far_high, "y", -1)
    (up_high, down_low), turned = terms(turned, (1, HIGH), (3, LOW))
    below_high, above_low = shift(up_high, "y", 1), shift(down_low, "y", -1)
    (up_low, down_high, mine), turned = terms(turned, (1, LOW), (3, HIGH), (0, (0, NZ)))
    half = SHAPE(up_low.shape, BF16)
    up_low, down_high = kernel_call(
        passing_kernel, "passing", [half] * 2, [VMEM] * 4, [VMEM] * 2
    )(up_low, far_low, down_high, far_high)
    below_low, above_high = shift(up_low, "y", 1), shift(down_high, "y", -1)

    def parted(value):
        return value.reshape(-1, 2, SLOT_CAP, TILE, TILE)

    eight = SHAPE((NM, SLOT_CAP, TILE, TILE), BF16)
    four = SHAPE((NM // 2, SLOT_CAP, TILE, TILE), BF16)
    keep, low, high = kernel_call(
        y_sum_kernel, "y_sum", [eight, four, four], [SMEM] + [VMEM] * 5, [VMEM] * 3
    )(ids, *map(parted, (mine, below_low, above_low, below_high, above_high)))

    pairs = kernel_call(pair_sum_kernel, "pair_sum", eight, [VMEM] * 3, VMEM)(
        keep, shift(low, Z, 1), shift(high, Z, -1)
    )
    pairs, grads = lax.optimization_barrier((pairs, grads))
    arrived = exchange(pairs, ("q", "d"))
    own_grad, squares = kernel_call(
        own_grad_kernel, "own_grad",
        [SHAPE((SLOT_CAP, TILE, TILE), F32), SHAPE((NY * NZ // 4, 8, TILE), F32)],
        [SMEM, SMEM, VMEM], [VMEM] * 2,
    )(ids, owner_counts, arrived)

    stay, give = kernel_call(
        contrib_kernel, "contribs", [SHAPE((tokens // 2, width), BF16)] * 2,
        [SMEM] * 3 + [VMEM] * 2, [VMEM] * 2, [pltpu.SMEM((tile_total + 8,), jnp.int32)],
        moved=1 << 12,
    )(*lists, grads, delta_all)

    rows = tokens // (2 * NX)
    taken = shift(give, "core", 1)
    share, *others = kernel_call(
        core_sum_kernel, "core_sum", [SHAPE((rows, width), BF16)] * NX,
        [SMEM] + [VMEM] * 2, [VMEM] * NX, moved=1 << 12,
    )(ids, stay.reshape(NX, rows, width), taken.reshape(NX, rows, width))
    share = share.astype(F32)
    for away, part in enumerate(others):
        share = share + shift(part, "x", away + 1).astype(F32)
    squares, share = lax.optimization_barrier((squares, share.astype(BF16)))
    gathered = lax.all_gather(share, ("x", "core"), axis=0, tiled=True)
    input_grad = kernel_call(
        copy_kernel, "result", SHAPE((tokens, width), BF16), [ANY], ANY,
        [pltpu.SemaphoreType.DMA], moved=4 << 20,
    )(gathered)

    squares = exchange(squares, ("y", "d", "p"))
    squares = kernel_call(relay_kernel, "relay", SHAPE((NZ // 4 * NX * 2, 8, TILE), F32), [VMEM], VMEM)(squares)
    squares = exchange(squares, ("q", "x", "core"))
    squares, input_grad = lax.optimization_barrier((squares, input_grad))
    count_all = float(NX * 2 * tile_total * TILE * TILE)

    def adam(*refs):
        adam_kernel(count_all, *refs)

    outs = kernel_call(
        adam, "adam", [SHAPE(delta_value.shape, F32)] * 3, [SMEM] * 2 + [VMEM] * 5, [VMEM] * 3
    )(ids, owner_counts, squares, own_grad, delta_value, moment_one, moment_two)
    return (input_grad, *outs)


def solution(mesh):
    grid = Mesh(mesh.devices.reshape(NY, 4, 2, 2, NX, 2), ("y", "q", "d", "p", "x", "core"))
    dp, tensor = ("y", "q", "d", "p"), ("x", "core")
    tokens = P(dp, tensor)
    lists = P(tensor, None)
    slots = P(tensor, dp, None, None)
    return jax.shard_map(
        body,
        mesh=grid,
        in_specs=(tokens,) * 4 + (lists,) * 3 + (slots,) * 3,
        out_specs=(P(dp, None),) + (slots,) * 3,
        check_vma=False,
    )
```

```python
import functools

import jax
import jax.numpy as jnp
from jax import lax
from jax.experimental import pallas as pl
from jax.experimental.pallas import tpu as pltpu
from jax.sharding import Mesh, PartitionSpec as P

NY, NM, NX = 4, 8, 4
NZ = 2 * NM
Z = ("m", "p")
TILE = 128
SLOT_CAP = 2
LOW, HIGH = (0, NZ // 2), (NZ // 2, NZ)
BF16, F32 = jnp.bfloat16, jnp.float32
SMEM = pl.BlockSpec(memory_space=pltpu.SMEM)
VMEM = pl.BlockSpec(memory_space=pltpu.VMEM)
ANY = pl.BlockSpec(memory_space=pl.ANY)
SHAPE = jax.ShapeDtypeStruct


def kernel_call(
    kernel, name, outs, ins, out_specs, scratch=(), flops=0, moved=1 << 20, vmem=48
):
    return pl.pallas_call(
        kernel,
        out_shape=outs,
        in_specs=ins,
        out_specs=out_specs,
        scratch_shapes=scratch,
        compiler_params=pltpu.CompilerParams(vmem_limit_bytes=vmem * 1024 * 1024),
        cost_estimate=pl.CostEstimate(flops=flops, bytes_accessed=moved, transcendentals=0),
        name=name,
    )


def shift(value, axis, step):
    size = lax.axis_size(axis)
    return lax.ppermute(value, axis, [(i, (i + step) % size) for i in range(size)])


def exchange(value, axis):
    return lax.all_to_all(value, axis, split_axis=0, concat_axis=0, tiled=True)


def spread(value, axis):
    copies = jnp.broadcast_to(value[None], (lax.axis_size(axis),) + value.shape)
    return exchange(copies, axis)


def gate_kernel(ids_ref, gate_ref, up_ref, hidden_ref, grad_ref, turned_ref):
    blocks = 2 * NX
    rows = grad_ref.shape[1] // blocks
    core = ids_ref[3]
    for col in range(grad_ref.shape[0]):
        cut = slice(col * TILE, (col + 1) * TILE)
        gate = gate_ref[:, cut].astype(F32)
        sig = 1.0 / (1.0 + jnp.exp(-gate))
        value = (
            hidden_ref[:, cut].astype(F32)
            * up_ref[:, cut].astype(F32)
            * sig
            * (1.0 + gate * (1.0 - sig))
        )
        for block in range(blocks):
            place = pl.multiple_of((((block & 1) ^ core) * NX + (block >> 1)) * rows, rows)
            part = value[block * rows : (block + 1) * rows]
            grad_ref[col, pl.ds(place, rows)] = part.astype(BF16)
        turned_ref[col] = value.T.astype(BF16)


def load_features(own_ref, other_ref, features, sems, starts_ref, counts_ref):
    first = pltpu.make_async_copy(own_ref, features.at[0], sems.at[0])
    second = pltpu.make_async_copy(other_ref, features.at[1], sems.at[1])
    first.start()
    second.start()

    def owner_step(owner, start):
        starts_ref[owner] = start
        return start + counts_ref[0, owner]

    lax.fori_loop(0, counts_ref.shape[1], owner_step, 0)
    first.wait()
    second.wait()


def slot_products(group, owners, put, ids_ref, rows_ref, cols_ref, starts_ref, features, turned_ref):
    core = ids_ref[3]
    last = rows_ref.shape[1] - 1
    per_step = 4

    def step(index, carry):
        for part in range(per_step):
            owner = owners[0] + index * per_step + part
            start = starts_ref[group * NZ + owner]
            for rank in range(SLOT_CAP):
                k = jnp.minimum(start + rank, last)
                row = rows_ref[0, k]
                lane = pl.multiple_of((row & 7) * TILE, TILE)
                x = features[((row >> 3) & 1) ^ core, row >> 4, :, pl.ds(lane, TILE)]
                term = jnp.dot(turned_ref[cols_ref[0, k]], x, preferred_element_type=F32)
                put((index * per_step + part) * SLOT_CAP + rank, term.astype(BF16))
        return carry

    lax.fori_loop(0, (owners[1] - owners[0]) // per_step, step, 0)


def tile_kernel(
    parts, ids_ref, rows_ref, cols_ref, counts_ref, own_ref, other_ref, turned_ref, *refs
):
    features, starts_ref, sems = refs[len(parts) :]
    load_features(own_ref, other_ref, features, sems, starts_ref, counts_ref)
    for ref, (away, owners) in zip(refs, parts):

        def put(slot, term, ref=ref):
            ref[slot] = term

        slot_products(
            (ids_ref[0] + away) & (NY - 1), owners, put,
            ids_ref, rows_ref, cols_ref, starts_ref, features, turned_ref,
        )


def passing_kernel(up_ref, far_low_ref, down_ref, far_high_ref, up_out, down_out):
    up_out[...] = (up_ref[...].astype(F32) + far_low_ref[...].astype(F32)).astype(BF16)
    down_out[...] = (down_ref[...].astype(F32) + far_high_ref[...].astype(F32)).astype(BF16)


def y_sum_kernel(
    ids_ref, mine_ref, below_low_ref, above_low_ref, below_high_ref, above_high_ref,
    keep_ref, give_ref,
):
    parity = ids_ref[1] & 1
    half = NM // 2
    for m in range(NM):
        below, above = (below_low_ref, above_low_ref) if m < half else (below_high_ref, above_high_ref)

        def total(side):
            return (
                mine_ref[m, side].astype(F32)
                + below[m % half, side].astype(F32)
                + above[m % half, side].astype(F32)
            ).astype(BF16)

        keep_ref[m] = total(parity)
        give_ref[m] = total(1 - parity)


def pair_sum_kernel(keep_ref, taken_ref, out_ref):
    out_ref[...] = (keep_ref[...].astype(F32) + taken_ref[...].astype(F32)).astype(BF16)


def own_grad_kernel(ids_ref, counts_ref, arrived_ref, grad_ref, squares_ref):
    count = counts_ref[0, ids_ref[0] * NZ + ids_ref[1]]
    squares = jnp.zeros((TILE, TILE), F32)
    for rank in range(SLOT_CAP):
        total = arrived_ref[0, rank].astype(F32)
        for m in range(1, NM):
            total = total + arrived_ref[m, rank].astype(F32)
        total = jnp.where(rank < count, total, 0.0)
        grad_ref[rank] = total
        squares = squares + total * total
    squares_ref[...] = jnp.broadcast_to(jnp.sum(squares), squares_ref.shape)


def relay_kernel(arrived_ref, out_ref):
    total = jnp.sum(arrived_ref[...], axis=0, keepdims=True)
    out_ref[...] = jnp.broadcast_to(total, out_ref.shape)


def adam_kernel(
    count_all, ids_ref, counts_ref, arrived_ref, grad_ref, delta_ref, one_ref, two_ref,
    new_delta_ref, new_one_ref, new_two_ref,
):
    squares = jnp.sum(arrived_ref[...], axis=0)[0:1]
    factor = jnp.minimum(1.0, 1.0 / jnp.sqrt(squares / count_all + 1e-06))
    count = counts_ref[0, ids_ref[0] * NZ + ids_ref[1]]
    for rank in range(SLOT_CAP):
        live = rank < count
        clipped = factor * grad_ref[rank].T
        delta, one, two = delta_ref[0, rank], one_ref[0, rank], two_ref[0, rank]
        first = 0.9 * one + 0.1 * clipped
        second = 0.95 * two + 0.05 * clipped * clipped
        size = first / (1.0 - 0.9**10) / (jnp.sqrt(second / (1.0 - 0.95**10)) + 1e-08)
        updated = delta - 0.02 * (size + 0.1 * delta)
        new_delta_ref[0, rank] = jnp.where(live, updated, delta)
        new_one_ref[0, rank] = jnp.where(live, first, one)
        new_two_ref[0, rank] = jnp.where(live, second, two)


def turn_kernel(delta_ref, out_ref):
    for rank in range(SLOT_CAP):
        out_ref[rank] = delta_ref[0, rank].T.astype(BF16)


def contrib_kernel(
    rows_ref, cols_ref, counts_ref, grad_ref, delta_ref, stay_ref, give_ref, places_ref
):
    stay_ref[...] = jnp.zeros_like(stay_ref)
    give_ref[...] = jnp.zeros_like(give_ref)
    half = stay_ref.shape[0]

    def owner_step(owner, start):
        place = ((owner & (NZ - 1)) * NY + owner // NZ) * SLOT_CAP
        places_ref[start] = place
        places_ref[start + 1] = place + 1
        return start + counts_ref[0, owner]

    lax.fori_loop(0, counts_ref.shape[1], owner_step, 0)
    per_step = 28

    def step(index, carry):
        last, total = carry
        for part in range(per_step):
            k = index * per_step + part
            row = rows_ref[0, k]
            product = jnp.dot(
                grad_ref[cols_ref[0, k]], delta_ref[places_ref[k]], preferred_element_type=F32
            )
            total = jnp.where(row == last, total, 0.0) + product
            lane = pl.multiple_of(row * TILE, TILE)
            stay_ref[:, pl.ds(lane, TILE)] = total[:half].astype(BF16)
            give_ref[:, pl.ds(lane, TILE)] = total[half:].astype(BF16)
            last = row
        return last, total

    lax.fori_loop(
        0, rows_ref.shape[1] // per_step, step,
        (jnp.int32(-1), jnp.zeros((TILE, TILE), F32)),
    )


def core_sum_kernel(ids_ref, stay_ref, taken_ref, *out_refs):
    for away, ref in enumerate(out_refs):
        at = (ids_ref[2] + away) & (NX - 1)
        ref[...] = (stay_ref[at].astype(F32) + taken_ref[at].astype(F32)).astype(BF16)


def copy_kernel(in_ref, out_ref, held, sems):
    chunks = held.shape[0]
    rows = in_ref.shape[0] // chunks

    def part(ref, chunk):
        return ref.at[pl.ds(chunk * rows, rows)]

    loads = [
        pltpu.make_async_copy(part(in_ref, i), held.at[i], sems.at[0, i]) for i in range(chunks)
    ]
    stores = [
        pltpu.make_async_copy(held.at[i], part(out_ref, i), sems.at[1, i]) for i in range(chunks)
    ]
    for load in loads:
        load.start()
    for load, store in zip(loads, stores):
        load.wait()
        store.start()
    for store in stores:
        store.wait()


def body(
    features, gate_pre, up_pre, hidden_grad, tile_rows, tile_cols, owner_counts,
    delta_value, moment_one, moment_two,
):
    ids = jnp.stack([lax.axis_index(name) for name in ("y", Z, "x", "core")]).astype(jnp.int32)
    tokens, hidden = gate_pre.shape
    shard_width = features.shape[1]
    width = shard_width * NX * 2
    tile_total = tile_rows.shape[1]
    lists = (tile_rows, tile_cols, owner_counts)

    own = spread(features, "x")
    other = shift(own, "core", 1)

    delta_half = kernel_call(
        turn_kernel, "turn", SHAPE(delta_value.shape[1:], BF16), [VMEM], VMEM
    )(delta_value)
    delta_y = spread(delta_half, "y").reshape(NY * SLOT_CAP, TILE, TILE)
    delta_all = lax.all_gather(delta_y, Z, axis=0, tiled=True)

    grads, turned = kernel_call(
        gate_kernel, "gate", [SHAPE((hidden // TILE, tokens, TILE), BF16)] * 2,
        [SMEM] + [VMEM] * 3, [VMEM] * 2, flops=tokens * hidden * 12, moved=tokens * hidden * 10,
    )(ids, gate_pre, up_pre, hidden_grad)

    tile_ins = [SMEM] * 4 + [ANY, ANY, VMEM]
    tile_scratch = [
        pltpu.VMEM((2, NX, tokens, shard_width), BF16),
        pltpu.SMEM((owner_counts.shape[1],), jnp.int32),
        pltpu.SemaphoreType.DMA((2,)),
    ]

    def terms(turned, *parts):
        *values, turned = lax.optimization_barrier((*kernel_call(
            functools.partial(tile_kernel, parts), "tiles",
            [SHAPE(((last - first) * SLOT_CAP, TILE, TILE), BF16) for _, (first, last) in parts],
            tile_ins, [VMEM] * len(parts), tile_scratch,
            flops=2 * tile_total * TILE**3 // 4, moved=2 << 20,
        )(ids, *lists, own, other, turned), turned))
        return values, turned

    (far_low, far_high), turned = terms(turned, (2, LOW), (2, HIGH))
    far_low, far_high = shift(far_low, "y", 1), shift(far_high, "y", -1)
    (up_high, down_low), turned = terms(turned, (1, HIGH), (3, LOW))
    below_high, above_low = shift(up_high, "y", 1), shift(down_low, "y", -1)
    (up_low, down_high, mine), turned = terms(turned, (1, LOW), (3, HIGH), (0, (0, NZ)))
    half = SHAPE(up_low.shape, BF16)
    up_low, down_high = kernel_call(
        passing_kernel, "passing", [half] * 2, [VMEM] * 4, [VMEM] * 2
    )(up_low, far_low, down_high, far_high)
    below_low, above_high = shift(up_low, "y", 1), shift(down_high, "y", -1)

    def parted(value):
        return value.reshape(-1, 2, SLOT_CAP, TILE, TILE)

    eight = SHAPE((NM, SLOT_CAP, TILE, TILE), BF16)
    keep, give = kernel_call(
        y_sum_kernel, "y_sum", [eight] * 2, [SMEM] + [VMEM] * 5, [VMEM] * 2
    )(ids, *map(parted, (mine, below_low, above_low, below_high, above_high)))

    keep, grads = lax.optimization_barrier((keep, grads))
    partner = shift(give, "p", 1)
    stay, give = kernel_call(
        contrib_kernel, "contribs", [SHAPE((tokens // 2, width), BF16)] * 2,
        [SMEM] * 3 + [VMEM] * 2, [VMEM] * 2, [pltpu.SMEM((tile_total + 8,), jnp.int32)],
        moved=1 << 12,
    )(*lists, grads, delta_all)
    partner, give = lax.optimization_barrier((partner, give))
    pairs = kernel_call(pair_sum_kernel, "pair_sum", eight, [VMEM] * 2, VMEM)(keep, partner)
    arrived = exchange(pairs, "m")
    own_grad, squares = kernel_call(
        own_grad_kernel, "own_grad",
        [SHAPE((SLOT_CAP, TILE, TILE), F32), SHAPE((NY * NX * 2, 8, TILE), F32)],
        [SMEM, SMEM, VMEM], [VMEM] * 2,
    )(ids, owner_counts, arrived)


    rows = tokens // (2 * NX)
    _, give = lax.optimization_barrier((pairs, give))
    taken = shift(give, "core", 1)
    share, *others = kernel_call(
        core_sum_kernel, "core_sum", [SHAPE((rows, width), BF16)] * NX,
        [SMEM] + [VMEM] * 2, [VMEM] * NX, moved=1 << 12,
    )(ids, stay.reshape(NX, rows, width), taken.reshape(NX, rows, width))
    others = [shift(part, "x", away + 1) for away, part in enumerate(others)]
    squares, share, *others = lax.optimization_barrier((squares, share, *others))
    share = share.astype(F32)
    for part in others:
        share = share + part.astype(F32)
    gathered = lax.all_gather(share.astype(BF16), ("x", "core"), axis=0, tiled=True)
    input_grad = kernel_call(
        copy_kernel, "result", SHAPE((tokens, width), BF16), [ANY], ANY,
        [pltpu.VMEM((4, tokens // 4, width), BF16), pltpu.SemaphoreType.DMA((2, 4))],
        moved=4 << 20, vmem=63,
    )(gathered)

    squares = exchange(squares, ("y", "x", "core"))
    squares = kernel_call(relay_kernel, "relay", SHAPE((NZ, 8, TILE), F32), [VMEM], VMEM)(squares)
    squares = exchange(squares, Z)
    squares, input_grad = lax.optimization_barrier((squares, input_grad))
    count_all = float(NX * 2 * tile_total * TILE * TILE)

    def adam(*refs):
        adam_kernel(count_all, *refs)

    outs = kernel_call(
        adam, "adam", [SHAPE(delta_value.shape, F32)] * 3, [SMEM] * 2 + [VMEM] * 5, [VMEM] * 3
    )(ids, owner_counts, squares, own_grad, delta_value, moment_one, moment_two)
    return (input_grad, *outs)


def solution(mesh):
    grid = Mesh(mesh.devices.reshape(NY, NM, 2, NX, 2), ("y", "m", "p", "x", "core"))
    dp, tensor = ("y", "m", "p"), ("x", "core")
    tokens = P(dp, tensor)
    lists = P(tensor, None)
    slots = P(tensor, dp, None, None)
    return jax.shard_map(
        body,
        mesh=grid,
        in_specs=(tokens,) * 4 + (lists,) * 3 + (slots,) * 3,
        out_specs=(P(dp, None),) + (slots,) * 3,
        check_vma=False,
    )
```

```python
import functools

import jax
import jax.numpy as jnp
from jax import lax
from jax.experimental import pallas as pl
from jax.experimental.pallas import tpu as pltpu
from jax.sharding import Mesh, PartitionSpec as P

NY, NM, NX = 4, 8, 4
NZ = 2 * NM
Z = ("m", "p")
TILE = 128
SLOT_CAP = 2
LOW, HIGH = (0, NZ // 2), (NZ // 2, NZ)
BF16, F32 = jnp.bfloat16, jnp.float32
SMEM = pl.BlockSpec(memory_space=pltpu.SMEM)
VMEM = pl.BlockSpec(memory_space=pltpu.VMEM)
ANY = pl.BlockSpec(memory_space=pl.ANY)
SHAPE = jax.ShapeDtypeStruct


def kernel_call(
    kernel, name, outs, ins, out_specs, scratch=(), flops=0, moved=1 << 20, vmem=48
):
    return pl.pallas_call(
        kernel,
        out_shape=outs,
        in_specs=ins,
        out_specs=out_specs,
        scratch_shapes=scratch,
        compiler_params=pltpu.CompilerParams(vmem_limit_bytes=vmem * 1024 * 1024),
        cost_estimate=pl.CostEstimate(flops=flops, bytes_accessed=moved, transcendentals=0),
        name=name,
    )


def shift(value, axis, step):
    size = lax.axis_size(axis)
    return lax.ppermute(value, axis, [(i, (i + step) % size) for i in range(size)])


def exchange(value, axis):
    return lax.all_to_all(value, axis, split_axis=0, concat_axis=0, tiled=True)


def spread(value, axis):
    copies = jnp.broadcast_to(value[None], (lax.axis_size(axis),) + value.shape)
    return exchange(copies, axis)


def gate_kernel(ids_ref, gate_ref, up_ref, hidden_ref, grad_ref, turned_ref):
    blocks = 2 * NX
    rows = grad_ref.shape[1] // blocks
    core = ids_ref[3]
    for col in range(grad_ref.shape[0]):
        cut = slice(col * TILE, (col + 1) * TILE)
        gate = gate_ref[:, cut].astype(F32)
        sig = 1.0 / (1.0 + jnp.exp(-gate))
        value = (
            hidden_ref[:, cut].astype(F32)
            * up_ref[:, cut].astype(F32)
            * sig
            * (1.0 + gate * (1.0 - sig))
        )
        for block in range(blocks):
            place = pl.multiple_of((((block & 1) ^ core) * NX + (block >> 1)) * rows, rows)
            part = value[block * rows : (block + 1) * rows]
            grad_ref[col, pl.ds(place, rows)] = part.astype(BF16)
        turned_ref[col] = value.T.astype(BF16)


def load_features(own_ref, other_ref, features, sems, starts_ref, counts_ref):
    first = pltpu.make_async_copy(own_ref, features.at[0], sems.at[0])
    second = pltpu.make_async_copy(other_ref, features.at[1], sems.at[1])
    first.start()
    second.start()

    def owner_step(owner, start):
        starts_ref[owner] = start
        return start + counts_ref[0, owner]

    lax.fori_loop(0, counts_ref.shape[1], owner_step, 0)
    first.wait()
    second.wait()


def slot_products(group, owners, put, ids_ref, rows_ref, cols_ref, starts_ref, features, turned_ref):
    core = ids_ref[3]
    last = rows_ref.shape[1] - 1
    per_step = 4

    def step(index, carry):
        for part in range(per_step):
            owner = owners[0] + index * per_step + part
            start = starts_ref[group * NZ + owner]
            for rank in range(SLOT_CAP):
                k = jnp.minimum(start + rank, last)
                row = rows_ref[0, k]
                lane = pl.multiple_of((row & 7) * TILE, TILE)
                x = features[((row >> 3) & 1) ^ core, row >> 4, :, pl.ds(lane, TILE)]
                term = jnp.dot(turned_ref[cols_ref[0, k]], x, preferred_element_type=F32)
                put((index * per_step + part) * SLOT_CAP + rank, term.astype(BF16))
        return carry

    lax.fori_loop(0, (owners[1] - owners[0]) // per_step, step, 0)


def tile_kernel(
    parts, ids_ref, rows_ref, cols_ref, counts_ref, own_ref, other_ref, turned_ref, *refs
):
    features, starts_ref, sems = refs[len(parts) :]
    load_features(own_ref, other_ref, features, sems, starts_ref, counts_ref)
    for ref, (away, owners) in zip(refs, parts):

        def put(slot, term, ref=ref):
            ref[slot] = term

        slot_products(
            (ids_ref[0] + away) & (NY - 1), owners, put,
            ids_ref, rows_ref, cols_ref, starts_ref, features, turned_ref,
        )


def passing_kernel(up_ref, far_low_ref, down_ref, far_high_ref, up_out, down_out):
    up_out[...] = (up_ref[...].astype(F32) + far_low_ref[...].astype(F32)).astype(BF16)
    down_out[...] = (down_ref[...].astype(F32) + far_high_ref[...].astype(F32)).astype(BF16)


def y_sum_kernel(
    ids_ref, mine_ref, below_low_ref, above_low_ref, below_high_ref, above_high_ref,
    keep_ref, give_ref,
):
    parity = ids_ref[1] & 1
    half = NM // 2
    for m in range(NM):
        below, above = (below_low_ref, above_low_ref) if m < half else (below_high_ref, above_high_ref)

        def total(side):
            return (
                mine_ref[m, side].astype(F32)
                + below[m % half, side].astype(F32)
                + above[m % half, side].astype(F32)
            ).astype(BF16)

        keep_ref[m] = total(parity)
        give_ref[m] = total(1 - parity)


def pair_sum_kernel(keep_ref, taken_ref, out_ref):
    out_ref[...] = (keep_ref[...].astype(F32) + taken_ref[...].astype(F32)).astype(BF16)


def own_grad_kernel(ids_ref, counts_ref, arrived_ref, grad_ref, squares_ref):
    count = counts_ref[0, ids_ref[0] * NZ + ids_ref[1]]
    squares = jnp.zeros((TILE, TILE), F32)
    for rank in range(SLOT_CAP):
        total = arrived_ref[0, rank].astype(F32)
        for m in range(1, NM):
            total = total + arrived_ref[m, rank].astype(F32)
        total = jnp.where(rank < count, total, 0.0)
        grad_ref[rank] = total
        squares = squares + total * total
    squares_ref[...] = jnp.broadcast_to(jnp.sum(squares), squares_ref.shape)


def relay_kernel(arrived_ref, out_ref):
    total = jnp.sum(arrived_ref[...], axis=0, keepdims=True)
    out_ref[...] = jnp.broadcast_to(total, out_ref.shape)


def adam_kernel(
    count_all, ids_ref, counts_ref, arrived_ref, grad_ref, delta_ref, one_ref, two_ref,
    new_delta_ref, new_one_ref, new_two_ref,
):
    squares = jnp.sum(arrived_ref[...], axis=0)[0:1]
    factor = jnp.minimum(1.0, 1.0 / jnp.sqrt(squares / count_all + 1e-06))
    count = counts_ref[0, ids_ref[0] * NZ + ids_ref[1]]
    for rank in range(SLOT_CAP):
        live = rank < count
        clipped = factor * grad_ref[rank].T
        delta, one, two = delta_ref[0, rank], one_ref[0, rank], two_ref[0, rank]
        first = 0.9 * one + 0.1 * clipped
        second = 0.95 * two + 0.05 * clipped * clipped
        size = first / (1.0 - 0.9**10) / (jnp.sqrt(second / (1.0 - 0.95**10)) + 1e-08)
        updated = delta - 0.02 * (size + 0.1 * delta)
        new_delta_ref[0, rank] = jnp.where(live, updated, delta)
        new_one_ref[0, rank] = jnp.where(live, first, one)
        new_two_ref[0, rank] = jnp.where(live, second, two)


def turn_kernel(delta_ref, out_ref):
    for rank in range(SLOT_CAP):
        out_ref[rank] = delta_ref[0, rank].T.astype(BF16)


def contrib_kernel(
    ids_ref, rows_ref, cols_ref, counts_ref, grad_ref, delta_ref, stay_ref, give_ref, places_ref
):
    stay_ref[...] = jnp.zeros_like(stay_ref)
    give_ref[...] = jnp.zeros_like(give_ref)
    half = stay_ref.shape[0]
    y = ids_ref[0]

    def owner_step(owner, start):
        place = ((owner & (NZ - 1)) * NY + ((owner // NZ - y) & (NY - 1))) * SLOT_CAP
        places_ref[start] = place
        places_ref[start + 1] = place + 1
        return start + counts_ref[0, owner]

    lax.fori_loop(0, counts_ref.shape[1], owner_step, 0)
    per_step = 28

    def step(index, carry):
        last, total = carry
        for part in range(per_step):
            k = index * per_step + part
            row = rows_ref[0, k]
            product = jnp.dot(
                grad_ref[cols_ref[0, k]], delta_ref[places_ref[k]], preferred_element_type=F32
            )
            total = jnp.where(row == last, total, 0.0) + product
            lane = pl.multiple_of(row * TILE, TILE)
            stay_ref[:, pl.ds(lane, TILE)] = total[:half].astype(BF16)
            give_ref[:, pl.ds(lane, TILE)] = total[half:].astype(BF16)
            last = row
        return last, total

    lax.fori_loop(
        0, rows_ref.shape[1] // per_step, step,
        (jnp.int32(-1), jnp.zeros((TILE, TILE), F32)),
    )


def core_sum_kernel(ids_ref, stay_ref, taken_ref, *out_refs):
    for away, ref in enumerate(out_refs):
        at = (ids_ref[2] + away) & (NX - 1)
        ref[...] = (stay_ref[at].astype(F32) + taken_ref[at].astype(F32)).astype(BF16)


def copy_kernel(in_ref, out_ref, held, sems):
    chunks = held.shape[0]
    rows = in_ref.shape[0] // chunks

    def part(ref, chunk):
        return ref.at[pl.ds(chunk * rows, rows)]

    loads = [
        pltpu.make_async_copy(part(in_ref, i), held.at[i], sems.at[0, i]) for i in range(chunks)
    ]
    stores = [
        pltpu.make_async_copy(held.at[i], part(out_ref, i), sems.at[1, i]) for i in range(chunks)
    ]
    for load in loads:
        load.start()
    for load, store in zip(loads, stores):
        load.wait()
        store.start()
    for store in stores:
        store.wait()


def body(
    features, gate_pre, up_pre, hidden_grad, tile_rows, tile_cols, owner_counts,
    delta_value, moment_one, moment_two,
):
    ids = jnp.stack([lax.axis_index(name) for name in ("y", Z, "x", "core")]).astype(jnp.int32)
    tokens, hidden = gate_pre.shape
    shard_width = features.shape[1]
    width = shard_width * NX * 2
    tile_total = tile_rows.shape[1]
    lists = (tile_rows, tile_cols, owner_counts)

    own = spread(features, "x")
    other = shift(own, "core", 1)

    delta_half = kernel_call(
        turn_kernel, "turn", SHAPE(delta_value.shape[1:], BF16), [VMEM], VMEM
    )(delta_value)
    delta_y = jnp.concatenate(
        [delta_half] + [shift(delta_half, "y", -away) for away in range(1, NY)], axis=0
    )
    _, delta_y = lax.optimization_barrier((own, delta_y))
    delta_all = lax.all_gather(delta_y, Z, axis=0, tiled=True)

    grads, turned = kernel_call(
        gate_kernel, "gate", [SHAPE((hidden // TILE, tokens, TILE), BF16)] * 2,
        [SMEM] + [VMEM] * 3, [VMEM] * 2, flops=tokens * hidden * 12, moved=tokens * hidden * 10,
    )(ids, gate_pre, up_pre, hidden_grad)

    tile_ins = [SMEM] * 4 + [ANY, ANY, VMEM]
    tile_scratch = [
        pltpu.VMEM((2, NX, tokens, shard_width), BF16),
        pltpu.SMEM((owner_counts.shape[1],), jnp.int32),
        pltpu.SemaphoreType.DMA((2,)),
    ]

    def terms(turned, *parts):
        *values, turned = lax.optimization_barrier((*kernel_call(
            functools.partial(tile_kernel, parts), "tiles",
            [SHAPE(((last - first) * SLOT_CAP, TILE, TILE), BF16) for _, (first, last) in parts],
            tile_ins, [VMEM] * len(parts), tile_scratch,
            flops=2 * tile_total * TILE**3 // 4, moved=2 << 20,
        )(ids, *lists, own, other, turned), turned))
        return values, turned

    (far_low, far_high), turned = terms(turned, (2, LOW), (2, HIGH))
    far_low, far_high = shift(far_low, "y", 1), shift(far_high, "y", -1)
    (up_high, down_low), turned = terms(turned, (1, HIGH), (3, LOW))
    below_high, above_low = shift(up_high, "y", 1), shift(down_low, "y", -1)
    (up_low, down_high, mine), turned = terms(turned, (1, LOW), (3, HIGH), (0, (0, NZ)))
    half = SHAPE(up_low.shape, BF16)
    up_low, down_high = kernel_call(
        passing_kernel, "passing", [half] * 2, [VMEM] * 4, [VMEM] * 2
    )(up_low, far_low, down_high, far_high)
    below_low, above_high = shift(up_low, "y", 1), shift(down_high, "y", -1)

    def parted(value):
        return value.reshape(-1, 2, SLOT_CAP, TILE, TILE)

    eight = SHAPE((NM, SLOT_CAP, TILE, TILE), BF16)
    keep, give = kernel_call(
        y_sum_kernel, "y_sum", [eight] * 2, [SMEM] + [VMEM] * 5, [VMEM] * 2
    )(ids, *map(parted, (mine, below_low, above_low, below_high, above_high)))

    partner = shift(give, "p", 1)
    pairs = kernel_call(pair_sum_kernel, "pair_sum", eight, [VMEM] * 2, VMEM)(keep, partner)
    pairs, grads = lax.optimization_barrier((pairs, grads))
    arrived = exchange(pairs, "m")
    own_grad, squares = kernel_call(
        own_grad_kernel, "own_grad",
        [SHAPE((SLOT_CAP, TILE, TILE), F32), SHAPE((NY * NX * 2, 8, TILE), F32)],
        [SMEM, SMEM, VMEM], [VMEM] * 2,
    )(ids, owner_counts, arrived)


    stay, give = kernel_call(
        contrib_kernel, "contribs", [SHAPE((tokens // 2, width), BF16)] * 2,
        [SMEM] * 4 + [VMEM] * 2, [VMEM] * 2, [pltpu.SMEM((tile_total + 8,), jnp.int32)],
        moved=1 << 12,
    )(ids, *lists, grads, delta_all)

    rows = tokens // (2 * NX)
    taken = shift(give, "core", 1)
    share, *others = kernel_call(
        core_sum_kernel, "core_sum", [SHAPE((rows, width), BF16)] * NX,
        [SMEM] + [VMEM] * 2, [VMEM] * NX, moved=1 << 12,
    )(ids, stay.reshape(NX, rows, width), taken.reshape(NX, rows, width))
    others = [shift(part, "x", away + 1) for away, part in enumerate(others)]
    squares, share, *others = lax.optimization_barrier((squares, share, *others))
    share = share.astype(F32)
    for part in others:
        share = share + part.astype(F32)
    gathered = lax.all_gather(share.astype(BF16), ("x", "core"), axis=0, tiled=True)
    input_grad = kernel_call(
        copy_kernel, "result", SHAPE((tokens, width), BF16), [ANY], ANY,
        [pltpu.VMEM((4, tokens // 4, width), BF16), pltpu.SemaphoreType.DMA((2, 4))],
        moved=4 << 20, vmem=63,
    )(gathered)

    squares = exchange(squares, ("y", "x", "core"))
    squares = kernel_call(relay_kernel, "relay", SHAPE((NZ, 8, TILE), F32), [VMEM], VMEM)(squares)
    squares = exchange(squares, Z)
    squares, input_grad = lax.optimization_barrier((squares, input_grad))
    count_all = float(NX * 2 * tile_total * TILE * TILE)

    def adam(*refs):
        adam_kernel(count_all, *refs)

    outs = kernel_call(
        adam, "adam", [SHAPE(delta_value.shape, F32)] * 3, [SMEM] * 2 + [VMEM] * 5, [VMEM] * 3
    )(ids, owner_counts, squares, own_grad, delta_value, moment_one, moment_two)
    return (input_grad, *outs)


def solution(mesh):
    grid = Mesh(mesh.devices.reshape(NY, NM, 2, NX, 2), ("y", "m", "p", "x", "core"))
    dp, tensor = ("y", "m", "p"), ("x", "core")
    tokens = P(dp, tensor)
    lists = P(tensor, None)
    slots = P(tensor, dp, None, None)
    return jax.shard_map(
        body,
        mesh=grid,
        in_specs=(tokens,) * 4 + (lists,) * 3 + (slots,) * 3,
        out_specs=(P(dp, None),) + (slots,) * 3,
        check_vma=False,
    )
```

```python
import functools

import jax
import jax.numpy as jnp
from jax import lax
from jax.experimental import pallas as pl
from jax.experimental.pallas import tpu as pltpu
from jax.sharding import Mesh, PartitionSpec as P

NY, NM, NX = 4, 8, 4
NZ = 2 * NM
Z = ("m", "p")
TILE = 128
SLOT_CAP = 2
LOW, HIGH = (0, NZ // 2), (NZ // 2, NZ)
BF16, F32 = jnp.bfloat16, jnp.float32
SMEM = pl.BlockSpec(memory_space=pltpu.SMEM)
VMEM = pl.BlockSpec(memory_space=pltpu.VMEM)
ANY = pl.BlockSpec(memory_space=pl.ANY)
SHAPE = jax.ShapeDtypeStruct


def kernel_call(
    kernel, name, outs, ins, out_specs, scratch=(), flops=0, moved=1 << 20, vmem=48
):
    return pl.pallas_call(
        kernel,
        out_shape=outs,
        in_specs=ins,
        out_specs=out_specs,
        scratch_shapes=scratch,
        compiler_params=pltpu.CompilerParams(vmem_limit_bytes=vmem * 1024 * 1024),
        cost_estimate=pl.CostEstimate(flops=flops, bytes_accessed=moved, transcendentals=0),
        name=name,
    )


def shift(value, axis, step):
    size = lax.axis_size(axis)
    return lax.ppermute(value, axis, [(i, (i + step) % size) for i in range(size)])


def exchange(value, axis):
    return lax.all_to_all(value, axis, split_axis=0, concat_axis=0, tiled=True)


def spread(value, axis):
    copies = jnp.broadcast_to(value[None], (lax.axis_size(axis),) + value.shape)
    return exchange(copies, axis)


def gate_kernel(ids_ref, gate_ref, up_ref, hidden_ref, grad_ref, turned_ref):
    blocks = 2 * NX
    rows = grad_ref.shape[1] // blocks
    core = ids_ref[3]
    for col in range(grad_ref.shape[0]):
        cut = slice(col * TILE, (col + 1) * TILE)
        gate = gate_ref[:, cut].astype(F32)
        sig = 1.0 / (1.0 + jnp.exp(-gate))
        value = (
            hidden_ref[:, cut].astype(F32)
            * up_ref[:, cut].astype(F32)
            * sig
            * (1.0 + gate * (1.0 - sig))
        )
        for block in range(blocks):
            place = pl.multiple_of((((block & 1) ^ core) * NX + (block >> 1)) * rows, rows)
            part = value[block * rows : (block + 1) * rows]
            grad_ref[col, pl.ds(place, rows)] = part.astype(BF16)
        turned_ref[col] = value.T.astype(BF16)


def load_features(own_ref, other_ref, features, sems, starts_ref, counts_ref):
    first = pltpu.make_async_copy(own_ref, features.at[0], sems.at[0])
    second = pltpu.make_async_copy(other_ref, features.at[1], sems.at[1])
    first.start()
    second.start()

    def owner_step(owner, start):
        starts_ref[owner] = start
        return start + counts_ref[0, owner]

    lax.fori_loop(0, counts_ref.shape[1], owner_step, 0)
    first.wait()
    second.wait()


def slot_products(group, owners, put, ids_ref, rows_ref, cols_ref, starts_ref, features, turned_ref):
    core = ids_ref[3]
    last = rows_ref.shape[1] - 1
    per_step = 4

    def step(index, carry):
        for part in range(per_step):
            owner = owners[0] + index * per_step + part
            start = starts_ref[group * NZ + owner]
            for rank in range(SLOT_CAP):
                k = jnp.minimum(start + rank, last)
                row = rows_ref[0, k]
                lane = pl.multiple_of((row & 7) * TILE, TILE)
                x = features[((row >> 3) & 1) ^ core, row >> 4, :, pl.ds(lane, TILE)]
                term = jnp.dot(turned_ref[cols_ref[0, k]], x, preferred_element_type=F32)
                put((index * per_step + part) * SLOT_CAP + rank, term.astype(BF16))
        return carry

    lax.fori_loop(0, (owners[1] - owners[0]) // per_step, step, 0)


def tile_kernel(
    parts, ids_ref, rows_ref, cols_ref, counts_ref, own_ref, other_ref, turned_ref, *refs
):
    features, starts_ref, sems = refs[len(parts) :]
    load_features(own_ref, other_ref, features, sems, starts_ref, counts_ref)
    for ref, (away, owners) in zip(refs, parts):

        def put(slot, term, ref=ref):
            ref[slot] = term

        slot_products(
            (ids_ref[0] + away) & (NY - 1), owners, put,
            ids_ref, rows_ref, cols_ref, starts_ref, features, turned_ref,
        )


def passing_kernel(up_ref, far_low_ref, down_ref, far_high_ref, up_out, down_out):
    up_out[...] = (up_ref[...].astype(F32) + far_low_ref[...].astype(F32)).astype(BF16)
    down_out[...] = (down_ref[...].astype(F32) + far_high_ref[...].astype(F32)).astype(BF16)


def y_sum_kernel(
    ids_ref, mine_ref, below_low_ref, above_low_ref, below_high_ref, above_high_ref,
    keep_ref, give_ref,
):
    parity = ids_ref[1] & 1
    half = NM // 2
    for m in range(NM):
        below, above = (below_low_ref, above_low_ref) if m < half else (below_high_ref, above_high_ref)

        def total(side):
            return (
                mine_ref[m, side].astype(F32)
                + below[m % half, side].astype(F32)
                + above[m % half, side].astype(F32)
            ).astype(BF16)

        keep_ref[m] = total(parity)
        give_ref[m] = total(1 - parity)


def pair_sum_kernel(keep_ref, taken_ref, _, out_ref):
    out_ref[...] = (keep_ref[...].astype(F32) + taken_ref[...].astype(F32)).astype(BF16)


def own_grad_kernel(ids_ref, counts_ref, arrived_ref, grad_ref, squares_ref):
    count = counts_ref[0, ids_ref[0] * NZ + ids_ref[1]]
    squares = jnp.zeros((TILE, TILE), F32)
    for rank in range(SLOT_CAP):
        total = arrived_ref[0, rank].astype(F32)
        for m in range(1, NM):
            total = total + arrived_ref[m, rank].astype(F32)
        total = jnp.where(rank < count, total, 0.0)
        grad_ref[rank] = total
        squares = squares + total * total
    squares_ref[...] = jnp.broadcast_to(jnp.sum(squares), squares_ref.shape)


def relay_kernel(arrived_ref, out_ref):
    total = jnp.sum(arrived_ref[...], axis=0, keepdims=True)
    out_ref[...] = jnp.broadcast_to(total, out_ref.shape)


def adam_kernel(
    count_all, ids_ref, counts_ref, arrived_ref, grad_ref, delta_ref, one_ref, two_ref,
    new_delta_ref, new_one_ref, new_two_ref,
):
    squares = jnp.sum(arrived_ref[...], axis=0)[0:1]
    factor = jnp.minimum(1.0, 1.0 / jnp.sqrt(squares / count_all + 1e-06))
    count = counts_ref[0, ids_ref[0] * NZ + ids_ref[1]]
    for rank in range(SLOT_CAP):
        live = rank < count
        clipped = factor * grad_ref[rank].T
        delta, one, two = delta_ref[0, rank], one_ref[0, rank], two_ref[0, rank]
        first = 0.9 * one + 0.1 * clipped
        second = 0.95 * two + 0.05 * clipped * clipped
        size = first / (1.0 - 0.9**10) / (jnp.sqrt(second / (1.0 - 0.95**10)) + 1e-08)
        updated = delta - 0.02 * (size + 0.1 * delta)
        new_delta_ref[0, rank] = jnp.where(live, updated, delta)
        new_one_ref[0, rank] = jnp.where(live, first, one)
        new_two_ref[0, rank] = jnp.where(live, second, two)


def turn_kernel(delta_ref, out_ref):
    for rank in range(SLOT_CAP):
        out_ref[rank] = delta_ref[0, rank].T.astype(BF16)


def contrib_kernel(
    rows_ref, cols_ref, counts_ref, grad_ref, delta_ref, stay_ref, give_ref, places_ref
):
    stay_ref[...] = jnp.zeros_like(stay_ref)
    give_ref[...] = jnp.zeros_like(give_ref)
    half = stay_ref.shape[0]

    def owner_step(owner, start):
        place = ((owner & (NZ - 1)) * NY + owner // NZ) * SLOT_CAP
        places_ref[start] = place
        places_ref[start + 1] = place + 1
        return start + counts_ref[0, owner]

    lax.fori_loop(0, counts_ref.shape[1], owner_step, 0)
    per_step = 28

    def step(index, carry):
        last, total = carry
        for part in range(per_step):
            k = index * per_step + part
            row = rows_ref[0, k]
            product = jnp.dot(
                grad_ref[cols_ref[0, k]], delta_ref[places_ref[k]], preferred_element_type=F32
            )
            total = jnp.where(row == last, total, 0.0) + product
            lane = pl.multiple_of(row * TILE, TILE)
            stay_ref[:, pl.ds(lane, TILE)] = total[:half].astype(BF16)
            give_ref[:, pl.ds(lane, TILE)] = total[half:].astype(BF16)
            last = row
        return last, total

    lax.fori_loop(
        0, rows_ref.shape[1] // per_step, step,
        (jnp.int32(-1), jnp.zeros((TILE, TILE), F32)),
    )


def core_sum_kernel(ids_ref, stay_ref, taken_ref, *out_refs):
    for away, ref in enumerate(out_refs):
        at = (ids_ref[2] + away) & (NX - 1)
        ref[...] = (stay_ref[at].astype(F32) + taken_ref[at].astype(F32)).astype(BF16)


def copy_kernel(in_ref, out_ref, held, sems):
    chunks = held.shape[0]
    rows = in_ref.shape[0] // chunks

    def part(ref, chunk):
        return ref.at[pl.ds(chunk * rows, rows)]

    loads = [
        pltpu.make_async_copy(part(in_ref, i), held.at[i], sems.at[0, i]) for i in range(chunks)
    ]
    stores = [
        pltpu.make_async_copy(held.at[i], part(out_ref, i), sems.at[1, i]) for i in range(chunks)
    ]
    for load in loads:
        load.start()
    for load, store in zip(loads, stores):
        load.wait()
        store.start()
    for store in stores:
        store.wait()


def body(
    features, gate_pre, up_pre, hidden_grad, tile_rows, tile_cols, owner_counts,
    delta_value, moment_one, moment_two,
):
    ids = jnp.stack([lax.axis_index(name) for name in ("y", Z, "x", "core")]).astype(jnp.int32)
    tokens, hidden = gate_pre.shape
    shard_width = features.shape[1]
    width = shard_width * NX * 2
    tile_total = tile_rows.shape[1]
    lists = (tile_rows, tile_cols, owner_counts)

    own = spread(features, "x")
    other = shift(own, "core", 1)

    delta_half = kernel_call(
        turn_kernel, "turn", SHAPE(delta_value.shape[1:], BF16), [VMEM], VMEM
    )(delta_value)
    delta_y = spread(delta_half, "y").reshape(NY * SLOT_CAP, TILE, TILE)
    delta_all = lax.all_gather(delta_y, Z, axis=0, tiled=True)

    grads, turned = kernel_call(
        gate_kernel, "gate", [SHAPE((hidden // TILE, tokens, TILE), BF16)] * 2,
        [SMEM] + [VMEM] * 3, [VMEM] * 2, flops=tokens * hidden * 12, moved=tokens * hidden * 10,
    )(ids, gate_pre, up_pre, hidden_grad)

    tile_ins = [SMEM] * 4 + [ANY, ANY, VMEM]
    tile_scratch = [
        pltpu.VMEM((2, NX, tokens, shard_width), BF16),
        pltpu.SMEM((owner_counts.shape[1],), jnp.int32),
        pltpu.SemaphoreType.DMA((2,)),
    ]

    def terms(turned, *parts):
        *values, turned = lax.optimization_barrier((*kernel_call(
            functools.partial(tile_kernel, parts), "tiles",
            [SHAPE(((last - first) * SLOT_CAP, TILE, TILE), BF16) for _, (first, last) in parts],
            tile_ins, [VMEM] * len(parts), tile_scratch,
            flops=2 * tile_total * TILE**3 // 4, moved=2 << 20,
        )(ids, *lists, own, other, turned), turned))
        return values, turned

    (far_low, far_high), turned = terms(turned, (2, LOW), (2, HIGH))
    far_low, far_high = shift(far_low, "y", 1), shift(far_high, "y", -1)
    (up_high, down_low), turned = terms(turned, (1, HIGH), (3, LOW))
    below_high, above_low = shift(up_high, "y", 1), shift(down_low, "y", -1)
    (up_low, down_high, mine), turned = terms(turned, (1, LOW), (3, HIGH), (0, (0, NZ)))
    half = SHAPE(up_low.shape, BF16)
    up_low, down_high = kernel_call(
        passing_kernel, "passing", [half] * 2, [VMEM] * 4, [VMEM] * 2
    )(up_low, far_low, down_high, far_high)
    below_low, above_high = shift(up_low, "y", 1), shift(down_high, "y", -1)

    def parted(value):
        return value.reshape(-1, 2, SLOT_CAP, TILE, TILE)

    eight = SHAPE((NM, SLOT_CAP, TILE, TILE), BF16)
    keep, give = kernel_call(
        y_sum_kernel, "y_sum", [eight] * 2, [SMEM] + [VMEM] * 5, [VMEM] * 2
    )(ids, *map(parted, (mine, below_low, above_low, below_high, above_high)))

    keep, grads = lax.optimization_barrier((keep, grads))
    partner = shift(give, "p", 1)
    stay, give = kernel_call(
        contrib_kernel, "contribs", [SHAPE((tokens // 2, width), BF16)] * 2,
        [SMEM] * 3 + [VMEM] * 2, [VMEM] * 2, [pltpu.SMEM((tile_total + 8,), jnp.int32)],
        moved=1 << 12,
    )(*lists, grads, delta_all)
    pairs = kernel_call(pair_sum_kernel, "pair_sum", eight, [VMEM] * 2 + [ANY], VMEM)(
        keep, partner, give
    )
    arrived = exchange(pairs, "m")
    own_grad, squares = kernel_call(
        own_grad_kernel, "own_grad",
        [SHAPE((SLOT_CAP, TILE, TILE), F32), SHAPE((NZ, 8, TILE), F32)],
        [SMEM, SMEM, VMEM], [VMEM] * 2,
    )(ids, owner_counts, arrived)


    rows = tokens // (2 * NX)
    _, give = lax.optimization_barrier((pairs, give))
    taken = shift(give, "core", 1)
    share, *others = kernel_call(
        core_sum_kernel, "core_sum", [SHAPE((rows, width), BF16)] * NX,
        [SMEM] + [VMEM] * 2, [VMEM] * NX, moved=1 << 12,
    )(ids, stay.reshape(NX, rows, width), taken.reshape(NX, rows, width))
    others = [shift(part, "x", away + 1) for away, part in enumerate(others)]
    squares, share, *others = lax.optimization_barrier((squares, share, *others))
    share = share.astype(F32)
    for part in others:
        share = share + part.astype(F32)
    gathered = lax.all_gather(share.astype(BF16), ("x", "core"), axis=0, tiled=True)
    input_grad = kernel_call(
        copy_kernel, "result", SHAPE((tokens, width), BF16), [ANY], ANY,
        [pltpu.VMEM((4, tokens // 4, width), BF16), pltpu.SemaphoreType.DMA((2, 4))],
        moved=4 << 20, vmem=63,
    )(gathered)

    squares = exchange(squares, Z)
    near = SHAPE((NY * NX * 2, 8, TILE), F32)
    squares = kernel_call(relay_kernel, "relay", near, [VMEM], VMEM)(squares)
    squares = exchange(squares, ("y", "x", "core"))
    squares, input_grad = lax.optimization_barrier((squares, input_grad))
    count_all = float(NX * 2 * tile_total * TILE * TILE)

    def adam(*refs):
        adam_kernel(count_all, *refs)

    outs = kernel_call(
        adam, "adam", [SHAPE(delta_value.shape, F32)] * 3, [SMEM] * 2 + [VMEM] * 5, [VMEM] * 3
    )(ids, owner_counts, squares, own_grad, delta_value, moment_one, moment_two)
    return (input_grad, *outs)


def solution(mesh):
    grid = Mesh(mesh.devices.reshape(NY, NM, 2, NX, 2), ("y", "m", "p", "x", "core"))
    dp, tensor = ("y", "m", "p"), ("x", "core")
    tokens = P(dp, tensor)
    lists = P(tensor, None)
    slots = P(tensor, dp, None, None)
    return jax.shard_map(
        body,
        mesh=grid,
        in_specs=(tokens,) * 4 + (lists,) * 3 + (slots,) * 3,
        out_specs=(P(dp, None),) + (slots,) * 3,
        check_vma=False,
    )
```

```python
import functools

import jax
import jax.numpy as jnp
from jax import lax
from jax.experimental import pallas as pl
from jax.experimental.pallas import tpu as pltpu
from jax.sharding import Mesh, PartitionSpec as P

NY, NM, NX = 4, 8, 4
NZ = 2 * NM
Z = ("m", "p")
TILE = 128
SLOT_CAP = 2
LOW, HIGH = (0, NZ // 2), (NZ // 2, NZ)
BF16, F32 = jnp.bfloat16, jnp.float32
SMEM = pl.BlockSpec(memory_space=pltpu.SMEM)
VMEM = pl.BlockSpec(memory_space=pltpu.VMEM)
ANY = pl.BlockSpec(memory_space=pl.ANY)
SHAPE = jax.ShapeDtypeStruct


def kernel_call(
    kernel, name, outs, ins, out_specs, scratch=(), flops=0, moved=1 << 20, vmem=48
):
    return pl.pallas_call(
        kernel,
        out_shape=outs,
        in_specs=ins,
        out_specs=out_specs,
        scratch_shapes=scratch,
        compiler_params=pltpu.CompilerParams(vmem_limit_bytes=vmem * 1024 * 1024),
        cost_estimate=pl.CostEstimate(flops=flops, bytes_accessed=moved, transcendentals=0),
        name=name,
    )


def swap(value, axis, bits):
    return lax.ppermute(value, axis, [(i, i ^ bits) for i in range(lax.axis_size(axis))])


def exchange(value, axis):
    return lax.all_to_all(value, axis, split_axis=0, concat_axis=0, tiled=True)


def spread(value, axis):
    copies = jnp.broadcast_to(value[None], (lax.axis_size(axis),) + value.shape)
    return exchange(copies, axis)


def gate_kernel(ids_ref, gate_ref, up_ref, hidden_ref, grad_ref, turned_ref):
    blocks = 2 * NX
    rows = grad_ref.shape[1] // blocks
    core = ids_ref[3]
    for col in range(grad_ref.shape[0]):
        cut = slice(col * TILE, (col + 1) * TILE)
        gate = gate_ref[:, cut].astype(F32)
        sig = 1.0 / (1.0 + jnp.exp(-gate))
        value = (
            hidden_ref[:, cut].astype(F32)
            * up_ref[:, cut].astype(F32)
            * sig
            * (1.0 + gate * (1.0 - sig))
        )
        for block in range(blocks):
            place = pl.multiple_of((((block & 1) ^ core) * NX + (block >> 1)) * rows, rows)
            part = value[block * rows : (block + 1) * rows]
            grad_ref[col, pl.ds(place, rows)] = part.astype(BF16)
        turned_ref[col] = value.T.astype(BF16)


def load_features(own_ref, other_ref, features, sems, starts_ref, counts_ref):
    first = pltpu.make_async_copy(own_ref, features.at[0], sems.at[0])
    second = pltpu.make_async_copy(other_ref, features.at[1], sems.at[1])
    first.start()
    second.start()

    def owner_step(owner, start):
        starts_ref[owner] = start
        return start + counts_ref[0, owner]

    lax.fori_loop(0, counts_ref.shape[1], owner_step, 0)
    first.wait()
    second.wait()


def slot_products(group, owners, put, ids_ref, rows_ref, cols_ref, starts_ref, features, turned_ref):
    core = ids_ref[3]
    last = rows_ref.shape[1] - 1
    per_step = 4

    def step(index, carry):
        for part in range(per_step):
            owner = owners[0] + index * per_step + part
            start = starts_ref[group * NZ + owner]
            for rank in range(SLOT_CAP):
                k = jnp.minimum(start + rank, last)
                row = rows_ref[0, k]
                lane = pl.multiple_of((row & 7) * TILE, TILE)
                x = features[((row >> 3) & 1) ^ core, row >> 4, :, pl.ds(lane, TILE)]
                term = jnp.dot(turned_ref[cols_ref[0, k]], x, preferred_element_type=F32)
                put((index * per_step + part) * SLOT_CAP + rank, term.astype(BF16))
        return carry

    lax.fori_loop(0, (owners[1] - owners[0]) // per_step, step, 0)


def tile_kernel(
    parts, ids_ref, rows_ref, cols_ref, counts_ref, own_ref, other_ref, turned_ref, *refs
):
    features, starts_ref, sems = refs[len(parts) :]
    load_features(own_ref, other_ref, features, sems, starts_ref, counts_ref)
    for ref, (bits, owners) in zip(refs, parts):

        def put(slot, term, ref=ref):
            ref[slot] = term

        slot_products(
            ids_ref[0] ^ bits, owners, put,
            ids_ref, rows_ref, cols_ref, starts_ref, features, turned_ref,
        )


def passing_kernel(one_ref, for_one_ref, other_ref, for_other_ref, one_out, other_out):
    one_out[...] = (one_ref[...].astype(F32) + for_one_ref[...].astype(F32)).astype(BF16)
    other_out[...] = (other_ref[...].astype(F32) + for_other_ref[...].astype(F32)).astype(BF16)


def y_sum_kernel(
    ids_ref, mine_ref, one_low_ref, other_low_ref, one_high_ref, other_high_ref,
    keep_ref, give_ref,
):
    parity = ids_ref[1] & 1
    half = NM // 2
    for m in range(NM):
        one, other = (one_low_ref, other_low_ref) if m < half else (one_high_ref, other_high_ref)

        def total(side):
            return (
                mine_ref[m, side].astype(F32)
                + one[m % half, side].astype(F32)
                + other[m % half, side].astype(F32)
            ).astype(BF16)

        keep_ref[m] = total(parity)
        give_ref[m] = total(1 - parity)


def pair_sum_kernel(keep_ref, taken_ref, _, out_ref):
    out_ref[...] = (keep_ref[...].astype(F32) + taken_ref[...].astype(F32)).astype(BF16)


def own_grad_kernel(ids_ref, counts_ref, arrived_ref, grad_ref, squares_ref):
    count = counts_ref[0, ids_ref[0] * NZ + ids_ref[1]]
    squares = jnp.zeros((TILE, TILE), F32)
    for rank in range(SLOT_CAP):
        total = arrived_ref[0, rank].astype(F32)
        for m in range(1, NM):
            total = total + arrived_ref[m, rank].astype(F32)
        total = jnp.where(rank < count, total, 0.0)
        grad_ref[rank] = total
        squares = squares + total * total
    squares_ref[...] = jnp.broadcast_to(jnp.sum(squares), squares_ref.shape)


def relay_kernel(arrived_ref, out_ref):
    total = jnp.sum(arrived_ref[...], axis=0, keepdims=True)
    out_ref[...] = jnp.broadcast_to(total, out_ref.shape)


def adam_kernel(
    count_all, ids_ref, counts_ref, arrived_ref, grad_ref, delta_ref, one_ref, two_ref,
    new_delta_ref, new_one_ref, new_two_ref,
):
    squares = jnp.sum(arrived_ref[...], axis=0)[0:1]
    factor = jnp.minimum(1.0, 1.0 / jnp.sqrt(squares / count_all + 1e-06))
    count = counts_ref[0, ids_ref[0] * NZ + ids_ref[1]]
    for rank in range(SLOT_CAP):
        live = rank < count
        clipped = factor * grad_ref[rank].T
        delta, one, two = delta_ref[0, rank], one_ref[0, rank], two_ref[0, rank]
        first = 0.9 * one + 0.1 * clipped
        second = 0.95 * two + 0.05 * clipped * clipped
        size = first / (1.0 - 0.9**10) / (jnp.sqrt(second / (1.0 - 0.95**10)) + 1e-08)
        updated = delta - 0.02 * (size + 0.1 * delta)
        new_delta_ref[0, rank] = jnp.where(live, updated, delta)
        new_one_ref[0, rank] = jnp.where(live, first, one)
        new_two_ref[0, rank] = jnp.where(live, second, two)


def turn_kernel(delta_ref, out_ref):
    for rank in range(SLOT_CAP):
        out_ref[rank] = delta_ref[0, rank].T.astype(BF16)


def contrib_kernel(
    rows_ref, cols_ref, counts_ref, grads_ref, deltas_ref, stay_ref, give_ref,
    places_ref, grad_ref, delta_ref, sems,
):
    loads = [
        pltpu.make_async_copy(deltas_ref, delta_ref, sems.at[0]),
        pltpu.make_async_copy(grads_ref, grad_ref, sems.at[1]),
    ]
    for load in loads:
        load.start()
    stay_ref[...] = jnp.zeros_like(stay_ref)
    give_ref[...] = jnp.zeros_like(give_ref)
    half = stay_ref.shape[0]

    def owner_step(owner, start):
        place = ((owner & (NZ - 1)) * NY + owner // NZ) * SLOT_CAP
        places_ref[start] = place
        places_ref[start + 1] = place + 1
        return start + counts_ref[0, owner]

    lax.fori_loop(0, counts_ref.shape[1], owner_step, 0)
    for load in loads:
        load.wait()
    per_step = 28

    def step(index, carry):
        last, total = carry
        for part in range(per_step):
            k = index * per_step + part
            row = rows_ref[0, k]
            product = jnp.dot(
                grad_ref[cols_ref[0, k]], delta_ref[places_ref[k]], preferred_element_type=F32
            )
            total = jnp.where(row == last, total, 0.0) + product
            lane = pl.multiple_of(row * TILE, TILE)
            stay_ref[:, pl.ds(lane, TILE)] = total[:half].astype(BF16)
            give_ref[:, pl.ds(lane, TILE)] = total[half:].astype(BF16)
            last = row
        return last, total

    lax.fori_loop(
        0, rows_ref.shape[1] // per_step, step,
        (jnp.int32(-1), jnp.zeros((TILE, TILE), F32)),
    )


def core_sum_kernel(ids_ref, stay_ref, taken_ref, *out_refs):
    for bits, ref in enumerate(out_refs):
        at = ids_ref[2] ^ bits
        ref[...] = (stay_ref[at].astype(F32) + taken_ref[at].astype(F32)).astype(BF16)


def copy_kernel(in_ref, out_ref, held, sems):
    chunks = held.shape[0]
    rows = in_ref.shape[0] // chunks

    def part(ref, chunk):
        return ref.at[pl.ds(chunk * rows, rows)]

    loads = [
        pltpu.make_async_copy(part(in_ref, i), held.at[i], sems.at[0, i]) for i in range(chunks)
    ]
    stores = [
        pltpu.make_async_copy(held.at[i], part(out_ref, i), sems.at[1, i]) for i in range(chunks)
    ]
    for load in loads:
        load.start()
    for load, store in zip(loads, stores):
        load.wait()
        store.start()
    for store in stores:
        store.wait()


def body(
    features, gate_pre, up_pre, hidden_grad, tile_rows, tile_cols, owner_counts,
    delta_value, moment_one, moment_two,
):
    ids = jnp.stack([lax.axis_index(name) for name in ("y", Z, "x", "core")]).astype(jnp.int32)
    tokens, hidden = gate_pre.shape
    shard_width = features.shape[1]
    width = shard_width * NX * 2
    tile_total = tile_rows.shape[1]
    lists = (tile_rows, tile_cols, owner_counts)

    own = spread(features, "x")
    other = swap(own, "core", 1)

    delta_half = kernel_call(
        turn_kernel, "turn", SHAPE(delta_value.shape[1:], BF16), [VMEM], VMEM
    )(delta_value)
    delta_y = spread(delta_half, "y").reshape(NY * SLOT_CAP, TILE, TILE)
    delta_all = lax.all_gather(delta_y, Z, axis=0, tiled=True)

    grads, turned = kernel_call(
        gate_kernel, "gate", [SHAPE((hidden // TILE, tokens, TILE), BF16)] * 2,
        [SMEM] + [VMEM] * 3, [VMEM] * 2, flops=tokens * hidden * 12, moved=tokens * hidden * 10,
    )(ids, gate_pre, up_pre, hidden_grad)

    tile_ins = [SMEM] * 4 + [ANY, ANY, VMEM]
    tile_scratch = [
        pltpu.VMEM((2, NX, tokens, shard_width), BF16),
        pltpu.SMEM((owner_counts.shape[1],), jnp.int32),
        pltpu.SemaphoreType.DMA((2,)),
    ]

    def terms(turned, *parts):
        *values, turned = lax.optimization_barrier((*kernel_call(
            functools.partial(tile_kernel, parts), "tiles",
            [SHAPE(((last - first) * SLOT_CAP, TILE, TILE), BF16) for _, (first, last) in parts],
            tile_ins, [VMEM] * len(parts), tile_scratch,
            flops=2 * tile_total * TILE**3 // 4, moved=2 << 20,
        )(ids, *lists, own, other, turned), turned))
        return values, turned

    (far_low, far_high), turned = terms(turned, (2, LOW), (2, HIGH))
    far_low, far_high = swap(far_low, "y", 1), swap(far_high, "y", 3)
    (one_low, other_high), turned = terms(turned, (1, LOW), (3, HIGH))
    one_low, other_high = swap(one_low, "y", 1), swap(other_high, "y", 3)
    (one_high, other_low, mine), turned = terms(turned, (1, HIGH), (3, LOW), (0, (0, NZ)))
    half = SHAPE(one_high.shape, BF16)
    one_high, other_low = kernel_call(
        passing_kernel, "passing", [half] * 2, [VMEM] * 4, [VMEM] * 2
    )(one_high, far_high, other_low, far_low)
    one_high, other_low = swap(one_high, "y", 1), swap(other_low, "y", 3)

    def parted(value):
        return value.reshape(-1, 2, SLOT_CAP, TILE, TILE)

    eight = SHAPE((NM, SLOT_CAP, TILE, TILE), BF16)
    keep, give = kernel_call(
        y_sum_kernel, "y_sum", [eight] * 2, [SMEM] + [VMEM] * 5, [VMEM] * 2
    )(ids, *map(parted, (mine, one_low, other_low, one_high, other_high)))

    keep, grads = lax.optimization_barrier((keep, grads))
    partner = swap(give, "p", 1)
    stay, give = kernel_call(
        contrib_kernel, "contribs", [SHAPE((tokens // 2, width), BF16)] * 2,
        [SMEM] * 3 + [ANY] * 2, [VMEM] * 2,
        [
            pltpu.SMEM((tile_total + 8,), jnp.int32),
            pltpu.VMEM(grads.shape, BF16),
            pltpu.VMEM(delta_all.shape, BF16),
            pltpu.SemaphoreType.DMA((2,)),
        ],
        moved=1 << 12,
    )(*lists, grads, delta_all)
    pairs = kernel_call(pair_sum_kernel, "pair_sum", eight, [VMEM] * 2 + [ANY], VMEM)(
        keep, partner, stay
    )
    arrived = exchange(pairs, "m")
    own_grad, squares = kernel_call(
        own_grad_kernel, "own_grad",
        [SHAPE((SLOT_CAP, TILE, TILE), F32), SHAPE((NY * NX * 2, 8, TILE), F32)],
        [SMEM, SMEM, VMEM], [VMEM] * 2,
    )(ids, owner_counts, arrived)


    rows = tokens // (2 * NX)
    _, give = lax.optimization_barrier((pairs, give))
    taken = swap(give, "core", 1)
    share, *others = kernel_call(
        core_sum_kernel, "core_sum", [SHAPE((rows, width), BF16)] * NX,
        [SMEM] + [VMEM] * 2, [VMEM] * NX, moved=1 << 12,
    )(ids, stay.reshape(NX, rows, width), taken.reshape(NX, rows, width))
    others = [swap(part, "x", bits + 1) for bits, part in enumerate(others)]
    squares, share, *others = lax.optimization_barrier((squares, share, *others))
    share = share.astype(F32)
    for part in others:
        share = share + part.astype(F32)
    gathered = lax.all_gather(share.astype(BF16), ("x", "core"), axis=0, tiled=True)
    input_grad = kernel_call(
        copy_kernel, "result", SHAPE((tokens, width), BF16), [ANY], ANY,
        [pltpu.VMEM((4, tokens // 4, width), BF16), pltpu.SemaphoreType.DMA((2, 4))],
        moved=4 << 20, vmem=63,
    )(gathered)

    squares = exchange(squares, ("y", "x", "core"))
    squares = kernel_call(relay_kernel, "relay", SHAPE((NZ, 8, TILE), F32), [VMEM], VMEM)(squares)
    squares = exchange(squares, Z)
    squares, input_grad = lax.optimization_barrier((squares, input_grad))
    count_all = float(NX * 2 * tile_total * TILE * TILE)

    def adam(*refs):
        adam_kernel(count_all, *refs)

    outs = kernel_call(
        adam, "adam", [SHAPE(delta_value.shape, F32)] * 3, [SMEM] * 2 + [VMEM] * 5, [VMEM] * 3
    )(ids, owner_counts, squares, own_grad, delta_value, moment_one, moment_two)
    return (input_grad, *outs)


def solution(mesh):
    grid = Mesh(mesh.devices.reshape(NY, NM, 2, NX, 2), ("y", "m", "p", "x", "core"))
    dp, tensor = ("y", "m", "p"), ("x", "core")
    tokens = P(dp, tensor)
    lists = P(tensor, None)
    slots = P(tensor, dp, None, None)
    return jax.shard_map(
        body,
        mesh=grid,
        in_specs=(tokens,) * 4 + (lists,) * 3 + (slots,) * 3,
        out_specs=(P(dp, None),) + (slots,) * 3,
        check_vma=False,
    )
```

```python
import functools

import jax
import jax.numpy as jnp
from jax import lax
from jax.experimental import pallas as pl
from jax.experimental.pallas import tpu as pltpu
from jax.sharding import Mesh, PartitionSpec as P

NY, NM, NX = 4, 8, 4
NZ = 2 * NM
Z = ("m", "p")
TILE = 128
SLOT_CAP = 2
LOW, HIGH = (0, NZ // 2), (NZ // 2, NZ)
BF16, F32 = jnp.bfloat16, jnp.float32
SMEM = pl.BlockSpec(memory_space=pltpu.SMEM)
VMEM = pl.BlockSpec(memory_space=pltpu.VMEM)
ANY = pl.BlockSpec(memory_space=pl.ANY)
SHAPE = jax.ShapeDtypeStruct


def kernel_call(
    kernel, name, outs, ins, out_specs, scratch=(), flops=0, moved=1 << 20, vmem=48
):
    return pl.pallas_call(
        kernel,
        out_shape=outs,
        in_specs=ins,
        out_specs=out_specs,
        scratch_shapes=scratch,
        compiler_params=pltpu.CompilerParams(vmem_limit_bytes=vmem * 1024 * 1024),
        cost_estimate=pl.CostEstimate(flops=flops, bytes_accessed=moved, transcendentals=0),
        name=name,
    )


def swap(value, axis, bits):
    return lax.ppermute(value, axis, [(i, i ^ bits) for i in range(lax.axis_size(axis))])


def exchange(value, axis):
    return lax.all_to_all(value, axis, split_axis=0, concat_axis=0, tiled=True)


def spread(value, axis):
    copies = jnp.broadcast_to(value[None], (lax.axis_size(axis),) + value.shape)
    return exchange(copies, axis)


def gate_kernel(ids_ref, gate_ref, up_ref, hidden_ref, grad_ref, turned_ref):
    blocks = 2 * NX
    rows = grad_ref.shape[1] // blocks
    core = ids_ref[3]
    for col in range(grad_ref.shape[0]):
        cut = slice(col * TILE, (col + 1) * TILE)
        gate = gate_ref[:, cut].astype(F32)
        sig = 1.0 / (1.0 + jnp.exp(-gate))
        value = (
            hidden_ref[:, cut].astype(F32)
            * up_ref[:, cut].astype(F32)
            * sig
            * (1.0 + gate * (1.0 - sig))
        )
        for block in range(blocks):
            place = pl.multiple_of((((block & 1) ^ core) * NX + (block >> 1)) * rows, rows)
            part = value[block * rows : (block + 1) * rows]
            grad_ref[col, pl.ds(place, rows)] = part.astype(BF16)
        turned_ref[col] = value.T.astype(BF16)


def load_features(own_ref, other_ref, features, sems, starts_ref, counts_ref):
    first = pltpu.make_async_copy(own_ref, features.at[0], sems.at[0])
    second = pltpu.make_async_copy(other_ref, features.at[1], sems.at[1])
    first.start()
    second.start()

    def owner_step(owner, start):
        starts_ref[owner] = start
        return start + counts_ref[0, owner]

    lax.fori_loop(0, counts_ref.shape[1], owner_step, 0)
    first.wait()
    second.wait()


def slot_products(group, owners, put, ids_ref, rows_ref, cols_ref, starts_ref, features, turned_ref):
    core = ids_ref[3]
    last = rows_ref.shape[1] - 1
    per_step = 4

    def step(index, carry):
        for part in range(per_step):
            owner = owners[0] + index * per_step + part
            start = starts_ref[group * NZ + owner]
            for rank in range(SLOT_CAP):
                k = jnp.minimum(start + rank, last)
                row = rows_ref[0, k]
                lane = pl.multiple_of((row & 7) * TILE, TILE)
                x = features[((row >> 3) & 1) ^ core, row >> 4, :, pl.ds(lane, TILE)]
                term = jnp.dot(turned_ref[cols_ref[0, k]], x, preferred_element_type=F32)
                put((index * per_step + part) * SLOT_CAP + rank, term)
        return carry

    lax.fori_loop(0, (owners[1] - owners[0]) // per_step, step, 0)


def tile_kernel(
    parts, ids_ref, rows_ref, cols_ref, counts_ref, own_ref, other_ref, turned_ref, *refs
):
    features, starts_ref, sems = refs[-3:]
    load_features(own_ref, other_ref, features, sems, starts_ref, counts_ref)
    for ref, (bits, owners, extra) in zip(refs[-3 - len(parts) :], parts):

        def put(slot, term, ref=ref, extra=extra):
            if extra is not None:
                term = term + refs[extra][slot].astype(F32)
            ref[slot] = term.astype(BF16)

        slot_products(
            ids_ref[0] ^ bits, owners, put,
            ids_ref, rows_ref, cols_ref, starts_ref, features, turned_ref,
        )


def y_sum_kernel(
    ids_ref, mine_ref, one_low_ref, other_low_ref, one_high_ref, other_high_ref,
    keep_ref, give_ref,
):
    parity = ids_ref[1] & 1
    half = NM // 2
    for m in range(NM):
        one, other = (one_low_ref, other_low_ref) if m < half else (one_high_ref, other_high_ref)

        def total(side):
            return (
                mine_ref[m, side].astype(F32)
                + one[m % half, side].astype(F32)
                + other[m % half, side].astype(F32)
            ).astype(BF16)

        keep_ref[m] = total(parity)
        give_ref[m] = total(1 - parity)


def pair_sum_kernel(keep_ref, taken_ref, _, out_ref):
    out_ref[...] = (keep_ref[...].astype(F32) + taken_ref[...].astype(F32)).astype(BF16)


def own_grad_kernel(ids_ref, counts_ref, arrived_ref, grad_ref, squares_ref):
    count = counts_ref[0, ids_ref[0] * NZ + ids_ref[1]]
    squares = jnp.zeros((TILE, TILE), F32)
    for rank in range(SLOT_CAP):
        total = arrived_ref[0, rank].astype(F32)
        for m in range(1, NM):
            total = total + arrived_ref[m, rank].astype(F32)
        total = jnp.where(rank < count, total, 0.0)
        grad_ref[rank] = total
        squares = squares + total * total
    squares_ref[...] = jnp.broadcast_to(jnp.sum(squares), squares_ref.shape)


def relay_kernel(arrived_ref, out_ref):
    total = jnp.sum(arrived_ref[...], axis=0, keepdims=True)
    out_ref[...] = jnp.broadcast_to(total, out_ref.shape)


def adam_kernel(
    count_all, ids_ref, counts_ref, arrived_ref, grad_ref, delta_ref, one_ref, two_ref,
    new_delta_ref, new_one_ref, new_two_ref,
):
    squares = jnp.sum(arrived_ref[...], axis=0)[0:1]
    factor = jnp.minimum(1.0, 1.0 / jnp.sqrt(squares / count_all + 1e-06))
    count = counts_ref[0, ids_ref[0] * NZ + ids_ref[1]]
    for rank in range(SLOT_CAP):
        live = rank < count
        clipped = factor * grad_ref[rank].T
        delta, one, two = delta_ref[0, rank], one_ref[0, rank], two_ref[0, rank]
        first = 0.9 * one + 0.1 * clipped
        second = 0.95 * two + 0.05 * clipped * clipped
        size = first / (1.0 - 0.9**10) / (jnp.sqrt(second / (1.0 - 0.95**10)) + 1e-08)
        updated = delta - 0.02 * (size + 0.1 * delta)
        new_delta_ref[0, rank] = jnp.where(live, updated, delta)
        new_one_ref[0, rank] = jnp.where(live, first, one)
        new_two_ref[0, rank] = jnp.where(live, second, two)


def turn_kernel(delta_ref, out_ref):
    for rank in range(SLOT_CAP):
        out_ref[rank] = delta_ref[0, rank].T.astype(BF16)


def contrib_kernel(
    rows_ref, cols_ref, counts_ref, grads_ref, deltas_ref, stay_ref, give_ref,
    places_ref, grad_ref, delta_ref, sems,
):
    loads = [
        pltpu.make_async_copy(deltas_ref, delta_ref, sems.at[0]),
        pltpu.make_async_copy(grads_ref, grad_ref, sems.at[1]),
    ]
    for load in loads:
        load.start()
    stay_ref[...] = jnp.zeros_like(stay_ref)
    give_ref[...] = jnp.zeros_like(give_ref)
    half = stay_ref.shape[0]

    def owner_step(owner, start):
        place = ((owner & (NZ - 1)) * NY + owner // NZ) * SLOT_CAP
        places_ref[start] = place
        places_ref[start + 1] = place + 1
        return start + counts_ref[0, owner]

    lax.fori_loop(0, counts_ref.shape[1], owner_step, 0)
    for load in loads:
        load.wait()
    per_step = 28

    def step(index, carry):
        last, total = carry
        for part in range(per_step):
            k = index * per_step + part
            row = rows_ref[0, k]
            product = jnp.dot(
                grad_ref[cols_ref[0, k]], delta_ref[places_ref[k]], preferred_element_type=F32
            )
            total = jnp.where(row == last, total, 0.0) + product
            lane = pl.multiple_of(row * TILE, TILE)
            stay_ref[:, pl.ds(lane, TILE)] = total[:half].astype(BF16)
            give_ref[:, pl.ds(lane, TILE)] = total[half:].astype(BF16)
            last = row
        return last, total

    lax.fori_loop(
        0, rows_ref.shape[1] // per_step, step,
        (jnp.int32(-1), jnp.zeros((TILE, TILE), F32)),
    )


def core_sum_kernel(ids_ref, stay_ref, taken_ref, *out_refs):
    for bits, ref in enumerate(out_refs):
        at = ids_ref[2] ^ bits
        ref[...] = (stay_ref[at].astype(F32) + taken_ref[at].astype(F32)).astype(BF16)


def copy_kernel(in_ref, out_ref, held, sems):
    chunks = held.shape[0]
    rows = in_ref.shape[0] // chunks

    def part(ref, chunk):
        return ref.at[pl.ds(chunk * rows, rows)]

    loads = [
        pltpu.make_async_copy(part(in_ref, i), held.at[i], sems.at[0, i]) for i in range(chunks)
    ]
    stores = [
        pltpu.make_async_copy(held.at[i], part(out_ref, i), sems.at[1, i]) for i in range(chunks)
    ]
    for load in loads:
        load.start()
    for load, store in zip(loads, stores):
        load.wait()
        store.start()
    for store in stores:
        store.wait()


def body(
    features, gate_pre, up_pre, hidden_grad, tile_rows, tile_cols, owner_counts,
    delta_value, moment_one, moment_two,
):
    ids = jnp.stack([lax.axis_index(name) for name in ("y", Z, "x", "core")]).astype(jnp.int32)
    tokens, hidden = gate_pre.shape
    shard_width = features.shape[1]
    width = shard_width * NX * 2
    tile_total = tile_rows.shape[1]
    lists = (tile_rows, tile_cols, owner_counts)

    own = spread(features, "x")
    other = swap(own, "core", 1)

    delta_half = kernel_call(
        turn_kernel, "turn", SHAPE(delta_value.shape[1:], BF16), [VMEM], VMEM
    )(delta_value)
    delta_y = spread(delta_half, "y").reshape(NY * SLOT_CAP, TILE, TILE)
    delta_all = lax.all_gather(delta_y, Z, axis=0, tiled=True)

    grads, turned = kernel_call(
        gate_kernel, "gate", [SHAPE((hidden // TILE, tokens, TILE), BF16)] * 2,
        [SMEM] + [VMEM] * 3, [VMEM] * 2, flops=tokens * hidden * 12, moved=tokens * hidden * 10,
    )(ids, gate_pre, up_pre, hidden_grad)

    tile_ins = [SMEM] * 4 + [ANY, ANY, VMEM]
    tile_scratch = [
        pltpu.VMEM((2, NX, tokens, shard_width), BF16),
        pltpu.SMEM((owner_counts.shape[1],), jnp.int32),
        pltpu.SemaphoreType.DMA((2,)),
    ]

    def terms(parts, *extras):
        return kernel_call(
            functools.partial(tile_kernel, parts), "tiles",
            [SHAPE(((last - first) * SLOT_CAP, TILE, TILE), BF16) for _, (first, last), _ in parts],
            tile_ins + [VMEM] * len(extras), [VMEM] * len(parts), tile_scratch,
            flops=2 * tile_total * TILE**3 // 4, moved=2 << 20,
        )(ids, *lists, own, other, turned, *extras)

    far_low, far_high, one_low, other_high = terms(
        ((2, LOW, None), (2, HIGH, None), (1, LOW, None), (3, HIGH, None))
    )
    far_low, far_high = swap(far_low, "y", 1), swap(far_high, "y", 3)
    one_low, other_high = swap(one_low, "y", 1), swap(other_high, "y", 3)
    one_high, other_low, mine = terms(
        ((1, HIGH, 0), (3, LOW, 1), (0, (0, NZ), None)), far_high, far_low
    )
    one_high, other_low = swap(one_high, "y", 1), swap(other_low, "y", 3)

    def parted(value):
        return value.reshape(-1, 2, SLOT_CAP, TILE, TILE)

    eight = SHAPE((NM, SLOT_CAP, TILE, TILE), BF16)
    keep, give = kernel_call(
        y_sum_kernel, "y_sum", [eight] * 2, [SMEM] + [VMEM] * 5, [VMEM] * 2
    )(ids, *map(parted, (mine, one_low, other_low, one_high, other_high)))

    keep, grads = lax.optimization_barrier((keep, grads))
    partner = swap(give, "p", 1)
    stay, give = kernel_call(
        contrib_kernel, "contribs", [SHAPE((tokens // 2, width), BF16)] * 2,
        [SMEM] * 3 + [ANY] * 2, [VMEM] * 2,
        [
            pltpu.SMEM((tile_total + 8,), jnp.int32),
            pltpu.VMEM(grads.shape, BF16),
            pltpu.VMEM(delta_all.shape, BF16),
            pltpu.SemaphoreType.DMA((2,)),
        ],
        moved=1 << 12,
    )(*lists, grads, delta_all)
    pairs = kernel_call(pair_sum_kernel, "pair_sum", eight, [VMEM] * 2 + [ANY], VMEM)(
        keep, partner, stay
    )
    arrived = exchange(pairs, "m")
    own_grad, squares = kernel_call(
        own_grad_kernel, "own_grad",
        [SHAPE((SLOT_CAP, TILE, TILE), F32), SHAPE((NY * NX * 2, 8, TILE), F32)],
        [SMEM, SMEM, VMEM], [VMEM] * 2,
    )(ids, owner_counts, arrived)


    rows = tokens // (2 * NX)
    _, give = lax.optimization_barrier((pairs, give))
    taken = swap(give, "core", 1)
    share, *others = kernel_call(
        core_sum_kernel, "core_sum", [SHAPE((rows, width), BF16)] * NX,
        [SMEM] + [VMEM] * 2, [VMEM] * NX, moved=1 << 12,
    )(ids, stay.reshape(NX, rows, width), taken.reshape(NX, rows, width))
    others = [swap(others[bits - 1], "x", bits) for bits in (2, 1, 3)]
    squares, share, *others = lax.optimization_barrier((squares, share, *others))
    share = share.astype(F32)
    for part in others:
        share = share + part.astype(F32)
    gathered = lax.all_gather(share.astype(BF16), ("x", "core"), axis=0, tiled=True)
    input_grad = kernel_call(
        copy_kernel, "result", SHAPE((tokens, width), BF16), [ANY], ANY,
        [pltpu.VMEM((4, tokens // 4, width), BF16), pltpu.SemaphoreType.DMA((2, 4))],
        moved=4 << 20, vmem=63,
    )(gathered)

    squares = exchange(squares, ("y", "x", "core"))
    squares = kernel_call(relay_kernel, "relay", SHAPE((NZ, 8, TILE), F32), [VMEM], VMEM)(squares)
    squares = exchange(squares, Z)
    squares, input_grad = lax.optimization_barrier((squares, input_grad))
    count_all = float(NX * 2 * tile_total * TILE * TILE)

    def adam(*refs):
        adam_kernel(count_all, *refs)

    outs = kernel_call(
        adam, "adam", [SHAPE(delta_value.shape, F32)] * 3, [SMEM] * 2 + [VMEM] * 5, [VMEM] * 3
    )(ids, owner_counts, squares, own_grad, delta_value, moment_one, moment_two)
    return (input_grad, *outs)


def solution(mesh):
    grid = Mesh(mesh.devices.reshape(NY, NM, 2, NX, 2), ("y", "m", "p", "x", "core"))
    dp, tensor = ("y", "m", "p"), ("x", "core")
    tokens = P(dp, tensor)
    lists = P(tensor, None)
    slots = P(tensor, dp, None, None)
    return jax.shard_map(
        body,
        mesh=grid,
        in_specs=(tokens,) * 4 + (lists,) * 3 + (slots,) * 3,
        out_specs=(P(dp, None),) + (slots,) * 3,
        check_vma=False,
    )
```

```python
import functools

import jax
import jax.numpy as jnp
from jax import lax
from jax.experimental import pallas as pl
from jax.experimental.pallas import tpu as pltpu
from jax.sharding import Mesh, PartitionSpec as P

NY, NM, NX = 4, 8, 4
NZ = 2 * NM
Z = ("m", "p")
TILE = 128
SLOT_CAP = 2
LOW, HIGH = (0, NZ // 2), (NZ // 2, NZ)
BF16, F32 = jnp.bfloat16, jnp.float32
SMEM = pl.BlockSpec(memory_space=pltpu.SMEM)
VMEM = pl.BlockSpec(memory_space=pltpu.VMEM)
ANY = pl.BlockSpec(memory_space=pl.ANY)
SHAPE = jax.ShapeDtypeStruct


def kernel_call(
    kernel, name, outs, ins, out_specs, scratch=(), flops=0, moved=1 << 20, vmem=16
):
    return pl.pallas_call(
        kernel,
        out_shape=outs,
        in_specs=ins,
        out_specs=out_specs,
        scratch_shapes=scratch,
        compiler_params=pltpu.CompilerParams(vmem_limit_bytes=vmem * 1024 * 1024),
        cost_estimate=pl.CostEstimate(flops=flops, bytes_accessed=moved, transcendentals=0),
        name=name,
    )


def swap(value, axis, bits):
    return lax.ppermute(value, axis, [(i, i ^ bits) for i in range(lax.axis_size(axis))])


def exchange(value, axis):
    return lax.all_to_all(value, axis, split_axis=0, concat_axis=0, tiled=True)


def spread(value, axis):
    copies = jnp.broadcast_to(value[None], (lax.axis_size(axis),) + value.shape)
    return exchange(copies, axis)


def gate_kernel(ids_ref, gate_ref, up_ref, hidden_ref, grad_ref, turned_ref):
    blocks = 2 * NX
    rows = grad_ref.shape[1] // blocks
    core = ids_ref[3]
    for col in range(grad_ref.shape[0]):
        cut = slice(col * TILE, (col + 1) * TILE)
        gate = gate_ref[:, cut].astype(F32)
        sig = 1.0 / (1.0 + jnp.exp(-gate))
        value = (
            hidden_ref[:, cut].astype(F32)
            * up_ref[:, cut].astype(F32)
            * sig
            * (1.0 + gate * (1.0 - sig))
        )
        for block in range(blocks):
            place = pl.multiple_of((((block & 1) ^ core) * NX + (block >> 1)) * rows, rows)
            part = value[block * rows : (block + 1) * rows]
            grad_ref[col, pl.ds(place, rows)] = part.astype(BF16)
        turned_ref[col] = value.T.astype(BF16)


def load_features(own_ref, other_ref, features, sems, starts_ref, counts_ref):
    first = pltpu.make_async_copy(own_ref, features.at[0], sems.at[0])
    second = pltpu.make_async_copy(other_ref, features.at[1], sems.at[1])
    first.start()
    second.start()

    def owner_step(owner, start):
        starts_ref[owner] = start
        return start + counts_ref[0, owner]

    lax.fori_loop(0, counts_ref.shape[1], owner_step, 0)
    first.wait()
    second.wait()


def slot_products(group, owners, put, ids_ref, rows_ref, cols_ref, starts_ref, features, turned_ref):
    core = ids_ref[3]
    last = rows_ref.shape[1] - 1
    per_step = 4

    def step(index, carry):
        for part in range(per_step):
            owner = owners[0] + index * per_step + part
            start = starts_ref[group * NZ + owner]
            for rank in range(SLOT_CAP):
                k = jnp.minimum(start + rank, last)
                row = rows_ref[0, k]
                lane = pl.multiple_of((row & 7) * TILE, TILE)
                x = features[((row >> 3) & 1) ^ core, row >> 4, :, pl.ds(lane, TILE)]
                term = jnp.dot(turned_ref[cols_ref[0, k]], x, preferred_element_type=F32)
                put((index * per_step + part) * SLOT_CAP + rank, term)
        return carry

    lax.fori_loop(0, (owners[1] - owners[0]) // per_step, step, 0)


def tile_kernel(
    parts, ids_ref, rows_ref, cols_ref, counts_ref, own_ref, other_ref, turned_ref, *refs
):
    features, starts_ref, sems = refs[-3:]
    load_features(own_ref, other_ref, features, sems, starts_ref, counts_ref)
    for ref, (bits, owners, extra) in zip(refs[-3 - len(parts) :], parts):

        def put(slot, term, ref=ref, extra=extra):
            if extra is not None:
                term = term + refs[extra][slot].astype(F32)
            ref[slot] = term.astype(BF16)

        slot_products(
            ids_ref[0] ^ bits, owners, put,
            ids_ref, rows_ref, cols_ref, starts_ref, features, turned_ref,
        )


def y_sum_kernel(
    ids_ref, mine_ref, one_low_ref, other_low_ref, one_high_ref, other_high_ref,
    keep_ref, give_ref,
):
    parity = ids_ref[1] & 1
    half = NM // 2
    for m in range(NM):
        one, other = (one_low_ref, other_low_ref) if m < half else (one_high_ref, other_high_ref)

        def total(side):
            return (
                mine_ref[m, side].astype(F32)
                + one[m % half, side].astype(F32)
                + other[m % half, side].astype(F32)
            ).astype(BF16)

        keep_ref[m] = total(parity)
        give_ref[m] = total(1 - parity)


def pair_sum_kernel(keep_ref, taken_ref, _, out_ref):
    out_ref[...] = (keep_ref[...].astype(F32) + taken_ref[...].astype(F32)).astype(BF16)


def own_grad_kernel(ids_ref, counts_ref, arrived_ref, grad_ref, squares_ref):
    count = counts_ref[0, ids_ref[0] * NZ + ids_ref[1]]
    squares = jnp.zeros((TILE, TILE), F32)
    for rank in range(SLOT_CAP):
        total = arrived_ref[0, rank].astype(F32)
        for m in range(1, NM):
            total = total + arrived_ref[m, rank].astype(F32)
        total = jnp.where(rank < count, total, 0.0)
        grad_ref[rank] = total
        squares = squares + total * total
    squares_ref[...] = jnp.broadcast_to(jnp.sum(squares), squares_ref.shape)


def relay_kernel(arrived_ref, out_ref):
    total = jnp.sum(arrived_ref[...], axis=0, keepdims=True)
    out_ref[...] = jnp.broadcast_to(total, out_ref.shape)


def adam_kernel(
    count_all, ids_ref, counts_ref, arrived_ref, grad_ref, delta_ref, one_ref, two_ref,
    new_delta_ref, new_one_ref, new_two_ref,
):
    squares = jnp.sum(arrived_ref[...], axis=0)[0:1]
    factor = jnp.minimum(1.0, 1.0 / jnp.sqrt(squares / count_all + 1e-06))
    count = counts_ref[0, ids_ref[0] * NZ + ids_ref[1]]
    for rank in range(SLOT_CAP):
        live = rank < count
        clipped = factor * grad_ref[rank].T
        delta, one, two = delta_ref[0, rank], one_ref[0, rank], two_ref[0, rank]
        first = 0.9 * one + 0.1 * clipped
        second = 0.95 * two + 0.05 * clipped * clipped
        size = first / (1.0 - 0.9**10) / (jnp.sqrt(second / (1.0 - 0.95**10)) + 1e-08)
        updated = delta - 0.02 * (size + 0.1 * delta)
        new_delta_ref[0, rank] = jnp.where(live, updated, delta)
        new_one_ref[0, rank] = jnp.where(live, first, one)
        new_two_ref[0, rank] = jnp.where(live, second, two)


def turn_kernel(delta_ref, out_ref, held, sem):
    load = pltpu.make_async_copy(delta_ref, held, sem)
    load.start()
    load.wait()
    for rank in range(SLOT_CAP):
        turned = held[0, rank].T.astype(BF16)
        for y in range(NY):
            out_ref[y, rank] = turned


def contrib_kernel(
    rows_ref, cols_ref, counts_ref, grads_ref, deltas_ref, _, stay_ref, give_ref, token_ref,
    places_ref, grad_ref, delta_ref, sems,
):
    loads = [
        pltpu.make_async_copy(deltas_ref, delta_ref, sems.at[0]),
        pltpu.make_async_copy(grads_ref, grad_ref, sems.at[1]),
    ]
    for load in loads:
        load.start()
    stay_ref[...] = jnp.zeros_like(stay_ref)
    give_ref[...] = jnp.zeros_like(give_ref)
    token_ref[...] = jnp.zeros_like(token_ref)
    half = stay_ref.shape[0]

    def owner_step(owner, start):
        place = ((owner & (NZ - 1)) * NY + owner // NZ) * SLOT_CAP
        places_ref[start] = place
        places_ref[start + 1] = place + 1
        return start + counts_ref[0, owner]

    lax.fori_loop(0, counts_ref.shape[1], owner_step, 0)
    for load in loads:
        load.wait()
    per_step = 28

    def step(index, carry):
        last, total = carry
        for part in range(per_step):
            k = index * per_step + part
            row = rows_ref[0, k]
            product = jnp.dot(
                grad_ref[cols_ref[0, k]], delta_ref[places_ref[k]], preferred_element_type=F32
            )
            total = jnp.where(row == last, total, 0.0) + product
            lane = pl.multiple_of(row * TILE, TILE)
            stay_ref[:, pl.ds(lane, TILE)] = total[:half].astype(BF16)
            give_ref[:, pl.ds(lane, TILE)] = total[half:].astype(BF16)
            last = row
        return last, total

    lax.fori_loop(
        0, rows_ref.shape[1] // per_step, step,
        (jnp.int32(-1), jnp.zeros((TILE, TILE), F32)),
    )


def core_sum_kernel(ids_ref, stay_ref, taken_ref, *out_refs):
    for bits, ref in enumerate(out_refs):
        at = ids_ref[2] ^ bits
        ref[...] = (stay_ref[at].astype(F32) + taken_ref[at].astype(F32)).astype(BF16)


def copy_kernel(in_ref, out_ref, held, sems):
    chunks = held.shape[0]
    rows = in_ref.shape[0] // chunks

    def part(ref, chunk):
        return ref.at[pl.ds(chunk * rows, rows)]

    loads = [
        pltpu.make_async_copy(part(in_ref, i), held.at[i], sems.at[0, i]) for i in range(chunks)
    ]
    stores = [
        pltpu.make_async_copy(held.at[i], part(out_ref, i), sems.at[1, i]) for i in range(chunks)
    ]
    for load in loads:
        load.start()
    for load, store in zip(loads, stores):
        load.wait()
        store.start()
    for store in stores:
        store.wait()


def body(
    features, gate_pre, up_pre, hidden_grad, tile_rows, tile_cols, owner_counts,
    delta_value, moment_one, moment_two,
):
    ids = jnp.stack([lax.axis_index(name) for name in ("y", Z, "x", "core")]).astype(jnp.int32)
    tokens, hidden = gate_pre.shape
    shard_width = features.shape[1]
    width = shard_width * NX * 2
    tile_total = tile_rows.shape[1]
    lists = (tile_rows, tile_cols, owner_counts)

    own = spread(features, "x")
    other = swap(own, "core", 1)

    copies = kernel_call(
        turn_kernel, "turn", SHAPE((NY,) + delta_value.shape[1:], BF16), [ANY], VMEM,
        [pltpu.VMEM(delta_value.shape, F32), pltpu.SemaphoreType.DMA], vmem=63,
    )(delta_value)
    delta_y = exchange(copies, "y").reshape(NY * SLOT_CAP, TILE, TILE)
    delta_all = lax.all_gather(delta_y, Z, axis=0, tiled=True)

    grads, turned = kernel_call(
        gate_kernel, "gate", [SHAPE((hidden // TILE, tokens, TILE), BF16)] * 2,
        [SMEM] + [VMEM] * 3, [VMEM] * 2, flops=tokens * hidden * 12, moved=tokens * hidden * 10,
    )(ids, gate_pre, up_pre, hidden_grad)

    tile_ins = [SMEM] * 4 + [ANY, ANY, VMEM]
    tile_scratch = [
        pltpu.VMEM((2, NX, tokens, shard_width), BF16),
        pltpu.SMEM((owner_counts.shape[1],), jnp.int32),
        pltpu.SemaphoreType.DMA((2,)),
    ]

    def terms(parts, *extras):
        return kernel_call(
            functools.partial(tile_kernel, parts), "tiles",
            [SHAPE(((last - first) * SLOT_CAP, TILE, TILE), BF16) for _, (first, last), _ in parts],
            tile_ins + [VMEM] * len(extras), [VMEM] * len(parts), tile_scratch,
            flops=2 * tile_total * TILE**3 // 4, moved=2 << 20,
        )(ids, *lists, own, other, turned, *extras)

    far_low, far_high, one_low, other_high = terms(
        ((2, LOW, None), (2, HIGH, None), (1, LOW, None), (3, HIGH, None))
    )
    far_low, far_high = swap(far_low, "y", 1), swap(far_high, "y", 3)
    one_low, other_high = swap(one_low, "y", 1), swap(other_high, "y", 3)
    one_high, other_low, mine = terms(
        ((1, HIGH, 0), (3, LOW, 1), (0, (0, NZ), None)), far_high, far_low
    )
    one_high, other_low = swap(one_high, "y", 1), swap(other_low, "y", 3)

    def parted(value):
        return value.reshape(-1, 2, SLOT_CAP, TILE, TILE)

    eight = SHAPE((NM, SLOT_CAP, TILE, TILE), BF16)
    keep, give = kernel_call(
        y_sum_kernel, "y_sum", [eight] * 2, [SMEM] + [VMEM] * 5, [VMEM] * 2
    )(ids, *map(parted, (mine, one_low, other_low, one_high, other_high)))

    partner = swap(give, "p", 1)
    stay, give, token = kernel_call(
        contrib_kernel, "contribs",
        [SHAPE((tokens // 2, width), BF16)] * 2 + [SHAPE((8, TILE), F32)],
        [SMEM] * 3 + [ANY] * 3, [VMEM] * 3,
        [
            pltpu.SMEM((tile_total + 8,), jnp.int32),
            pltpu.VMEM(grads.shape, BF16),
            pltpu.VMEM(delta_all.shape, BF16),
            pltpu.SemaphoreType.DMA((2,)),
        ],
        moved=1 << 12, vmem=48,
    )(*lists, grads, delta_all, keep)
    pairs = kernel_call(pair_sum_kernel, "pair_sum", eight, [VMEM] * 3, VMEM)(
        keep, partner, token
    )
    arrived = exchange(pairs, "m")
    own_grad, squares = kernel_call(
        own_grad_kernel, "own_grad",
        [SHAPE((SLOT_CAP, TILE, TILE), F32), SHAPE((NY * NX * 2, 8, TILE), F32)],
        [SMEM, SMEM, VMEM], [VMEM] * 2,
    )(ids, owner_counts, arrived)


    rows = tokens // (2 * NX)
    _, give = lax.optimization_barrier((pairs, give))
    taken = swap(give, "core", 1)
    share, *others = kernel_call(
        core_sum_kernel, "core_sum", [SHAPE((rows, width), BF16)] * NX,
        [SMEM] + [VMEM] * 2, [VMEM] * NX, moved=1 << 12,
    )(ids, stay.reshape(NX, rows, width), taken.reshape(NX, rows, width))
    others = [swap(others[bits - 1], "x", bits) for bits in (2, 1, 3)]
    squares, share, *others = lax.optimization_barrier((squares, share, *others))
    share = share.astype(F32)
    for part in others:
        share = share + part.astype(F32)
    gathered = lax.all_gather(share.astype(BF16), ("x", "core"), axis=0, tiled=True)
    input_grad = kernel_call(
        copy_kernel, "result", SHAPE((tokens, width), BF16), [ANY], ANY,
        [pltpu.VMEM((4, tokens // 4, width), BF16), pltpu.SemaphoreType.DMA((2, 4))],
        moved=4 << 20, vmem=63,
    )(gathered)

    squares = exchange(squares, ("y", "x", "core"))
    squares = kernel_call(relay_kernel, "relay", SHAPE((NZ, 8, TILE), F32), [VMEM], VMEM)(squares)
    squares = exchange(squares, Z)
    squares, input_grad = lax.optimization_barrier((squares, input_grad))
    count_all = float(NX * 2 * tile_total * TILE * TILE)

    def adam(*refs):
        adam_kernel(count_all, *refs)

    outs = kernel_call(
        adam, "adam", [SHAPE(delta_value.shape, F32)] * 3, [SMEM] * 2 + [VMEM] * 5, [VMEM] * 3
    )(ids, owner_counts, squares, own_grad, delta_value, moment_one, moment_two)
    return (input_grad, *outs)


def solution(mesh):
    grid = Mesh(mesh.devices.reshape(NY, NM, 2, NX, 2), ("y", "m", "p", "x", "core"))
    dp, tensor = ("y", "m", "p"), ("x", "core")
    tokens = P(dp, tensor)
    lists = P(tensor, None)
    slots = P(tensor, dp, None, None)
    return jax.shard_map(
        body,
        mesh=grid,
        in_specs=(tokens,) * 4 + (lists,) * 3 + (slots,) * 3,
        out_specs=(P(dp, None),) + (slots,) * 3,
        check_vma=False,
    )
```

```python
import functools

import jax
import jax.numpy as jnp
from jax import lax
from jax.experimental import pallas as pl
from jax.experimental.pallas import tpu as pltpu
from jax.sharding import Mesh, PartitionSpec as P

NY, NM, NX = 4, 8, 4
NZ = 2 * NM
Z = ("m", "p")
TILE = 128
SLOT_CAP = 2
LOW, HIGH = (0, NZ // 2), (NZ // 2, NZ)
BF16, F32 = jnp.bfloat16, jnp.float32
SMEM = pl.BlockSpec(memory_space=pltpu.SMEM)
VMEM = pl.BlockSpec(memory_space=pltpu.VMEM)
ANY = pl.BlockSpec(memory_space=pl.ANY)
SHAPE = jax.ShapeDtypeStruct


def kernel_call(
    kernel, name, outs, ins, out_specs, scratch=(), flops=0, moved=1 << 20, vmem=16
):
    return pl.pallas_call(
        kernel,
        out_shape=outs,
        in_specs=ins,
        out_specs=out_specs,
        scratch_shapes=scratch,
        compiler_params=pltpu.CompilerParams(vmem_limit_bytes=vmem * 1024 * 1024),
        cost_estimate=pl.CostEstimate(flops=flops, bytes_accessed=moved, transcendentals=0),
        name=name,
    )


def swap(value, axis, bits):
    return lax.ppermute(value, axis, [(i, i ^ bits) for i in range(lax.axis_size(axis))])


def exchange(value, axis):
    return lax.all_to_all(value, axis, split_axis=0, concat_axis=0, tiled=True)


def spread(value, axis):
    copies = jnp.broadcast_to(value[None], (lax.axis_size(axis),) + value.shape)
    return exchange(copies, axis)


def gate_kernel(ids_ref, gate_ref, up_ref, hidden_ref, grad_ref, turned_ref):
    blocks = 2 * NX
    rows = grad_ref.shape[1] // blocks
    core = ids_ref[3]
    for col in range(grad_ref.shape[0]):
        cut = slice(col * TILE, (col + 1) * TILE)
        gate = gate_ref[:, cut].astype(F32)
        sig = 1.0 / (1.0 + jnp.exp(-gate))
        value = (
            hidden_ref[:, cut].astype(F32)
            * up_ref[:, cut].astype(F32)
            * sig
            * (1.0 + gate * (1.0 - sig))
        )
        for block in range(blocks):
            place = pl.multiple_of((((block & 1) ^ core) * NX + (block >> 1)) * rows, rows)
            part = value[block * rows : (block + 1) * rows]
            grad_ref[col, pl.ds(place, rows)] = part.astype(BF16)
        turned_ref[col] = value.T.astype(BF16)


def load_features(own_ref, other_ref, features, sems, starts_ref, counts_ref):
    first = pltpu.make_async_copy(own_ref, features.at[0], sems.at[0])
    second = pltpu.make_async_copy(other_ref, features.at[1], sems.at[1])
    first.start()
    second.start()

    def owner_step(owner, start):
        starts_ref[owner] = start
        return start + counts_ref[0, owner]

    lax.fori_loop(0, counts_ref.shape[1], owner_step, 0)
    first.wait()
    second.wait()


def slot_products(group, owners, put, ids_ref, rows_ref, cols_ref, starts_ref, features, turned_ref):
    core = ids_ref[3]
    last = rows_ref.shape[1] - 1
    per_step = 4

    def step(index, carry):
        for part in range(per_step):
            owner = owners[0] + index * per_step + part
            start = starts_ref[group * NZ + owner]
            for rank in range(SLOT_CAP):
                k = jnp.minimum(start + rank, last)
                row = rows_ref[0, k]
                lane = pl.multiple_of((row & 7) * TILE, TILE)
                x = features[((row >> 3) & 1) ^ core, row >> 4, :, pl.ds(lane, TILE)]
                term = jnp.dot(turned_ref[cols_ref[0, k]], x, preferred_element_type=F32)
                put((index * per_step + part) * SLOT_CAP + rank, term)
        return carry

    lax.fori_loop(0, (owners[1] - owners[0]) // per_step, step, 0)


def tile_kernel(
    parts, ids_ref, rows_ref, cols_ref, counts_ref, own_ref, other_ref, turned_ref, *refs
):
    features, starts_ref, sems = refs[-3:]
    load_features(own_ref, other_ref, features, sems, starts_ref, counts_ref)
    for ref, (bits, owners, extra) in zip(refs[-3 - len(parts) :], parts):

        def put(slot, term, ref=ref, extra=extra):
            if extra is not None:
                term = term + refs[extra][slot].astype(F32)
            ref[slot] = term.astype(BF16)

        slot_products(
            ids_ref[0] ^ bits, owners, put,
            ids_ref, rows_ref, cols_ref, starts_ref, features, turned_ref,
        )


def y_sum_kernel(
    ids_ref, mine_ref, one_low_ref, other_low_ref, one_high_ref, other_high_ref,
    keep_ref, give_ref,
):
    parity = ids_ref[1] & 1
    half = NM // 2
    for m in range(NM):
        one, other = (one_low_ref, other_low_ref) if m < half else (one_high_ref, other_high_ref)

        def total(side):
            return (
                mine_ref[m, side].astype(F32)
                + one[m % half, side].astype(F32)
                + other[m % half, side].astype(F32)
            ).astype(BF16)

        keep_ref[m] = total(parity)
        give_ref[m] = total(1 - parity)


def pair_sum_kernel(keep_ref, taken_ref, _, out_ref):
    out_ref[...] = (keep_ref[...].astype(F32) + taken_ref[...].astype(F32)).astype(BF16)


def own_grad_kernel(ids_ref, counts_ref, arrived_ref, grad_ref, squares_ref):
    count = counts_ref[0, ids_ref[0] * NZ + ids_ref[1]]
    squares = jnp.zeros((TILE, TILE), F32)
    for rank in range(SLOT_CAP):
        total = arrived_ref[0, rank].astype(F32)
        for m in range(1, NM):
            total = total + arrived_ref[m, rank].astype(F32)
        total = jnp.where(rank < count, total, 0.0)
        grad_ref[rank] = total
        squares = squares + total * total
    squares_ref[...] = jnp.broadcast_to(jnp.sum(squares), squares_ref.shape)


def relay_kernel(arrived_ref, out_ref):
    total = jnp.sum(arrived_ref[...], axis=0, keepdims=True)
    out_ref[...] = jnp.broadcast_to(total, out_ref.shape)


def adam_kernel(
    count_all, ids_ref, counts_ref, arrived_ref, grad_ref, delta_ref, one_ref, two_ref,
    new_delta_ref, new_one_ref, new_two_ref,
):
    squares = jnp.sum(arrived_ref[...], axis=0)[0:1]
    factor = jnp.minimum(1.0, 1.0 / jnp.sqrt(squares / count_all + 1e-06))
    count = counts_ref[0, ids_ref[0] * NZ + ids_ref[1]]
    for rank in range(SLOT_CAP):
        live = rank < count
        clipped = factor * grad_ref[rank].T
        delta, one, two = delta_ref[0, rank], one_ref[0, rank], two_ref[0, rank]
        first = 0.9 * one + 0.1 * clipped
        second = 0.95 * two + 0.05 * clipped * clipped
        size = first / (1.0 - 0.9**10) / (jnp.sqrt(second / (1.0 - 0.95**10)) + 1e-08)
        updated = delta - 0.02 * (size + 0.1 * delta)
        new_delta_ref[0, rank] = jnp.where(live, updated, delta)
        new_one_ref[0, rank] = jnp.where(live, first, one)
        new_two_ref[0, rank] = jnp.where(live, second, two)


def turn_kernel(delta_ref, out_ref):
    for rank in range(SLOT_CAP):
        out_ref[rank] = delta_ref[0, rank].T.astype(BF16)


def contrib_kernel(
    rows_ref, cols_ref, counts_ref, grads_ref, deltas_ref, _, stay_ref, give_ref, token_ref,
    places_ref, grad_ref, delta_ref, sems,
):
    loads = [
        pltpu.make_async_copy(deltas_ref, delta_ref, sems.at[0]),
        pltpu.make_async_copy(grads_ref, grad_ref, sems.at[1]),
    ]
    for load in loads:
        load.start()
    stay_ref[...] = jnp.zeros_like(stay_ref)
    give_ref[...] = jnp.zeros_like(give_ref)
    token_ref[...] = jnp.zeros_like(token_ref)
    half = stay_ref.shape[0]

    def owner_step(owner, start):
        place = ((owner & (NZ - 1)) * NY + owner // NZ) * SLOT_CAP
        places_ref[start] = place
        places_ref[start + 1] = place + 1
        return start + counts_ref[0, owner]

    lax.fori_loop(0, counts_ref.shape[1], owner_step, 0)
    for load in loads:
        load.wait()
    per_step = 28

    def step(index, carry):
        last, total = carry
        for part in range(per_step):
            k = index * per_step + part
            row = rows_ref[0, k]
            product = jnp.dot(
                grad_ref[cols_ref[0, k]], delta_ref[places_ref[k]], preferred_element_type=F32
            )
            total = jnp.where(row == last, total, 0.0) + product
            lane = pl.multiple_of(row * TILE, TILE)
            stay_ref[:, pl.ds(lane, TILE)] = total[:half].astype(BF16)
            give_ref[:, pl.ds(lane, TILE)] = total[half:].astype(BF16)
            last = row
        return last, total

    lax.fori_loop(
        0, rows_ref.shape[1] // per_step, step,
        (jnp.int32(-1), jnp.zeros((TILE, TILE), F32)),
    )


def core_sum_kernel(ids_ref, stay_ref, taken_ref, *out_refs):
    for bits, ref in enumerate(out_refs):
        at = ids_ref[2] ^ bits
        ref[...] = (stay_ref[at].astype(F32) + taken_ref[at].astype(F32)).astype(BF16)


def copy_kernel(in_ref, out_ref, held, sems):
    chunks = held.shape[0]
    rows = in_ref.shape[0] // chunks

    def part(ref, chunk):
        return ref.at[pl.ds(chunk * rows, rows)]

    loads = [
        pltpu.make_async_copy(part(in_ref, i), held.at[i], sems.at[0, i]) for i in range(chunks)
    ]
    stores = [
        pltpu.make_async_copy(held.at[i], part(out_ref, i), sems.at[1, i]) for i in range(chunks)
    ]
    for load in loads:
        load.start()
    for load, store in zip(loads, stores):
        load.wait()
        store.start()
    for store in stores:
        store.wait()


def body(
    features, gate_pre, up_pre, hidden_grad, tile_rows, tile_cols, owner_counts,
    delta_value, moment_one, moment_two,
):
    ids = jnp.stack([lax.axis_index(name) for name in ("y", Z, "x", "core")]).astype(jnp.int32)
    tokens, hidden = gate_pre.shape
    shard_width = features.shape[1]
    width = shard_width * NX * 2
    tile_total = tile_rows.shape[1]
    lists = (tile_rows, tile_cols, owner_counts)

    own = spread(features, "x")
    other = swap(own, "core", 1)

    delta_half = kernel_call(
        turn_kernel, "turn", SHAPE(delta_value.shape[1:], BF16), [VMEM], VMEM
    )(delta_value)
    delta_y = spread(delta_half, "y").reshape(NY * SLOT_CAP, TILE, TILE)
    delta_all = lax.all_gather(delta_y, Z, axis=0, tiled=True)

    grads, turned = kernel_call(
        gate_kernel, "gate", [SHAPE((hidden // TILE, tokens, TILE), BF16)] * 2,
        [SMEM] + [VMEM] * 3, [VMEM] * 2, flops=tokens * hidden * 12, moved=tokens * hidden * 10,
    )(ids, gate_pre, up_pre, hidden_grad)

    tile_ins = [SMEM] * 4 + [ANY, ANY, VMEM]
    tile_scratch = [
        pltpu.VMEM((2, NX, tokens, shard_width), BF16),
        pltpu.SMEM((owner_counts.shape[1],), jnp.int32),
        pltpu.SemaphoreType.DMA((2,)),
    ]

    def terms(parts, *extras):
        return kernel_call(
            functools.partial(tile_kernel, parts), "tiles",
            [SHAPE(((last - first) * SLOT_CAP, TILE, TILE), BF16) for _, (first, last), _ in parts],
            tile_ins + [VMEM] * len(extras), [VMEM] * len(parts), tile_scratch,
            flops=2 * tile_total * TILE**3 // 4, moved=2 << 20,
        )(ids, *lists, own, other, turned, *extras)

    far_low, far_high, one_low, other_high = terms(
        ((2, LOW, None), (2, HIGH, None), (1, LOW, None), (3, HIGH, None))
    )
    far_low, far_high = swap(far_low, "y", 1), swap(far_high, "y", 3)
    one_low, other_high = swap(one_low, "y", 1), swap(other_high, "y", 3)
    one_high, other_low, mine = terms(
        ((1, HIGH, 0), (3, LOW, 1), (0, (0, NZ), None)), far_high, far_low
    )
    one_high, other_low = swap(one_high, "y", 1), swap(other_low, "y", 3)

    def parted(value):
        return value.reshape(-1, 2, SLOT_CAP, TILE, TILE)

    eight = SHAPE((NM, SLOT_CAP, TILE, TILE), BF16)
    keep, give = kernel_call(
        y_sum_kernel, "y_sum", [eight] * 2, [SMEM] + [VMEM] * 5, [VMEM] * 2
    )(ids, *map(parted, (mine, one_low, other_low, one_high, other_high)))

    partner = swap(give, "p", 1)
    stay, give, token = kernel_call(
        contrib_kernel, "contribs",
        [SHAPE((tokens // 2, width), BF16)] * 2 + [SHAPE((8, TILE), F32)],
        [SMEM] * 3 + [ANY] * 3, [VMEM] * 3,
        [
            pltpu.SMEM((tile_total + 8,), jnp.int32),
            pltpu.VMEM(grads.shape, BF16),
            pltpu.VMEM(delta_all.shape, BF16),
            pltpu.SemaphoreType.DMA((2,)),
        ],
        moved=1 << 12, vmem=48,
    )(*lists, grads, delta_all, keep)
    pairs = kernel_call(pair_sum_kernel, "pair_sum", eight, [VMEM] * 3, VMEM)(
        keep, partner, token
    )
    arrived = exchange(pairs, "m")
    own_grad, squares = kernel_call(
        own_grad_kernel, "own_grad",
        [SHAPE((SLOT_CAP, TILE, TILE), F32), SHAPE((NY * NX * 2, 8, TILE), F32)],
        [SMEM, SMEM, VMEM], [VMEM] * 2,
    )(ids, owner_counts, arrived)

    rows = tokens // (2 * NX)
    _, give = lax.optimization_barrier((pairs, give))
    taken = swap(give, "core", 1)
    share, *others = kernel_call(
        core_sum_kernel, "core_sum", [SHAPE((rows, width), BF16)] * NX,
        [SMEM] + [VMEM] * 2, [VMEM] * NX, moved=1 << 12,
    )(ids, stay.reshape(NX, rows, width), taken.reshape(NX, rows, width))
    others = [swap(others[bits - 1], "x", bits) for bits in (2, 1, 3)]
    squares, share, *others = lax.optimization_barrier((squares, share, *others))
    share = share.astype(F32)
    for part in others:
        share = share + part.astype(F32)
    gathered = lax.all_gather(share.astype(BF16), ("x", "core"), axis=0, tiled=True)
    input_grad = kernel_call(
        copy_kernel, "result", SHAPE((tokens, width), BF16), [ANY], ANY,
        [pltpu.VMEM((4, tokens // 4, width), BF16), pltpu.SemaphoreType.DMA((2, 4))],
        moved=4 << 20, vmem=63,
    )(gathered)

    squares = exchange(squares, ("y", "x", "core"))
    squares = kernel_call(relay_kernel, "relay", SHAPE((NZ, 8, TILE), F32), [VMEM], VMEM)(squares)
    squares = exchange(squares, Z)
    squares, input_grad = lax.optimization_barrier((squares, input_grad))
    count_all = float(NX * 2 * tile_total * TILE * TILE)

    def adam(*refs):
        adam_kernel(count_all, *refs)

    outs = kernel_call(
        adam, "adam", [SHAPE(delta_value.shape, F32)] * 3, [SMEM] * 2 + [VMEM] * 5, [VMEM] * 3
    )(ids, owner_counts, squares, own_grad, delta_value, moment_one, moment_two)
    return (input_grad, *outs)


def solution(mesh):
    grid = Mesh(mesh.devices.reshape(NY, NM, 2, NX, 2), ("y", "m", "p", "x", "core"))
    dp, tensor = ("y", "m", "p"), ("x", "core")
    tokens = P(dp, tensor)
    lists = P(tensor, None)
    slots = P(tensor, dp, None, None)
    return jax.shard_map(
        body,
        mesh=grid,
        in_specs=(tokens,) * 4 + (lists,) * 3 + (slots,) * 3,
        out_specs=(P(dp, None),) + (slots,) * 3,
        check_vma=False,
    )
```

```python
import functools

import jax
import jax.numpy as jnp
from jax import lax
from jax.experimental import pallas as pl
from jax.experimental.pallas import tpu as pltpu
from jax.sharding import Mesh, PartitionSpec as P

NY, NM, NX = 4, 8, 4
NZ = 2 * NM
Z = ("m", "p")
TILE = 128
SLOT_CAP = 2
LOW, HIGH = (0, NZ // 2), (NZ // 2, NZ)
BF16, F32 = jnp.bfloat16, jnp.float32
SMEM = pl.BlockSpec(memory_space=pltpu.SMEM)
VMEM = pl.BlockSpec(memory_space=pltpu.VMEM)
ANY = pl.BlockSpec(memory_space=pl.ANY)
SHAPE = jax.ShapeDtypeStruct


def kernel_call(
    kernel, name, outs, ins, out_specs, scratch=(), flops=0, moved=1 << 20, vmem=48
):
    return pl.pallas_call(
        kernel,
        out_shape=outs,
        in_specs=ins,
        out_specs=out_specs,
        scratch_shapes=scratch,
        compiler_params=pltpu.CompilerParams(vmem_limit_bytes=vmem * 1024 * 1024),
        cost_estimate=pl.CostEstimate(flops=flops, bytes_accessed=moved, transcendentals=0),
        name=name,
    )


def swap(value, axis, bits):
    return lax.ppermute(value, axis, [(i, i ^ bits) for i in range(lax.axis_size(axis))])


def exchange(value, axis):
    return lax.all_to_all(value, axis, split_axis=0, concat_axis=0, tiled=True)


def spread(value, axis):
    copies = jnp.broadcast_to(value[None], (lax.axis_size(axis),) + value.shape)
    return exchange(copies, axis)


def gate_kernel(ids_ref, gate_ref, up_ref, hidden_ref, grad_ref, turned_ref):
    blocks = 2 * NX
    rows = grad_ref.shape[1] // blocks
    core = ids_ref[3]
    for col in range(grad_ref.shape[0]):
        cut = slice(col * TILE, (col + 1) * TILE)
        gate = gate_ref[:, cut].astype(F32)
        sig = 1.0 / (1.0 + jnp.exp(-gate))
        value = (
            hidden_ref[:, cut].astype(F32)
            * up_ref[:, cut].astype(F32)
            * sig
            * (1.0 + gate * (1.0 - sig))
        )
        for block in range(blocks):
            place = pl.multiple_of((((block & 1) ^ core) * NX + (block >> 1)) * rows, rows)
            part = value[block * rows : (block + 1) * rows]
            grad_ref[col, pl.ds(place, rows)] = part.astype(BF16)
        turned_ref[col] = value.T.astype(BF16)


def load_features(own_ref, other_ref, features, sems, starts_ref, counts_ref):
    first = pltpu.make_async_copy(own_ref, features.at[0], sems.at[0])
    second = pltpu.make_async_copy(other_ref, features.at[1], sems.at[1])
    first.start()
    second.start()

    def owner_step(owner, start):
        starts_ref[owner] = start
        return start + counts_ref[0, owner]

    lax.fori_loop(0, counts_ref.shape[1], owner_step, 0)
    first.wait()
    second.wait()


def slot_products(group, owners, put, ids_ref, rows_ref, cols_ref, starts_ref, features, turned_ref):
    core = ids_ref[3]
    last = rows_ref.shape[1] - 1
    per_step = 8

    def step(index, carry):
        for part in range(per_step):
            owner = owners[0] + index * per_step + part
            start = starts_ref[group * NZ + owner]
            for rank in range(SLOT_CAP):
                k = jnp.minimum(start + rank, last)
                row = rows_ref[0, k]
                lane = pl.multiple_of((row & 7) * TILE, TILE)
                x = features[((row >> 3) & 1) ^ core, row >> 4, :, pl.ds(lane, TILE)]
                term = jnp.dot(turned_ref[cols_ref[0, k]], x, preferred_element_type=F32)
                put((index * per_step + part) * SLOT_CAP + rank, term)
        return carry

    lax.fori_loop(0, (owners[1] - owners[0]) // per_step, step, 0)


def tile_kernel(
    parts, ids_ref, rows_ref, cols_ref, counts_ref, own_ref, other_ref, turned_ref, *refs
):
    features, starts_ref, sems = refs[-3:]
    load_features(own_ref, other_ref, features, sems, starts_ref, counts_ref)
    for ref, (bits, owners, extra) in zip(refs[-3 - len(parts) :], parts):

        def put(slot, term, ref=ref, extra=extra):
            if extra is not None:
                term = term + refs[extra][slot].astype(F32)
            ref[slot] = term.astype(BF16)

        slot_products(
            ids_ref[0] ^ bits, owners, put,
            ids_ref, rows_ref, cols_ref, starts_ref, features, turned_ref,
        )


def y_sum_kernel(
    ids_ref, mine_ref, one_low_ref, other_low_ref, one_high_ref, other_high_ref,
    keep_ref, give_ref,
):
    parity = ids_ref[1] & 1
    half = NM // 2
    for m in range(NM):
        one, other = (one_low_ref, other_low_ref) if m < half else (one_high_ref, other_high_ref)

        def total(side):
            return (
                mine_ref[m, side].astype(F32)
                + one[m % half, side].astype(F32)
                + other[m % half, side].astype(F32)
            ).astype(BF16)

        keep_ref[m] = total(parity)
        give_ref[m] = total(1 - parity)


def pair_sum_kernel(keep_ref, taken_ref, _, out_ref):
    out_ref[...] = (keep_ref[...].astype(F32) + taken_ref[...].astype(F32)).astype(BF16)


def own_grad_kernel(ids_ref, counts_ref, arrived_ref, grad_ref, squares_ref):
    count = counts_ref[0, ids_ref[0] * NZ + ids_ref[1]]
    squares = jnp.zeros((TILE, TILE), F32)
    for rank in range(SLOT_CAP):
        total = arrived_ref[0, rank].astype(F32)
        for m in range(1, NM):
            total = total + arrived_ref[m, rank].astype(F32)
        total = jnp.where(rank < count, total, 0.0)
        grad_ref[rank] = total
        squares = squares + total * total
    squares_ref[...] = jnp.broadcast_to(jnp.sum(squares), squares_ref.shape)


def relay_kernel(arrived_ref, out_ref):
    total = jnp.sum(arrived_ref[...], axis=0, keepdims=True)
    out_ref[...] = jnp.broadcast_to(total, out_ref.shape)


def adam_kernel(
    count_all, ids_ref, counts_ref, arrived_ref, grad_ref, delta_ref, one_ref, two_ref,
    new_delta_ref, new_one_ref, new_two_ref,
):
    squares = jnp.sum(arrived_ref[...], axis=0)[0:1]
    factor = jnp.minimum(1.0, 1.0 / jnp.sqrt(squares / count_all + 1e-06))
    count = counts_ref[0, ids_ref[0] * NZ + ids_ref[1]]
    for rank in range(SLOT_CAP):
        live = rank < count
        clipped = factor * grad_ref[rank].T
        delta, one, two = delta_ref[0, rank], one_ref[0, rank], two_ref[0, rank]
        first = 0.9 * one + 0.1 * clipped
        second = 0.95 * two + 0.05 * clipped * clipped
        size = first / (1.0 - 0.9**10) / (jnp.sqrt(second / (1.0 - 0.95**10)) + 1e-08)
        updated = delta - 0.02 * (size + 0.1 * delta)
        new_delta_ref[0, rank] = jnp.where(live, updated, delta)
        new_one_ref[0, rank] = jnp.where(live, first, one)
        new_two_ref[0, rank] = jnp.where(live, second, two)


def turn_kernel(delta_ref, out_ref):
    for rank in range(SLOT_CAP):
        out_ref[rank] = delta_ref[0, rank].T.astype(BF16)


def contrib_kernel(
    rows_ref, cols_ref, counts_ref, grads_ref, deltas_ref, stay_ref, give_ref,
    places_ref, grad_ref, delta_ref, sems,
):
    loads = [
        pltpu.make_async_copy(deltas_ref, delta_ref, sems.at[0]),
        pltpu.make_async_copy(grads_ref, grad_ref, sems.at[1]),
    ]
    for load in loads:
        load.start()
    stay_ref[...] = jnp.zeros_like(stay_ref)
    give_ref[...] = jnp.zeros_like(give_ref)
    half = stay_ref.shape[0]

    def owner_step(owner, start):
        place = ((owner & (NZ - 1)) * NY + owner // NZ) * SLOT_CAP
        places_ref[start] = place
        places_ref[start + 1] = place + 1
        return start + counts_ref[0, owner]

    lax.fori_loop(0, counts_ref.shape[1], owner_step, 0)
    for load in loads:
        load.wait()
    per_step = 28

    def step(index, carry):
        last, total = carry
        for part in range(per_step):
            k = index * per_step + part
            row = rows_ref[0, k]
            product = jnp.dot(
                grad_ref[cols_ref[0, k]], delta_ref[places_ref[k]], preferred_element_type=F32
            )
            total = jnp.where(row == last, total, 0.0) + product
            lane = pl.multiple_of(row * TILE, TILE)
            stay_ref[:, pl.ds(lane, TILE)] = total[:half].astype(BF16)
            give_ref[:, pl.ds(lane, TILE)] = total[half:].astype(BF16)
            last = row
        return last, total

    lax.fori_loop(
        0, rows_ref.shape[1] // per_step, step,
        (jnp.int32(-1), jnp.zeros((TILE, TILE), F32)),
    )


def core_sum_kernel(ids_ref, stay_ref, taken_ref, *out_refs):
    for bits, ref in enumerate(out_refs):
        at = ids_ref[2] ^ bits
        ref[...] = (stay_ref[at].astype(F32) + taken_ref[at].astype(F32)).astype(BF16)


def copy_kernel(in_ref, out_ref, held, sems):
    chunks = held.shape[0]
    rows = in_ref.shape[0] // chunks

    def part(ref, chunk):
        return ref.at[pl.ds(chunk * rows, rows)]

    loads = [
        pltpu.make_async_copy(part(in_ref, i), held.at[i], sems.at[0, i]) for i in range(chunks)
    ]
    stores = [
        pltpu.make_async_copy(held.at[i], part(out_ref, i), sems.at[1, i]) for i in range(chunks)
    ]
    for load in loads:
        load.start()
    for load, store in zip(loads, stores):
        load.wait()
        store.start()
    for store in stores:
        store.wait()


def body(
    features, gate_pre, up_pre, hidden_grad, tile_rows, tile_cols, owner_counts,
    delta_value, moment_one, moment_two,
):
    ids = jnp.stack([lax.axis_index(name) for name in ("y", Z, "x", "core")]).astype(jnp.int32)
    tokens, hidden = gate_pre.shape
    shard_width = features.shape[1]
    width = shard_width * NX * 2
    tile_total = tile_rows.shape[1]
    lists = (tile_rows, tile_cols, owner_counts)

    own = spread(features, "x")
    other = swap(own, "core", 1)

    delta_half = kernel_call(
        turn_kernel, "turn", SHAPE(delta_value.shape[1:], BF16), [VMEM], VMEM
    )(delta_value)
    delta_y = spread(delta_half, "y").reshape(NY * SLOT_CAP, TILE, TILE)
    delta_all = lax.all_gather(delta_y, Z, axis=0, tiled=True)

    grads, turned = kernel_call(
        gate_kernel, "gate", [SHAPE((hidden // TILE, tokens, TILE), BF16)] * 2,
        [SMEM] + [VMEM] * 3, [VMEM] * 2, flops=tokens * hidden * 12, moved=tokens * hidden * 10,
    )(ids, gate_pre, up_pre, hidden_grad)

    tile_ins = [SMEM] * 4 + [ANY, ANY, VMEM]
    tile_scratch = [
        pltpu.VMEM((2, NX, tokens, shard_width), BF16),
        pltpu.SMEM((owner_counts.shape[1],), jnp.int32),
        pltpu.SemaphoreType.DMA((2,)),
    ]

    def terms(parts, *extras):
        return kernel_call(
            functools.partial(tile_kernel, parts), "tiles",
            [SHAPE(((last - first) * SLOT_CAP, TILE, TILE), BF16) for _, (first, last), _ in parts],
            tile_ins + [VMEM] * len(extras), [VMEM] * len(parts), tile_scratch,
            flops=2 * tile_total * TILE**3 // 4, moved=2 << 20,
        )(ids, *lists, own, other, turned, *extras)

    far_low, far_high, one_low, other_high = terms(
        ((2, LOW, None), (2, HIGH, None), (1, LOW, None), (3, HIGH, None))
    )
    far_low, far_high = swap(far_low, "y", 1), swap(far_high, "y", 3)
    one_low, other_high = swap(one_low, "y", 1), swap(other_high, "y", 3)
    one_high, other_low, mine = terms(
        ((1, HIGH, 0), (3, LOW, 1), (0, (0, NZ), None)), far_high, far_low
    )
    one_high, other_low = swap(one_high, "y", 1), swap(other_low, "y", 3)

    def parted(value):
        return value.reshape(-1, 2, SLOT_CAP, TILE, TILE)

    eight = SHAPE((NM, SLOT_CAP, TILE, TILE), BF16)
    keep, give = kernel_call(
        y_sum_kernel, "y_sum", [eight] * 2, [SMEM] + [VMEM] * 5, [VMEM] * 2
    )(ids, *map(parted, (mine, one_low, other_low, one_high, other_high)))

    keep, grads = lax.optimization_barrier((keep, grads))
    partner = swap(give, "p", 1)
    stay, give = kernel_call(
        contrib_kernel, "contribs", [SHAPE((tokens // 2, width), BF16)] * 2,
        [SMEM] * 3 + [ANY] * 2, [VMEM] * 2,
        [
            pltpu.SMEM((tile_total + 8,), jnp.int32),
            pltpu.VMEM(grads.shape, BF16),
            pltpu.VMEM(delta_all.shape, BF16),
            pltpu.SemaphoreType.DMA((2,)),
        ],
        moved=1 << 12,
    )(*lists, grads, delta_all)
    pairs = kernel_call(pair_sum_kernel, "pair_sum", eight, [VMEM] * 2 + [ANY], VMEM)(
        keep, partner, stay
    )
    arrived = exchange(pairs, "m")
    own_grad, squares = kernel_call(
        own_grad_kernel, "own_grad",
        [SHAPE((SLOT_CAP, TILE, TILE), F32), SHAPE((NY * NX * 2, 8, TILE), F32)],
        [SMEM, SMEM, VMEM], [VMEM] * 2,
    )(ids, owner_counts, arrived)


    rows = tokens // (2 * NX)
    _, give = lax.optimization_barrier((pairs, give))
    taken = swap(give, "core", 1)
    share, *others = kernel_call(
        core_sum_kernel, "core_sum", [SHAPE((rows, width), BF16)] * NX,
        [SMEM] + [VMEM] * 2, [VMEM] * NX, moved=1 << 12,
    )(ids, stay.reshape(NX, rows, width), taken.reshape(NX, rows, width))
    others = [swap(others[bits - 1], "x", bits) for bits in (2, 1, 3)]
    squares, share, *others = lax.optimization_barrier((squares, share, *others))
    share = share.astype(F32)
    for part in others:
        share = share + part.astype(F32)
    gathered = lax.all_gather(share.astype(BF16), ("x", "core"), axis=0, tiled=True)
    input_grad = kernel_call(
        copy_kernel, "result", SHAPE((tokens, width), BF16), [ANY], ANY,
        [pltpu.VMEM((4, tokens // 4, width), BF16), pltpu.SemaphoreType.DMA((2, 4))],
        moved=4 << 20, vmem=63,
    )(gathered)

    squares = exchange(squares, ("y", "x", "core"))
    squares = kernel_call(relay_kernel, "relay", SHAPE((NZ, 8, TILE), F32), [VMEM], VMEM)(squares)
    squares = exchange(squares, Z)
    squares, input_grad = lax.optimization_barrier((squares, input_grad))
    count_all = float(NX * 2 * tile_total * TILE * TILE)

    def adam(*refs):
        adam_kernel(count_all, *refs)

    outs = kernel_call(
        adam, "adam", [SHAPE(delta_value.shape, F32)] * 3, [SMEM] * 2 + [VMEM] * 5, [VMEM] * 3
    )(ids, owner_counts, squares, own_grad, delta_value, moment_one, moment_two)
    return (input_grad, *outs)


def solution(mesh):
    grid = Mesh(mesh.devices.reshape(NY, NM, 2, NX, 2), ("y", "m", "p", "x", "core"))
    dp, tensor = ("y", "m", "p"), ("x", "core")
    tokens = P(dp, tensor)
    lists = P(tensor, None)
    slots = P(tensor, dp, None, None)
    return jax.shard_map(
        body,
        mesh=grid,
        in_specs=(tokens,) * 4 + (lists,) * 3 + (slots,) * 3,
        out_specs=(P(dp, None),) + (slots,) * 3,
        check_vma=False,
    )
```
